32 devices in a mesh: seq: 32 (over z, y, x, core).
Axes of the slice: x: 2, y: 2, z: 4, core: 2. Of those that a mesh axis runs over, the one named last changes fastest.
Arguments:
- hidden: bfloat16 [8192, 1024], P('seq'), may hold values from -6 to 6
- segment_ids: int32 [8192], P('seq'), may hold values from 0 to 2, as said below
- in_weight: bfloat16 [2, 1024, 4384], P(None, 'seq'), may hold values from -0.1875 to 0.1875
- out_weight: bfloat16 [2, 2048, 1024], P(None, 'seq'), may hold values from -0.125 to 0.125
- conv_weight: bfloat16 [2, 4, 2304], P(None, None, 'seq'), may hold values from -3 to 3
- conv_bias: bfloat16 [2, 2304], P(None, 'seq'), may hold values from -3 to 3
- norm_gain: bfloat16 [2, 1024], P(None, 'seq'), may hold values from 0.099609375 to 1.8984375
- gate_gain: bfloat16 [2, 2048], P(None, 'seq'), may hold values from 0.099609375 to 1.8984375
- dt_bias: float32 [2, 32], replicated, may hold values from -6.9 to -2.3
- a_log: float32 [2, 32], replicated, may hold values from -5 to 1
- skip_param: float32 [2, 32], replicated, may hold values from 0.5 to 1.5
- cotangent: float32 [8192, 1024], P('seq'), may hold values from -6 to 6
Outputs:
- final_hidden: float32 [8192, 1024], P('seq')
- hidden_grad: float32 [8192, 1024], P('seq')
- in_weight_grad: float32 [2, 1024, 4384], P(None, 'seq')
- out_weight_grad: float32 [2, 2048, 1024], P(None, 'seq')
- conv_weight_grad: float32 [2, 4, 2304], P(None, None, 'seq')
- conv_bias_grad: float32 [2, 2304], P(None, 'seq')
- norm_gain_grad: float32 [2, 1024], P(None, 'seq')
- gate_gain_grad: float32 [2, 2048], P(None, 'seq')
- dt_bias_grad: float32 [2, 32], replicated
- a_log_grad: float32 [2, 32], replicated
- skip_grad: float32 [2, 32], replicated
The draws below stay inside these ranges and needn't reach their ends.
Inputs may be any that keep to these rules, and one draw needn't show every extreme that they name: `segment_ids`: ids never fall along the tokens and every id from 0 to 2 is used; document 0 ends within the first 256 tokens and document 2 begins within the last 256 tokens.
All inputs are finite; a program needn't handle non-finite values.
Results may differ from the reference program's by a relative error of at most 0.015.
Values may be sent and summed in bfloat16 or wider, within the bound.
No kernel may reach another device: no remote copies, remote signals or barrier semaphores. Data moves between devices by JAX's collectives and lax.ppermute only.
A program may use at most 512 MiB of HBM per device.

```python
import jax
import jax.numpy as jnp
from jax import lax

D = 1024
HEADS = 32
HEAD_DIM = 64
STATE = 128
CONV_K = 4
LAYERS = 2
TOK_DEV = 256
INNER = 2048
CONV_CH = 2304
PROJ = 4384
TOKENS = 8192


def draw_segment_ids(key, part):
    key = jax.random.fold_in(key, 7)
    first_key, second_key = jax.random.split(key)
    first_end = jax.random.randint(first_key, (), 1, TOK_DEV)
    second_end = jax.random.randint(second_key, (), TOKENS - TOK_DEV + 1, TOKENS)
    positions = jnp.arange(TOKENS)
    return (positions >= first_end).astype(jnp.int32) + (positions >= second_end).astype(jnp.int32)


def levels(key, shape, cuts, low, high):
    gain = 1.0
    for dim, shards_of in cuts:
        heights = jax.random.uniform(jax.random.fold_in(jax.random.fold_in(key, 6), dim), (shards_of,), jnp.float32, low / len(cuts), high / len(cuts))
        gain = gain * jnp.repeat(jnp.exp(heights), shape[dim] // shards_of).reshape((-1,) + (1,) * (len(shape) - 1 - dim))
    return gain


def gaussian(own_key, shape, scale, most, cuts=(), dtype=jnp.bfloat16):
    values = scale * jax.random.normal(own_key, shape, jnp.float32)
    if cuts:
        values = values * levels(own_key, shape, cuts, -0.22, 0.18)
    return jnp.clip(values, -most, most).astype(dtype)


def setup_inputs(seed: int = 0) -> dict:
    seeds = jax.random.split(jax.random.key(seed), 13)
    hidden = gaussian(seeds[0], (TOKENS, D), 1.0, 6.0, ((0, 32),))
    segment_ids = draw_segment_ids(jax.random.fold_in(seeds[12], 71), 0)
    in_weight = gaussian(seeds[2], (LAYERS, D, PROJ), D ** -0.5, 0.1875, ((1, 32),))
    out_weight = gaussian(seeds[3], (LAYERS, INNER, D), INNER ** -0.5, 0.125, ((1, 32),))
    conv_weight = gaussian(seeds[4], (LAYERS, CONV_K, CONV_CH), CONV_K ** -0.5, 3.0, ((2, 32),))
    conv_bias = gaussian(seeds[5], (LAYERS, CONV_CH), 0.5, 3.0, ((1, 32),))
    norm_gain = jnp.clip(1.0 + 0.18 * jax.random.normal(seeds[6], (LAYERS, D), jnp.float32), 0.099609375, 1.8984375).astype(jnp.bfloat16)
    gate_gain = jnp.clip(1.0 + 0.18 * jax.random.normal(seeds[7], (LAYERS, INNER), jnp.float32), 0.099609375, 1.8984375).astype(jnp.bfloat16)
    dt_bias = jnp.clip(jax.random.uniform(seeds[8], (LAYERS, HEADS), jnp.float32, -6.9, -2.3), -6.9, -2.3)
    a_log = jnp.clip(jax.random.uniform(seeds[9], (LAYERS, HEADS), jnp.float32, -5.0, 1.0), -5.0, 1.0)
    skip_param = jnp.clip(jax.random.uniform(seeds[10], (LAYERS, HEADS), jnp.float32, 0.5, 1.5), 0.5, 1.5)
    cotangent = gaussian(seeds[11], (TOKENS, D), 1.0, 6.0, ((0, 32),), jnp.float32)
    return {"hidden": hidden, "segment_ids": segment_ids, "in_weight": in_weight, "out_weight": out_weight, "conv_weight": conv_weight, "conv_bias": conv_bias, "norm_gain": norm_gain, "gate_gain": gate_gain, "dt_bias": dt_bias, "a_log": a_log, "skip_param": skip_param, "cotangent": cotangent}


EPS = 1e-05
PRECISE = lax.Precision.HIGHEST

@jax.custom_vjp
def low(v):
    return lax.optimization_barrier(v.astype(jnp.bfloat16)).astype(jnp.float32)

@jax.custom_vjp
def low_back(v):
    return v

def low_keep(v):
    return (low(v), None)

def low_pass(kept, grad):
    return (grad,)

def back_keep(v):
    return (v, None)

def back_low(kept, grad):
    return (low(grad),)
low.defvjp(low_keep, low_pass)
low_back.defvjp(back_keep, back_low)

def matmul(left_m, right_m):
    return jnp.dot(left_m, right_m, precision=PRECISE, preferred_element_type=jnp.float32)

def norm_input(residual, norm_g):
    inv_rms = lax.rsqrt(lax.optimization_barrier(jnp.mean(residual * residual, axis=-1, keepdims=True)) + EPS)
    return residual * inv_rms * norm_g

def conv_mix(padded, dt_raw, conv_w, conv_b, dt_b, a_lg, seg_pad):
    tokens_n = dt_raw.shape[0]
    own_segs = seg_pad[CONV_K - 1:]
    conv_out = jnp.zeros((tokens_n, conv_w.shape[1]), jnp.float32) + conv_b
    for offset in range(CONV_K):
        same_doc = (seg_pad[offset:offset + tokens_n] == own_segs).astype(jnp.float32)
        conv_out = conv_out + conv_w[offset] * padded[offset:offset + tokens_n] * same_doc[:, None]
    activated = jax.nn.silu(conv_out)
    head_in = activated[:, :INNER].reshape(tokens_n, HEADS, HEAD_DIM)
    b_rows = activated[:, INNER:INNER + STATE]
    c_rows = activated[:, INNER + STATE:]
    step_size = jax.nn.softplus(dt_raw + dt_b)
    return (head_in, b_rows, c_rows, step_size, -jnp.exp(a_lg))

def ssd_local(head_in, b_rows, c_rows, step_size, decay_rate, state_in, segments, before):
    log_decay = jnp.cumsum(step_size * decay_rate, axis=0)
    length = segments.shape[0]
    positions = jnp.arange(length)
    allowed = (positions[:, None] >= positions[None, :]) & (segments[:, None] == segments[None, :])
    allowed_cube = allowed[:, :, None]
    spread = jnp.where(allowed_cube, log_decay[:, None, :] - log_decay[None, :, :], 0.0)
    decayed = jnp.where(allowed_cube, jnp.exp(spread), 0.0)
    scores = jnp.einsum('tn,sn->ts', c_rows, b_rows, precision=PRECISE)
    mixing = scores[:, :, None] * decayed * step_size[None, :, :]
    within = jnp.einsum('tsh,shp->thp', mixing, head_in, precision=PRECISE)
    carry_on = (segments == before).astype(jnp.float32)
    inflow = jnp.exp(log_decay) * carry_on[:, None]
    return within + inflow[:, :, None] * jnp.einsum('tn,hpn->thp', c_rows, state_in, precision=PRECISE)

def state_local(head_in, b_rows, step_size, decay_rate, segments, before):
    log_decay = jnp.cumsum(step_size * decay_rate, axis=0)
    tail_doc = (segments == segments[-1]).astype(jnp.float32)
    weight_last = tail_doc[:, None] * jnp.exp(log_decay[-1][None, :] - log_decay) * step_size
    keep_all = jnp.exp(log_decay[-1]) * (segments[-1] == before).astype(jnp.float32)
    local_state = jnp.einsum('sh,shp,sn->hpn', weight_last, head_in, b_rows, precision=PRECISE)
    return (keep_all, local_state)

def post_mix(y_out, head_in, gate_z, skip_d, gate_g):
    tokens_n = gate_z.shape[0]
    y_full = (y_out + skip_d[:, None] * head_in).reshape(tokens_n, INNER)
    gated = y_full * jax.nn.silu(gate_z)
    inv_rms = lax.rsqrt(lax.optimization_barrier(jnp.mean(gated * gated, axis=-1, keepdims=True)) + EPS)
    return gated * inv_rms * gate_g

def layer_forward(residual, weights, seg_pad, block_segs, before_segs):
    in_w, out_w, conv_w, conv_b, norm_g, gate_g, dt_b, a_lg, skip_d = weights
    tokens_n = residual.shape[0]
    normed = low(norm_input(residual, norm_g))
    projected = low_back(low(matmul(normed, in_w)))
    gate_z = projected[:, :INNER]
    conv_in = projected[:, INNER:INNER + CONV_CH]
    dt_raw = projected[:, INNER + CONV_CH:]
    padded = jnp.concatenate([jnp.zeros((CONV_K - 1, CONV_CH), jnp.float32), conv_in], axis=0)
    head_in, b_rows, c_rows, step_size, decay_rate = conv_mix(padded, dt_raw, conv_w, conv_b, dt_b, a_lg, seg_pad)
    blocks = tokens_n // TOK_DEV

    def split_rows(values):
        return values.reshape((blocks, TOK_DEV) + values.shape[1:])

    def one_block(carried, pieces):
        head_blk, b_blk, c_blk, step_blk, seg_blk, before_blk = pieces
        y_blk = ssd_local(head_blk, b_blk, c_blk, step_blk, decay_rate, carried, seg_blk, before_blk)
        keep_all, local_state = state_local(head_blk, b_blk, step_blk, decay_rate, seg_blk, before_blk)
        return (keep_all[:, None, None] * carried + local_state, y_blk)
    start = jnp.zeros((HEADS, HEAD_DIM, STATE), jnp.float32)
    final_state, y_blocks = lax.scan(jax.checkpoint(one_block), start, (split_rows(head_in), split_rows(b_rows), split_rows(c_rows), split_rows(step_size), block_segs, before_segs))
    y_out = y_blocks.reshape(tokens_n, HEADS, HEAD_DIM)
    gnormed = low(post_mix(y_out, head_in, gate_z, skip_d, gate_g))
    return residual + low_back(matmul(gnormed, out_w))

def reference(hidden, segment_ids, in_weight, out_weight, conv_weight, conv_bias, norm_gain, gate_gain, dt_bias, a_log, skip_param, cotangent):
    tokens_n = hidden.shape[0]
    segs_int = segment_ids.astype(jnp.int32)
    seg_pad = jnp.concatenate([jnp.full((CONV_K - 1,), -1, jnp.int32), segs_int])
    block_segs = segs_int.reshape(tokens_n // TOK_DEV, TOK_DEV)
    before_segs = jnp.concatenate([jnp.full((1,), -1, jnp.int32), block_segs[:-1, -1]])
    params = jax.tree.map(lambda leaf_arr: leaf_arr.astype(jnp.float32), (in_weight, out_weight, conv_weight, conv_bias, norm_gain, gate_gain, dt_bias, a_log, skip_param))

    def forward(start_h, layer_params):
        residual = start_h
        for layer_idx in range(LAYERS):
            layer_w = jax.tree.map(lambda leaf_arr: leaf_arr[layer_idx], layer_params)
            residual = layer_forward(residual, layer_w, seg_pad, block_segs, before_segs)
        return residual
    final_hidden, pull_back = jax.vjp(forward, hidden.astype(jnp.float32), params)
    hidden_grad, grads = pull_back(cotangent.astype(jnp.float32))
    return (final_hidden, hidden_grad, grads[0], grads[1], grads[2], grads[3], grads[4], grads[5], grads[6], grads[7], grads[8])
```

```python
from functools import partial

import jax
import jax.numpy as jnp
import numpy as np
from jax import lax
from jax.experimental import pallas as pl
from jax.experimental.pallas import tpu as pltpu
from jax.sharding import PartitionSpec as P

HEADS = 32
HEAD_DIM = 64
STATE = 128
CONV_K = 4
INNER = 2048
CONV_CH = 2304
SIDE = CONV_CH + HEADS
WIDE = 2432
CUT = 1280
LANES = 128
PAIRS = HEADS // 2
HALO = 16
LEAD = HALO - (CONV_K - 1)
FAR = -1e30

EPS = 1e-05
F32 = jnp.float32
BF16 = jnp.bfloat16
EXACT = lax.Precision.HIGHEST
MB = 1024 * 1024


def axes_of(count):
    side = 4 if count >= 128 else 2
    plane = 2 * side * side
    return {"c": (2, 1), "x": (side, 2), "y": (side, 2 * side), "z": (count // plane, plane)}


def swap(value, flip):
    count = lax.axis_size("seq")
    return lax.ppermute(value, "seq", [(i, i ^ flip) for i in range(count)])


def shifted(shard, by):
    count = lax.axis_size("seq")
    return lax.ppermute(shard, "seq", [(i, i + by) for i in range(count) if 0 <= i + by < count])


def relative_places(count):
    axes = axes_of(count)
    places = np.zeros((1,), np.int32)
    for name in ("c", "y", "x", "z"):
        size, shift = axes[name]
        places = (places[:, None] + np.arange(size, dtype=np.int32)[None, :] * shift).reshape(-1)
    return places


def relative_order(count, me, block):
    places = jnp.asarray(np.repeat(relative_places(count), block))
    inner = jnp.asarray(np.tile(np.arange(block, dtype=np.int32), count))
    source = (places ^ me) * block + inner
    return (jnp.arange(count * block)[:, None] == source[None, :]).astype(BF16)


def gather_side(shard):
    axes = axes_of(lax.axis_size("seq"))

    def grow(value, name, axis):
        size, shift = axes[name]
        return jnp.stack([value] + [swap(value, d * shift) for d in range(1, size)], axis)

    line = grow(shard, "z", 0)
    left = grow(grow(line[:, :, :CUT], "x", 0), "y", 0)
    right = grow(grow(line[:, :, CUT:], "y", 0), "x", 1)
    left = left.reshape(-1, left.shape[-1])
    right = right.reshape(-1, right.shape[-1])
    return (left, swap(left, 1)), (right, swap(right, 1))


def reduce_shares(grad, order):
    axes = axes_of(lax.axis_size("seq"))
    sizes = tuple(axes[name][0] for name in ("c", "y", "x", "z"))
    rows = grad.shape[0] // int(np.prod(sizes))
    parts = grad.reshape(sizes + (rows, grad.shape[1]))
    names = ["c", "y", "x", "z"]
    terms = [parts]
    for name in ("c",) + order + ("z",):
        size, shift = axes[name]
        axis = names.index(name)
        names.remove(name)

        def total(index, terms=terms, axis=axis):
            picked = [lax.index_in_dim(t, index, axis, False).astype(F32) for t in terms]
            return sum(picked[1:], picked[0])

        if len(terms) == 1:
            pieces = [lax.index_in_dim(terms[0], d, axis, False) for d in range(size)]
        else:
            pieces = [total(d).astype(BF16) for d in range(size)]
        terms = [pieces[0]] + [swap(pieces[d], d * shift) for d in range(1, size)]
    picked = [t.astype(F32) for t in terms]
    return sum(picked[1:], picked[0])


def sum_all(value):
    flip = lax.axis_size("seq") // 2
    while flip:
        value = value + swap(value, flip)
        flip //= 2
    return value


def kernel_call(body, outs, args, scratch=(), limit=40, flops=0, moved=None):
    in_specs = [
        pl.BlockSpec(memory_space=pltpu.SMEM if a.dtype == jnp.int32 else pltpu.VMEM) for a in args
    ]
    size = sum(int(np.prod(a.shape)) * a.dtype.itemsize for a in args) + sum(
        int(np.prod(o[0])) * jnp.dtype(o[1]).itemsize for o in outs
    )
    return pl.pallas_call(
        body,
        out_shape=tuple(jax.ShapeDtypeStruct(*o) for o in outs),
        in_specs=in_specs,
        out_specs=tuple(pl.BlockSpec(memory_space=pltpu.VMEM) for _ in outs),
        scratch_shapes=list(scratch),
        compiler_params=pltpu.CompilerParams(vmem_limit_bytes=limit * MB),
        cost_estimate=pl.CostEstimate(flops=flops, bytes_accessed=size, transcendentals=0),
    )(*args)


def dot(left, right, precision=None):
    return jnp.dot(left, right, precision=precision, preferred_element_type=F32)


def dot_t(left, right):
    return lax.dot_general(left, right, (((1,), (1,)), ((), ())), preferred_element_type=F32)


def halves(value):
    high = value.astype(BF16)
    return high, (value - high.astype(F32)).astype(BF16)


def fine(form, left, right):
    (lh, ll), (rh, rl) = halves(left), halves(right)
    return form(lh, rh) + (form(ll, rh) + form(lh, rl))


def lanes_of(rows):
    return lax.broadcasted_iota(jnp.int32, (rows, LANES), 1)


def spread(values, pair):
    low = lanes_of(values.shape[0]) < HEAD_DIM
    return jnp.where(low, values[:, 2 * pair : 2 * pair + 1], values[:, 2 * pair + 1 : 2 * pair + 2])


def spread_row(row):
    return jnp.concatenate([spread(row, pair) for pair in range(PAIRS)], axis=1)


def head_sums(product, pair):
    rows = lax.broadcasted_iota(jnp.int32, (LANES, LANES), 0)
    cols = lax.broadcasted_iota(jnp.int32, (LANES, LANES), 1)
    pick = (cols == 2 * pair + (rows >= HEAD_DIM).astype(jnp.int32)).astype(BF16)
    high = product.astype(BF16)
    low = (product - high.astype(F32)).astype(BF16)
    return dot(high, pick) + dot(low, pick)


def sigmoid(v):
    return 1.0 / (1.0 + jnp.exp(-v))


def silu(v):
    return v * sigmoid(v)


def tile(pair):
    return slice(pair * LANES, (pair + 1) * LANES)


def pack_row(row):
    first = row.astype(BF16).astype(F32)
    second = (row - first).astype(BF16).astype(F32)
    third = row - first - second
    place = lax.broadcasted_iota(jnp.int32, (16, row.shape[1]), 0)
    packed = jnp.where(place == 0, first, jnp.where(place == 1, second, third))
    return jnp.where(place < 3, packed, 0.0).astype(BF16)


def unpack_row(rows):
    return jnp.sum(rows.astype(F32), axis=0, keepdims=True)


def emit_msg(total, keep, msg_o):
    msg_o[0:STATE, :] = total.astype(msg_o.dtype)
    if msg_o.dtype == F32:
        msg_o[STATE:, :] = jnp.broadcast_to(keep, (msg_o.shape[0] - STATE, keep.shape[1]))
    else:
        msg_o[STATE:, :] = pack_row(keep)


def read_msg(recv):
    if recv.dtype == F32:
        return recv[0:STATE, :], recv[STATE : STATE + 1, :]
    return recv[0:STATE, :].astype(F32), unpack_row(recv[STATE:, :])


def emit_full(total, keep, total_o, keep_o, msg_o):
    total_o[...] = total
    keep_o[...] = jnp.broadcast_to(keep, keep_o.shape)
    emit_msg(total, keep, msg_o)


def emit_halves(total, keep, upper, total_o, keep_o, msg_o):
    half = total.shape[1] // 2
    low, high = total[:, :half], total[:, half:]
    klow, khigh = keep[:, :half], keep[:, half:]
    total_o[...] = jnp.where(upper, high, low)
    keep_o[...] = jnp.broadcast_to(jnp.where(upper, khigh, klow), keep_o.shape)
    emit_msg(jnp.where(upper, low, high), jnp.where(upper, klow, khigh), msg_o)


def bit_of(me, flip):
    return (me[0] & flip) != 0


def state_outs(width, kind):
    tail = 8 if kind == F32 else 16
    return [((STATE, width), F32), ((8, width), F32), ((STATE + tail, width), kind)]


def halve_kernel(total, keep, recv, me, first_o, kfirst_o, total_o, keep_o, msg_o, *, flip, after, back):
    other, kother = read_msg(recv)
    mine, kmine = total[...], keep[0:1, :]
    first = jnp.logical_xor(bit_of(me, flip), not back)
    t_first = jnp.where(first, mine, other)
    t_second = jnp.where(first, other, mine)
    k_first = jnp.where(first, kmine, kother)
    k_second = jnp.where(first, kother, kmine)
    first_o[...] = t_first
    kfirst_o[...] = jnp.broadcast_to(k_first, kfirst_o.shape)
    joined = k_second * t_first + t_second
    if after:
        emit_halves(joined, k_first * k_second, bit_of(me, after), total_o, keep_o, msg_o)
    else:
        emit_full(joined, k_first * k_second, total_o, keep_o, msg_o)


def whole_kernel(total, keep, state, kstate, recv, me, state_o, kstate_o, total_o, keep_o, msg_o, *, flip, back):
    other, kother = read_msg(recv)
    mine, kmine = total[...], keep[0:1, :]
    later = jnp.logical_xor(bit_of(me, flip), back)
    kpre = kstate[0:1, :]
    state_o[...] = state[...] + jnp.where(later, kpre * other, 0.0)
    kstate_o[...] = jnp.broadcast_to(jnp.where(later, kpre * kother, kpre), kstate_o.shape)
    joined = jnp.where(later, kmine * other + mine, kother * mine + other)
    emit_full(joined, kmine * kother, total_o, keep_o, msg_o)


def last_kernel(state, kstate, recv, first, kfirst, me, mine_o, msg_o, *, flip, down, back):
    later = jnp.logical_xor(bit_of(me, flip), back)
    into = state[...] + jnp.where(later, kstate[0:1, :] * recv[0:STATE, :].astype(F32), 0.0)
    split_block(into, first, kfirst, me, mine_o, msg_o, down, back)


def split_block(into, first, kfirst, me, mine_o, msg_o, down, back):
    beyond = kfirst[0:1, :] * into + first[...]
    second = jnp.logical_xor(bit_of(me, down), back)
    mine_o[...] = jnp.where(second, beyond, into)
    msg_o[...] = jnp.where(second, into, beyond).astype(msg_o.dtype)


def join_halves(mine, recv, upper):
    theirs = recv[...].astype(F32)
    own = mine[...]
    return jnp.where(upper, theirs, own), jnp.where(upper, own, theirs)


def down_kernel(mine, recv, first, kfirst, me, mine_o, msg_o, *, up, down, back):
    low, high = join_halves(mine, recv, bit_of(me, up))
    split_block(jnp.concatenate([low, high], axis=1), first, kfirst, me, mine_o, msg_o, down, back)


def exchange(total, keep, msg, me, back):
    count = lax.axis_size("seq")
    kind = msg.dtype
    halving = (1, 2, 4)
    rest = [1 << k for k in range(3, count.bit_length() - 1)]
    saved = []
    recv = swap(msg, halving[0])
    for i, flip in enumerate(halving):
        width = total.shape[1]
        after = halving[i + 1] if i + 1 < len(halving) else 0
        outs = state_outs(width, kind)[:2] + state_outs(width // 2 if after else width, kind)
        first, kfirst, total, keep, msg = kernel_call(
            partial(halve_kernel, flip=flip, after=after, back=back),
            outs, (total, keep, recv, me), limit=12,
        )
        saved.append((first, kfirst))
        recv = swap(msg, after or rest[0])
    width = total.shape[1]
    state, kstate = jnp.zeros((STATE, width), F32), jnp.ones((8, width), F32)
    for i, flip in enumerate(rest[:-1]):
        state, kstate, total, keep, msg = kernel_call(
            partial(whole_kernel, flip=flip, back=back),
            state_outs(width, kind)[:2] + state_outs(width, kind),
            (total, keep, state, kstate, recv, me), limit=12,
        )
        recv = swap(msg, rest[i + 1])
    mine, msg = kernel_call(
        partial(last_kernel, flip=rest[-1], down=halving[2], back=back),
        [((STATE, width), F32), ((STATE, width), kind)],
        (state, kstate, recv) + saved[2] + (me,), limit=12,
    )
    for up in (2, 1):
        recv = swap(msg, halving[up])
        width *= 2
        mine, msg = kernel_call(
            partial(down_kernel, up=halving[up], down=halving[up - 1], back=back),
            [((STATE, width), F32), ((STATE, width), kind)],
            (mine, recv) + saved[up - 1] + (me,), limit=12,
        )
    return mine, swap(msg, 1)


def norm_kernel(h, halo, gain, out):
    for ref, at in ((halo, slice(0, HALO)), (h, slice(HALO, HALO + h.shape[0]))):
        v = ref[...].astype(F32)
        inv = lax.rsqrt(jnp.mean(v * v, axis=-1, keepdims=True) + EPS)
        out[at, :] = (v * inv * gain[0:1, :]).astype(BF16)


def norm_back_kernel(gn, h, g, gain, out, gain_o):
    v = h[...].astype(F32)
    grad = gn[...]
    inv = lax.rsqrt(jnp.mean(v * v, axis=-1, keepdims=True) + EPS)
    n = v * inv
    q = grad * gain[0:1, :]
    out[...] = g[...] + inv * (q - n * jnp.mean(q * n, axis=-1, keepdims=True))
    gain_o[...] = jnp.broadcast_to(jnp.sum(grad * n, axis=0, keepdims=True), gain_o.shape)


def triangle(rows, lower):
    r = lax.broadcasted_iota(jnp.int32, (rows, rows), 0)
    c = lax.broadcasted_iota(jnp.int32, (rows, rows), 1)
    return r >= c if lower else r <= c


def conv_state_kernel(pc, cw, hp, mk, me, conv_o, dt_o, log_o, total_o, keep_o, msg_o, xw, *low, precise):
    rows = mk.shape[0]
    marks = mk[...]
    raw = pc[HALO:, CONV_CH:WIDE].astype(F32) + hp[0:1, :]
    soft = jnp.maximum(raw, 0.0) + jnp.log1p(jnp.exp(-jnp.abs(raw)))
    dt = jnp.where(lanes_of(rows) < HEADS, soft, 0.0)
    log = dot(triangle(rows, True).astype(F32), dt * hp[1:2, :], EXACT)
    last = log[rows - 1 : rows, :]
    weight = marks[:, 4:5] * jnp.exp(last - log) * dt
    dt_o[...] = dt
    log_o[...] = log
    b_cols = None
    for j in range(CONV_CH // LANES):
        ext = pc[:, tile(j)].astype(F32)
        out = cw[4:5, tile(j)] + cw[3:4, tile(j)] * ext[HALO:, :]
        for k in range(CONV_K - 1):
            out = out + cw[k : k + 1, tile(j)] * ext[LEAD + k : LEAD + k + rows, :] * marks[:, k : k + 1]
        conv_o[:, tile(j)] = out
        if j < PAIRS:
            high, rest = halves(silu(out) * spread(weight, j))
            xw[:, tile(j)] = high
            if precise:
                low[0][:, tile(j)] = rest
        elif j == PAIRS:
            b_cols, b_rest = halves(silu(out).T)
    total = dot(b_cols, xw[...])
    if precise:
        total = total + (dot(b_rest, xw[...]) + dot(b_cols, low[0][...]))
    keep = spread_row(jnp.exp(last) * marks[rows - 1 : rows, 3:4])
    emit_halves(total, keep, bit_of(me, 1), total_o, keep_o, msg_o)


def mask_bias(mk, sr, rows):
    same = mk[:, 5:6] == sr[0:1, :]
    return jnp.where(jnp.logical_and(triangle(rows, True), same), 0.0, FAR)


def within_kernel(conv, dt, log, hp, mk, sr, y_o, xdt, lcol, lrow, *lower, precise):
    rows = mk.shape[0]
    b = silu(conv[:, tile(PAIRS)])
    c = silu(conv[:, tile(PAIRS + 1)])
    scores = fine(dot_t, c, b)
    bias = mask_bias(mk, sr, rows)
    dtv, logv = dt[...], log[...]
    lrow[...] = logv.T
    for j in range(PAIRS):
        x = silu(conv[:, tile(j)])
        high, rest = halves(x * spread(dtv, j))
        xdt[:, tile(j)] = high
        if precise:
            lower[0][:, tile(j)] = rest
        y_o[:, tile(j)] = x * spread(hp[2:3, :], j)
    for h in range(HEADS):
        lcol[h] = jnp.broadcast_to(logv[:, h : h + 1], (rows, LANES))
    low = lanes_of(rows) < HEAD_DIM

    def pair(j, _):
        at = pl.ds(pl.multiple_of(j * LANES, LANES), LANES)
        xp = xdt[:, at]
        res = []
        for q in range(2):
            col = lcol[2 * j + q]
            span = jnp.concatenate([col] * (rows // LANES), axis=1) - lrow[pl.ds(2 * j + q, 1), :]
            mix = scores * jnp.exp(span + bias)
            if precise:
                high, rest = halves(mix)
                res.append(dot(high, xp) + (dot(rest, xp) + dot(high, lower[0][:, at])))
            else:
                res.append(dot(mix.astype(BF16), xp))
        y_o[:, at] += jnp.where(low, res[0], res[1])
        return 0

    lax.fori_loop(0, PAIRS, pair, 0)


def post_kernel(yw, mine, recv, conv, log, mk, z, gg, me, y_o, gn_o, st_o, gated):
    rows = mk.shape[0]
    low, high = join_halves(mine, recv, bit_of(me, 1))
    st_o[:, : INNER // 2] = low.astype(BF16)
    st_o[:, INNER // 2 :] = high.astype(BF16)
    c = silu(conv[:, tile(PAIRS + 1)])
    inflow = jnp.exp(log[...]) * mk[:, 3:4]
    total = jnp.zeros((rows, LANES), F32)
    for j in range(PAIRS):
        state = (low if j < PAIRS // 2 else high)[:, tile(j % (PAIRS // 2))]
        y = yw[:, tile(j)] + fine(dot, c, state) * spread(inflow, j)
        y_o[:, tile(j)] = y
        v = y * silu(z[:, tile(j)].astype(F32))
        gated[:, tile(j)] = v
        total = total + v * v
    inv = lax.rsqrt(jnp.sum(total, axis=-1, keepdims=True) / INNER + EPS)
    for j in range(PAIRS):
        gn_o[:, tile(j)] = (gated[:, tile(j)] * inv * gg[0:1, tile(j)]).astype(BF16)


def post_back_kernel(ggn, y, z, gg, conv, log, mk, me, gy_o, gz_o, rows_o, total_o, keep_o, msg_o, ge):
    rows = mk.shape[0]
    logv = log[...]
    inflow = jnp.exp(logv) * mk[:, 3:4]
    total = jnp.zeros((rows, LANES), F32)
    cross = jnp.zeros((rows, LANES), F32)
    for j in range(PAIRS):
        v = y[:, tile(j)] * silu(z[:, tile(j)].astype(F32))
        total = total + v * v
        cross = cross + v * ggn[:, tile(j)] * gg[0:1, tile(j)]
    inv = lax.rsqrt(jnp.sum(total, axis=-1, keepdims=True) / INNER + EPS)
    mean = jnp.sum(cross, axis=-1, keepdims=True) * inv / INNER
    for j in range(PAIRS):
        zf = z[:, tile(j)].astype(F32)
        s = sigmoid(zf)
        sz = zf * s
        yv = y[:, tile(j)]
        n = yv * sz * inv
        up = ggn[:, tile(j)]
        gga = inv * (up * gg[0:1, tile(j)] - n * mean)
        gy = gga * sz
        gz_o[:, tile(j)] = (gga * yv * (s * (1.0 + zf * (1.0 - s)))).astype(BF16)
        gy_o[:, tile(j)] = gy.astype(BF16)
        ge[:, tile(j)] = (gy * spread(inflow, j)).astype(BF16)
        rows_o[0:1, tile(j)] = jnp.sum(up * n, axis=0, keepdims=True)
        rows_o[1:2, tile(j)] = jnp.sum(gy * silu(conv[:, tile(j)]), axis=0, keepdims=True)
    rows_o[2:8, :] = jnp.zeros((6, INNER), F32)
    c_cols = silu(conv[:, tile(PAIRS + 1)]).T.astype(BF16)
    state = dot(c_cols, ge[...])
    keep = spread_row(jnp.exp(logv[rows - 1 : rows, :]) * mk[rows - 1 : rows, 3:4])
    emit_halves(state, keep, bit_of(me, 1), total_o, keep_o, msg_o)


def within_back_kernel(conv, dt, log, gy, st, mk, sr, gxdt_o, gb_o, gc_o, gl_o, xdt, ge, lcol, lrow, gscore, lsum, csum):
    rows = mk.shape[0]
    bf = silu(conv[:, tile(PAIRS)])
    cf = silu(conv[:, tile(PAIRS + 1)])
    b, c = bf.astype(BF16), cf.astype(BF16)
    scores = fine(dot_t, bf, cf)
    same = mk[:, 5:6] == sr[0:1, :]
    bias = jnp.where(jnp.logical_and(triangle(rows, False), same), 0.0, FAR)
    dtv, logv = dt[...], log[...]
    lrow[...] = logv.T
    inflow = jnp.exp(logv) * mk[:, 3:4]
    flow = jnp.zeros((rows, LANES), F32)
    for j in range(PAIRS):
        xdt[:, tile(j)] = (silu(conv[:, tile(j)]) * spread(dtv, j)).astype(BF16)
        gyv = gy[:, tile(j)].astype(F32) * spread(inflow, j)
        ge[:, tile(j)] = gyv.astype(BF16)
        flow = flow + head_sums(gyv * dot(c, st[:, tile(j)]), j)
    for h in range(HEADS):
        lcol[h] = jnp.broadcast_to(logv[:, h : h + 1], (rows, LANES))
    lanes = lanes_of(rows)
    low = lanes < HEAD_DIM
    gscore[...] = jnp.zeros_like(gscore)
    csum[...] = jnp.zeros_like(csum)
    lsum[...] = jnp.zeros_like(lsum)

    def pair(j, _):
        at = pl.ds(pl.multiple_of(j * LANES, LANES), LANES)
        xp, gp = xdt[:, at], gy[:, at]
        res = []
        for q in range(2):
            h = 2 * j + q
            span = lrow[pl.ds(h, 1), :] - jnp.concatenate([lcol[h]] * (rows // LANES), axis=1)
            decay = jnp.exp(span + bias)
            mix = scores * decay
            own = jnp.where(low if q == 0 else jnp.logical_not(low), gp, jnp.zeros_like(gp))
            gmix = dot_t(xp, own)
            gscore[...] += gmix * decay
            term = gmix * mix
            lsum[pl.ds(h, 1), :] = jnp.sum(term, axis=0, keepdims=True)
            csum[...] += jnp.where(lanes == h, jnp.sum(term, axis=1, keepdims=True), 0.0)
            res.append(dot(mix.astype(BF16), gp))
        gxdt_o[:, at] = jnp.where(low, res[0], res[1])
        return 0

    lax.fori_loop(0, PAIRS, pair, 0)
    gs = gscore[...]
    gb_o[...] = dot(gs.astype(BF16), c)
    gc_o[...] = dot(gs.T.astype(BF16), b) + dot_t(ge[...], st[...])
    gl_o[...] = lsum[...].T - csum[...] + flow


def mixer_back_kernel(
    mine, recv, gxdt, gbi, gci, gli, gy, conv, dt, log, st, pc, cw, hp, mk, me,
    gp_o, wide_o, head_o, gb16, xe, acc,
):
    rows = mk.shape[0]
    marks = mk[...]
    low, high = join_halves(mine, recv, bit_of(me, 1))
    half = INNER // 2
    kg = jnp.zeros((8, LANES), F32)
    for part, value in ((0, low), (half, high)):
        gb16[:, part : part + half] = value.astype(BF16)
        rowsum = jnp.sum(value * st[:, part : part + half].astype(F32), axis=0, keepdims=True)
        for j in range(PAIRS // 2):
            pair = part // LANES + j
            kg = kg + head_sums(jnp.broadcast_to(rowsum[:, tile(j)], (8, LANES)), pair)
    dtv, logv = dt[...], log[...]
    last = logv[rows - 1 : rows, :]
    b = silu(conv[:, tile(PAIRS)]).astype(BF16)
    outflow = marks[:, 4:5] * jnp.exp(last - logv)
    gv = jnp.zeros((rows, LANES), F32)
    gd = jnp.zeros((rows, LANES), F32)

    def conv_back(j, gact, s, out):
        gco = gact * (s * (1.0 + out * (1.0 - s)))
        ext = pc[:, tile(j)].astype(F32)
        acc[...] = jnp.zeros_like(acc)
        for k in range(CONV_K):
            gk = gco if k == CONV_K - 1 else gco * marks[:, k : k + 1]
            wide_o[k : k + 1, tile(j)] = jnp.sum(gk * ext[LEAD + k : LEAD + k + rows, :], axis=0, keepdims=True)
            acc[LEAD + k : LEAD + k + rows, :] += gk * cw[k : k + 1, tile(j)]
        wide_o[4:5, tile(j)] = jnp.sum(gco, axis=0, keepdims=True)
        gp_o[:, tile(j)] = acc[...].astype(BF16)

    wide_o[5:8, :] = jnp.zeros((3, CONV_CH), F32)
    for j in range(PAIRS):
        out = conv[:, tile(j)]
        s = sigmoid(out)
        x = out * s
        dtp = spread(dtv, j)
        flow = spread(outflow, j)
        xd = x * dtp
        gxs = dot(b, gb16[:, tile(j)]) * flow
        xe[:, tile(j)] = (xd * flow).astype(BF16)
        gxd = gxdt[:, tile(j)] + gxs
        gv = gv + head_sums(xd * gxs, j)
        gd = gd + head_sums(x * gxd, j)
        conv_back(j, dtp * gxd + spread(hp[2:3, :], j) * gy[:, tile(j)].astype(F32), s, out)
    gb = gbi[...] + dot_t(xe[...], gb16[...])
    for j, grad in ((PAIRS, gb), (PAIRS + 1, gci[...])):
        out = conv[:, tile(j)]
        conv_back(j, grad, sigmoid(out), out)
    keep = jnp.exp(last) * marks[rows - 1 : rows, 3:4]
    edge = jnp.sum(gv, axis=0, keepdims=True) + kg[0:1, :] * keep
    place = lax.broadcasted_iota(jnp.int32, (rows, LANES), 0)
    gl = gli[...] - gv + jnp.where(place == rows - 1, edge, 0.0)
    ga = dot(triangle(rows, False).astype(F32), gl, EXACT)
    rate = hp[1:2, :]
    raw = pc[HALO:, CONV_CH:WIDE].astype(F32) + hp[0:1, :]
    graw = jnp.where(lanes_of(rows) < HEADS, (ga * rate + gd) * sigmoid(raw), 0.0)
    gp_o[0:HALO, CONV_CH:WIDE] = jnp.zeros((HALO, LANES), BF16)
    gp_o[HALO:, CONV_CH:WIDE] = graw.astype(BF16)
    head_o[0:1, :] = jnp.sum(graw, axis=0, keepdims=True)
    head_o[1:2, :] = rate * jnp.sum(ga * dtv, axis=0, keepdims=True)
    head_o[2:8, :] = jnp.zeros((6, LANES), F32)


def row_of(values, rows=8):
    pad = [(0, rows - values.shape[0]), (0, max(0, LANES - values.shape[1]))]
    return jnp.pad(values.astype(F32), pad)


def per_device(
    hidden, segment_ids, in_weight, out_weight, conv_weight, conv_bias, norm_gain, gate_gain,
    dt_bias, a_log, skip_param, cotangent,
):
    layers_n, in_rows = in_weight.shape[:2]
    out_rows = out_weight.shape[1]
    rows, width = hidden.shape
    count = lax.axis_size("seq")
    me = lax.axis_index("seq")
    me_ref = me.reshape(1).astype(jnp.int32)
    conv_n = conv_bias.shape[1]

    small = jnp.concatenate(
        [conv_weight.reshape(-1), conv_bias.reshape(-1), norm_gain.reshape(-1), gate_gain.reshape(-1)]
    )
    per_row = HEADS
    small = jnp.pad(small, (0, in_rows * per_row - small.shape[0])).reshape(in_rows, per_row)
    side = [in_weight[layer, :, INNER:] for layer in range(layers_n)]
    shards = [
        jnp.pad(
            jnp.concatenate([side[layer], small], axis=1) if layer == 0 else side[layer],
            ((0, 0), (0, WIDE - SIDE - (per_row if layer == 0 else 0))),
        )
        for layer in range(layers_n)
    ]
    halo = shifted(hidden[rows - HALO :], 1)
    seg_halo = shifted(segment_ids[rows - HALO :] + 1, 1) - 1
    first_side = gather_side(shards[0])

    packs = [
        jnp.concatenate(
            [in_weight[layer, :, : INNER // 2], in_weight[layer, :, INNER // 2 : INNER], out_weight[layer]], axis=0
        )
        for layer in range(layers_n)
    ]
    gathered = [lax.all_gather(pack, "seq") for pack in packs]

    seg_pad = jnp.concatenate([seg_halo[LEAD:], segment_ids])
    before = seg_pad[CONV_K - 2]
    columns = [seg_pad[k : k + rows] == segment_ids for k in range(CONV_K - 1)]
    columns += [segment_ids == before, segment_ids == segment_ids[-1], segment_ids]
    marks = jnp.pad(jnp.stack([col.astype(F32) for col in columns], axis=1), ((0, 0), (0, LANES - 6)))
    seg_row = jnp.broadcast_to(segment_ids.astype(F32)[None, :], (8, rows))

    order = relative_order(count, me, in_rows)
    out_order = relative_order(count, me, out_rows)

    (left, left2), (right, right2) = first_side
    at = slice(SIDE - CUT, SIDE - CUT + per_row)
    smalls = jnp.concatenate([right[:, at], right2[:, at]], axis=0).reshape(count, in_rows * per_row)
    place = (jnp.arange(count)[:, None] == (jnp.asarray(relative_places(count)) ^ me)[None, :]).astype(BF16)
    smalls = dot(place, smalls)
    sizes = [layers_n * CONV_K * conv_n, layers_n * conv_n, layers_n * in_rows, layers_n * out_rows]
    cuts = np.cumsum([0] + sizes)
    taps, biases, gains, gate_gains = (smalls[:, cuts[i] : cuts[i + 1]] for i in range(4))
    taps = taps.reshape(count, layers_n, CONV_K, conv_n).transpose(1, 2, 0, 3).reshape(layers_n, CONV_K, CONV_CH)
    biases = biases.reshape(count, layers_n, 1, conv_n).transpose(1, 2, 0, 3).reshape(layers_n, 1, CONV_CH)
    conv_rows = jnp.pad(jnp.concatenate([taps, biases], axis=1), ((0, 0), (0, 3), (0, 0)))
    gains = gains.reshape(count, layers_n, in_rows).transpose(1, 0, 2).reshape(layers_n, 1, width)
    gate_gains = gate_gains.reshape(count, layers_n, out_rows).transpose(1, 0, 2).reshape(layers_n, 1, INNER)
    gains = jnp.broadcast_to(gains, (layers_n, 8, width))
    gate_gains = jnp.broadcast_to(gate_gains, (layers_n, 8, INNER))

    scratch_wide = pltpu.VMEM((rows, INNER), BF16)
    scratch_cols = pltpu.VMEM((HEADS, rows, LANES), F32)
    scratch_rows = pltpu.VMEM((LANES, rows), F32)

    residual = hidden
    saved = []
    for layer in range(layers_n):
        if layer == 0:
            sides = first_side
        precise = layer + 1 < layers_n
        gain, gate = gains[layer], gate_gains[layer]
        (normed,) = kernel_call(norm_kernel, [((HALO + rows, width), BF16)], (residual, halo, gain), limit=16)
        normed_rel = dot(normed, order).astype(BF16)
        lower, upper = normed_rel[:, : width // 2], normed_rel[:, width // 2 :]
        (left, left2), (right, right2) = sides
        pc = jnp.concatenate(
            [(dot(lower, left) + dot(upper, left2)).astype(BF16), (dot(lower, right) + dot(upper, right2)).astype(BF16)],
            axis=1,
        )
        heads = jnp.stack([dt_bias[layer], -jnp.exp(a_log[layer]), skip_param[layer]])
        hp = row_of(heads)
        conv, dt, log, total, keep, msg = kernel_call(
            partial(conv_state_kernel, precise=precise),
            [((rows, CONV_CH), F32), ((rows, LANES), F32), ((rows, LANES), F32)] + state_outs(INNER // 2, F32),
            (pc, conv_rows[layer], hp, marks, me_ref),
            scratch=[scratch_wide] * (2 if precise else 1), flops=2 * rows * STATE * INNER * 8,
        )
        mine, recv = exchange(total, keep, msg, me_ref, False)
        if layer + 1 < layers_n:
            shard, _ = lax.optimization_barrier((shards[layer + 1], total))
            next_sides = gather_side(shard)
        pack = gathered[layer]
        z_low = pack[:, :in_rows].reshape(width, INNER // 2)
        z_high = pack[:, in_rows : 2 * in_rows].reshape(width, INNER // 2)
        out_w = pack[:, 2 * in_rows :].reshape(INNER, width)
        own = normed[HALO:]
        z = jnp.concatenate([dot(own, z_low).astype(BF16), dot(own, z_high).astype(BF16)], axis=1)
        (yw,) = kernel_call(
            partial(within_kernel, precise=precise), [((rows, INNER), F32)], (conv, dt, log, hp, marks, seg_row),
            scratch=[scratch_wide, scratch_cols, scratch_rows] + [scratch_wide] * precise,
            flops=2 * rows * rows * INNER * 16,
        )
        y, gnormed, state = kernel_call(
            post_kernel,
            [((rows, INNER), F32), ((rows, INNER), BF16), ((STATE, INNER), BF16)],
            (yw, mine, recv, conv, log, marks, z, gate, me_ref),
            scratch=[pltpu.VMEM((rows, INNER), F32)], flops=2 * rows * STATE * INNER * 8,
        )
        saved.append((residual, normed, normed_rel, pc, conv, dt, log, hp, z, y, gnormed, state, z_low, z_high, out_w, sides))
        residual = residual.astype(F32) + dot(gnormed, out_w)
        if layer + 1 < layers_n:
            halo = shifted(residual[rows - HALO :], 1)
            sides = next_sides

    grad = cotangent
    in_grads, out_grads, smalls = [None] * layers_n, [None] * layers_n, [None] * layers_n
    for layer in range(layers_n - 1, -1, -1):
        h, normed, normed_rel, pc, conv, dt, log, hp, z, y, gnormed, state, z_low, z_high, out_w, sides = saved[layer]
        gain, gate = gains[layer], gate_gains[layer]
        mixed = grad.astype(BF16)
        ggn = dot_t(mixed, out_w)
        gy, gz, wide_rows, total, keep, msg = kernel_call(
            post_back_kernel,
            [((rows, INNER), BF16), ((rows, INNER), BF16), ((8, INNER), F32)] + state_outs(INNER // 2, BF16),
            (ggn, y, z, gate, conv, log, marks, me_ref),
            scratch=[scratch_wide], flops=2 * rows * STATE * INNER * 8,
        )
        mine, recv = exchange(total, keep, msg, me_ref, True)
        gn_rel = dot(gnormed, out_order).astype(BF16)
        out_term = lax.dot_general(gn_rel, mixed, (((0,), (0,)), ((), ())), preferred_element_type=F32).astype(BF16)
        z_term = lax.dot_general(
            normed_rel[HALO:], gz, (((0,), (0,)), ((), ())), preferred_element_type=F32
        ).astype(BF16)
        z_share = reduce_shares(z_term, ("x", "y"))
        out_share = reduce_shares(out_term, ("y", "x"))
        gxdt, gb, gc, gl = kernel_call(
            within_back_kernel,
            [((rows, INNER), F32), ((rows, LANES), F32), ((rows, LANES), F32), ((rows, LANES), F32)],
            (conv, dt, log, gy, state, marks, seg_row),
            scratch=[
                scratch_wide, scratch_wide, scratch_cols, scratch_rows,
                pltpu.VMEM((rows, rows), F32), scratch_rows, pltpu.VMEM((rows, LANES), F32),
            ],
            flops=2 * rows * rows * INNER * 32,
        )
        gn_z = dot_t(gz[:, : INNER // 2], z_low) + dot_t(gz[:, INNER // 2 :], z_high)
        gp, conv_grads, head_grads = kernel_call(
            mixer_back_kernel,
            [((HALO + rows, WIDE), BF16), ((8, CONV_CH), F32), ((8, LANES), F32)],
            (mine, recv, gxdt, gb, gc, gl, gy, conv, dt, log, state, pc, conv_rows[layer], hp, marks, me_ref),
            scratch=[pltpu.VMEM((STATE, INNER), BF16), scratch_wide, pltpu.VMEM((HALO + rows, LANES), F32)],
            flops=2 * rows * STATE * INNER * 24,
        )
        spilled = shifted(gp[:HALO], -1)
        side_left = lax.dot_general(
            normed_rel, gp[:, :CUT], (((0,), (0,)), ((), ())), preferred_element_type=F32
        ).astype(BF16)
        side_right = lax.dot_general(
            normed_rel, gp[:, CUT:], (((0,), (0,)), ((), ())), preferred_element_type=F32
        ).astype(BF16)
        left_share = reduce_shares(side_left, ("x", "y"))
        right_share = reduce_shares(side_right, ("y", "x"))
        gp_own = jnp.concatenate([gp[HALO:rows], gp[rows:] + spilled], axis=0)
        (left, left2), (right, right2) = sides
        gp_left, gp_right = gp_own[:, :CUT], gp_own[:, CUT:]
        gn_rel = jnp.concatenate(
            [dot_t(gp_left, left) + dot_t(gp_right, right), dot_t(gp_left, left2) + dot_t(gp_right, right2)], axis=1
        )
        gn_high = gn_rel.astype(BF16)
        gn_low = (gn_rel - gn_high.astype(F32)).astype(BF16)
        gn = gn_z + dot_t(gn_high, order) + dot_t(gn_low, order)
        grad, gain_rows = kernel_call(
            norm_back_kernel, [((rows, width), F32), ((8, width), F32)], (gn, h, grad, gain), limit=24,
        )
        in_grads[layer] = jnp.concatenate([z_share, left_share, right_share[:, : SIDE - CUT]], axis=1)
        out_grads[layer] = out_share
        skip_grad = wide_rows[1].reshape(HEADS, HEAD_DIM).sum(axis=1)
        smalls[layer] = jnp.concatenate(
            [
                conv_grads[: CONV_K + 1].reshape(-1), gain_rows[0], wide_rows[0],
                head_grads[0, :HEADS], head_grads[1, :HEADS], skip_grad,
            ]
        )
    flat = jnp.stack(smalls)
    length = flat.shape[1]
    padded = -(-length // LANES) * LANES
    sums = sum_all(jnp.pad(flat, ((0, 0), (0, padded - length))).reshape(-1, LANES))
    sums = sums.reshape(layers_n, padded)

    def share(start, span):
        full = sums[:, start : start + span]
        return lax.dynamic_slice_in_dim(full, me * (span // count), span // count, 1)

    tap_sums = sums[:, : CONV_K * CONV_CH].reshape(layers_n, CONV_K, CONV_CH)
    tap_share = lax.dynamic_slice_in_dim(tap_sums, me * conv_n, conv_n, 2)
    at = CONV_K * CONV_CH
    bias_share = share(at, CONV_CH)
    gain_share = share(at + CONV_CH, width)
    gate_share = share(at + CONV_CH + width, INNER)
    at = at + CONV_CH + width + INNER
    return (
        residual, grad, jnp.stack(in_grads), jnp.stack(out_grads), tap_share, bias_share, gain_share, gate_share,
        sums[:, at : at + HEADS], sums[:, at + HEADS : at + 2 * HEADS], sums[:, at + 2 * HEADS : at + 3 * HEADS],
    )


def solution(mesh):
    return jax.shard_map(
        per_device,
        mesh=mesh,
        in_specs=(
            P("seq", None), P("seq"), P(None, "seq", None), P(None, "seq", None), P(None, None, "seq"),
            P(None, "seq"), P(None, "seq"), P(None, "seq"), P(), P(), P(), P("seq", None),
        ),
        out_specs=(
            P("seq", None), P("seq", None), P(None, "seq", None), P(None, "seq", None), P(None, None, "seq"),
            P(None, "seq"), P(None, "seq"), P(None, "seq"), P(), P(), P(),
        ),
        check_vma=False,
    )
```

```python
from functools import partial

import jax
import jax.numpy as jnp
import numpy as np
from jax import lax
from jax.experimental import pallas as pl
from jax.experimental.pallas import tpu as pltpu
from jax.sharding import PartitionSpec as P

HEADS = 32
HEAD_DIM = 64
STATE = 128
CONV_K = 4
INNER = 2048
CONV_CH = 2304
SIDE = CONV_CH + HEADS
WIDE = 2432
CUT = 1280
LANES = 128
PAIRS = HEADS // 2
HALO = 16
LEAD = HALO - (CONV_K - 1)
FAR = -1e30

EPS = 1e-05
F32 = jnp.float32
BF16 = jnp.bfloat16
EXACT = lax.Precision.HIGHEST
MB = 1024 * 1024
CAP = 16 * MB


def axes_of(count):
    side = 4 if count >= 128 else 2
    plane = 2 * side * side
    return {"c": (2, 1), "x": (side, 2), "y": (side, 2 * side), "z": (count // plane, plane)}


def swap(value, flip):
    count = lax.axis_size("seq")
    return lax.ppermute(value, "seq", [(i, i ^ flip) for i in range(count)])


def shifted(shard, by):
    count = lax.axis_size("seq")
    return lax.ppermute(shard, "seq", [(i, i + by) for i in range(count) if 0 <= i + by < count])


def relative_places(count):
    axes = axes_of(count)
    places = np.zeros((1,), np.int32)
    for name in ("c", "y", "x", "z"):
        size, shift = axes[name]
        places = (places[:, None] + np.arange(size, dtype=np.int32)[None, :] * shift).reshape(-1)
    return places


def column_order(places, me, block):
    count = len(places)
    places = jnp.asarray(np.repeat(places, block))
    inner = jnp.asarray(np.tile(np.arange(block, dtype=np.int32), count))
    source = (places ^ me) * block + inner
    return (jnp.arange(count * block)[:, None] == source[None, :]).astype(BF16)


class Gather:

    def __init__(self, shard):
        self.axes = axes_of(lax.axis_size("seq"))
        self.rows = shard.shape[0]
        self.kind = shard.dtype
        self.shard, self.sent = shard, self.send(shard, "z")

    def send(self, value, name):
        size, shift = self.axes[name]
        return [swap(value, d * shift) for d in range(1, size)]

    def outs(self, *lead):
        return [((*lead, self.rows, CUT), self.kind), ((*lead, self.rows, WIDE - CUT), self.kind)]

    def line(self, deps=()):
        everything = slice(None)
        cuts = ((everything, slice(0, CUT)), (everything, slice(CUT, WIDE)))
        pieces = [
            (value, side, cuts[side], d) for side in range(2) for d, value in enumerate([self.shard, *self.sent])
        ]
        self.left, self.right = copies_call(pieces, self.outs(self.axes["z"][0]), deps)
        self.sent = self.send(self.left, "x"), self.send(self.right, "y")
        return self.left

    def plane(self, deps=()):
        sides = ((self.left, *self.sent[0]), (self.right, *self.sent[1]))
        pieces = [(value, side, None, d) for side in range(2) for d, value in enumerate(sides[side])]
        line, across, up = (self.axes[name][0] for name in ("z", "x", "y"))
        outs = [self.outs(across, line)[0], self.outs(up, line)[1]]
        self.left, self.right = copies_call(pieces, outs, deps)
        self.sent = self.send(self.left, "y"), self.send(self.right, "x")
        return self.left

    def whole(self, deps=()):
        line, across, up = (self.axes[name][0] for name in ("z", "x", "y"))
        pieces = [(value, 0, None, d) for d, value in enumerate([self.left, *self.sent[0]])]
        pieces += [
            (value, 1, i, (i, d)) for d, value in enumerate([self.right, *self.sent[1]]) for i in range(up)
        ]
        left, right = copies_call(pieces, self.outs(up, across, line), deps)
        left, right = left.reshape(-1, left.shape[-1]), right.reshape(-1, right.shape[-1])
        return (left, swap(left, 1)), (right, swap(right, 1))


class Shares:

    def __init__(self, keep, send):
        line, plane = axes_of(lax.axis_size("seq"))["z"]
        self.groups = [(plane // 2, 2), (line, plane)]
        shape = (plane // 2, line, keep.shape[0] // (plane // 2 * line), keep.shape[1])
        self.send = send
        self.terms = [keep.reshape(shape), swap(send.reshape(shape), 1)]

    def step(self, deps=(), behind=None):
        size, shift = self.groups.pop(0)
        if deps:
            pieces = list(
                kernel_call(pieces_kernel, [(self.terms[0].shape[1:], BF16)] * size, self.terms, deps=deps)
            )
        else:
            none = 0.0
            if behind is not None:
                none = jnp.minimum(jnp.abs(behind[(0,) * behind.ndim].astype(F32)), 0.0)
            pieces = []
            for d in range(size):
                picked = [t[d].astype(F32) for t in self.terms]
                pieces.append((sum(picked[1:], picked[0]) + none).astype(BF16))
        self.terms = [pieces[0]] + [swap(pieces[d], d * shift) for d in range(1, size)]
        return pieces


def pieces_kernel(*refs):
    size = refs[0].shape[0]
    terms, outs = refs[:-size], refs[-size:]
    for d, out in enumerate(outs):
        total = terms[0][d].astype(F32)
        for term in terms[1:]:
            total = total + term[d].astype(F32)
        out[...] = total.astype(BF16)


def turned_dot(left, right):
    return lax.dot_general(left, right, (((0,), (0,)), ((), ())), preferred_element_type=F32).astype(BF16)


def share_terms(left, right):
    half = left.shape[1] // 2
    return Shares(turned_dot(left[:, :half], right), turned_dot(left[:, half:], right))


def plane_first(count):
    plane = axes_of(count)["z"][1]
    return np.arange(count).reshape(-1, plane).T.reshape(-1)


def scatter_planes(grad):
    count = lax.axis_size("seq")
    plane = axes_of(count)["z"][1]
    groups = np.arange(count).reshape(-1, plane).tolist()
    return lax.psum_scatter(grad, "seq", scatter_dimension=0, tiled=True, axis_index_groups=groups)


def scatter_lines(grad):
    count = lax.axis_size("seq")
    plane = axes_of(count)["z"][1]
    groups = np.arange(count).reshape(-1, plane).T.tolist()
    return lax.psum_scatter(grad, "seq", scatter_dimension=0, tiled=True, axis_index_groups=groups)


def round_kernel(value, out):
    out[...] = value[...].astype(BF16)


def add_kernel(left, right, *outs):
    total = left[...].astype(F32) + right[...].astype(F32)
    for out in outs:
        out[...] = total.astype(out.dtype)


def sum_rounds(value, first, last, deps=()):
    flip = first
    while flip >= last:
        kind = BF16 if flip > 1 else F32
        (value,) = kernel_call(add_kernel, [(value.shape, kind)], (value, swap(value, flip)), deps=deps)
        flip, deps = flip // 2, ()
    return value


def gather_small(value):
    flip = 1
    while flip < lax.axis_size("seq"):
        value = jnp.concatenate([value, swap(value, flip)], axis=0)
        flip *= 2
    return value


def held_bytes(shape, kind):
    *lead, rows, lanes = (1, *shape) if len(shape) < 2 else shape
    rows, lanes = -(-rows // 16) * 16, -(-lanes // LANES) * LANES
    return int(np.prod(lead, dtype=np.int64)) * rows * lanes * jnp.dtype(kind).itemsize


def room_for(arrays, scratch):
    total = sum(held_bytes(*a) for a in arrays) + sum(held_bytes(r.shape, r.dtype) for r in scratch)
    return total + total // 8 + 3 * MB


def far(array):
    return pltpu.with_memory_space_constraint(array, pltpu.HBM)


def kernel_call(body, outs, args, scratch=(), flops=0, deps=()):
    places = [pltpu.SMEM if a.dtype == jnp.int32 else pltpu.VMEM for a in args] + [pl.ANY] * len(deps)
    known = len(args)

    def run(*refs):
        body(*refs[:known], *refs[known + len(deps) :])

    size = sum(int(np.prod(a.shape)) * a.dtype.itemsize for a in args) + sum(
        int(np.prod(o[0])) * jnp.dtype(o[1]).itemsize for o in outs
    )
    return pl.pallas_call(
        run,
        out_shape=tuple(jax.ShapeDtypeStruct(*o) for o in outs),
        in_specs=[pl.BlockSpec(memory_space=p) for p in places],
        out_specs=tuple(pl.BlockSpec(memory_space=pltpu.VMEM) for _ in outs),
        scratch_shapes=list(scratch),
        compiler_params=pltpu.CompilerParams(vmem_limit_bytes=min(CAP, room_for([(a.shape, a.dtype) for a in args] + list(outs), scratch))
        ),
        cost_estimate=pl.CostEstimate(flops=flops, bytes_accessed=size, transcendentals=0),
    )(*args, *deps)


def streamed_call(body, outs, args, scratch=(), flops=0, streamed=None, raw=()):
    places = [pltpu.SMEM if a.dtype == jnp.int32 else pltpu.VMEM for a in args]
    size = sum(int(np.prod(a.shape)) * a.dtype.itemsize for a in (*args, streamed)) + sum(
        int(np.prod(o[0])) * jnp.dtype(o[1]).itemsize for o in (*outs, *raw)
    )
    return pl.pallas_call(
        body,
        out_shape=tuple(jax.ShapeDtypeStruct(*o) for o in (*outs, *raw)),
        in_specs=[pl.BlockSpec(memory_space=p) for p in (pltpu.HBM, *places)],
        out_specs=tuple(pl.BlockSpec(memory_space=p) for p in [pltpu.VMEM] * len(outs) + [pltpu.HBM] * len(raw)),
        scratch_shapes=[*scratch, pltpu.SemaphoreType.DMA((3 * len(raw),))],
        compiler_params=pltpu.CompilerParams(vmem_limit_bytes=room_for([], scratch) + 8 * MB),
        cost_estimate=pl.CostEstimate(flops=flops, bytes_accessed=size, transcendentals=0),
    )(streamed, *args)


def copies_call(pieces, outs, deps=()):
    arrays = [p[0] for p in pieces]
    known, written = len(arrays), len(outs)

    def run(*refs):
        refs = refs[:known] + refs[known + len(deps) :]
        results, held, (sems, out_sems) = refs[known : known + written], refs[known + written : -2], refs[-2:]
        copies = []
        for k, (_, out, source, target) in enumerate(pieces):
            src = refs[k] if source is None else refs[k].at[source]
            copies.append(pltpu.make_async_copy(src, held[out].at[target], sems.at[k]))
            copies[-1].start()
        for copy in copies:
            copy.wait()
        copies = []
        for k in range(written):
            copies.append(pltpu.make_async_copy(held[k], results[k], out_sems.at[k]))
            copies[-1].start()
        for copy in copies:
            copy.wait()

    size = sum(2 * int(np.prod(o[0])) * jnp.dtype(o[1]).itemsize for o in outs)
    return pl.pallas_call(
        run,
        out_shape=tuple(jax.ShapeDtypeStruct(*o) for o in outs),
        in_specs=[pl.BlockSpec(memory_space=pltpu.HBM)] * known + [pl.BlockSpec(memory_space=pl.ANY)] * len(deps),
        out_specs=tuple(pl.BlockSpec(memory_space=pltpu.HBM) for _ in outs),
        scratch_shapes=[pltpu.VMEM(*o) for o in outs]
        + [pltpu.SemaphoreType.DMA((known,)), pltpu.SemaphoreType.DMA((written,))],
        compiler_params=pltpu.CompilerParams(vmem_limit_bytes=room_for(outs, ())),
        cost_estimate=pl.CostEstimate(flops=0, bytes_accessed=size, transcendentals=0),
    )(*arrays, *deps)


def copy_kernel(value, out):
    out[...] = value[...]


def after(value, *deps):
    return kernel_call(copy_kernel, [(value.shape, value.dtype)], (value,), deps=deps)[0]


def dot(left, right, precision=None):
    return jnp.dot(left, right, precision=precision, preferred_element_type=F32)


def dot_t(left, right):
    return lax.dot_general(left, right, (((1,), (1,)), ((), ())), preferred_element_type=F32)


def halves(value):
    high = value.astype(BF16)
    return high, (value - high.astype(F32)).astype(BF16)


def fine(form, left, right):
    (lh, ll), (rh, rl) = halves(left), halves(right)
    return form(lh, rh) + (form(ll, rh) + form(lh, rl))


def lanes_of(rows):
    return lax.broadcasted_iota(jnp.int32, (rows, LANES), 1)


def spread(values, pair):
    low = lanes_of(values.shape[0]) < HEAD_DIM
    return jnp.where(low, values[:, 2 * pair : 2 * pair + 1], values[:, 2 * pair + 1 : 2 * pair + 2])


def spread_row(row):
    return jnp.concatenate([spread(row, pair) for pair in range(PAIRS)], axis=1)


def head_sums(product, pair):
    rows = lax.broadcasted_iota(jnp.int32, (LANES, LANES), 0)
    cols = lax.broadcasted_iota(jnp.int32, (LANES, LANES), 1)
    pick = (cols == 2 * pair + (rows >= HEAD_DIM).astype(jnp.int32)).astype(BF16)
    high = product.astype(BF16)
    low = (product - high.astype(F32)).astype(BF16)
    return dot(high, pick) + dot(low, pick)


def sigmoid(v):
    return 1.0 / (1.0 + jnp.exp(-v))


def silu(v):
    return v * sigmoid(v)


def parted(j, parts):
    half = PAIRS // 2
    return parts[j // half], tile(j % half)


def tile(pair):
    return slice(pair * LANES, (pair + 1) * LANES)


def pack_row(row):
    first = row.astype(BF16).astype(F32)
    second = (row - first).astype(BF16).astype(F32)
    third = row - first - second
    place = lax.broadcasted_iota(jnp.int32, (16, row.shape[1]), 0)
    packed = jnp.where(place == 0, first, jnp.where(place == 1, second, third))
    return jnp.where(place < 3, packed, 0.0).astype(BF16)


def unpack_row(rows):
    return jnp.sum(rows.astype(F32), axis=0, keepdims=True)


def emit_msg(total, keep, msg_o):
    msg_o[0:STATE, :] = total.astype(msg_o.dtype)
    if msg_o.dtype == F32:
        msg_o[STATE:, :] = jnp.broadcast_to(keep, (msg_o.shape[0] - STATE, keep.shape[1]))
    else:
        msg_o[STATE:, :] = pack_row(keep)


def read_msg(recv):
    if recv.dtype == F32:
        return recv[0:STATE, :], recv[STATE : STATE + 1, :]
    return recv[0:STATE, :].astype(F32), unpack_row(recv[STATE:, :])


def emit_halves(total, keep, upper, own_o, msg_o):
    half = total.shape[1] // 2
    low, high = total[:, :half], total[:, half:]
    klow, khigh = keep[:, :half], keep[:, half:]
    emit_msg(jnp.where(upper, high, low), jnp.where(upper, khigh, klow), own_o)
    emit_msg(jnp.where(upper, low, high), jnp.where(upper, klow, khigh), msg_o)


def bit_of(me, flip):
    return (me[0] & flip) != 0


def state_out(width, kind=F32):
    return ((STATE + (8 if kind == F32 else 16), width), kind)


def in_order(relative, place, back):
    size = len(relative)
    ordered = []
    for step in range(size):
        member = size - 1 - step if back else step
        value = relative[0]
        for d in range(1, size):
            value = jnp.where(jnp.bitwise_xor(place, member) == d, relative[d], value)
        ordered.append(value)
    return ordered


def place_of(me, shift, size):
    return jnp.bitwise_and(lax.shift_right_logical(me[0], shift.bit_length() - 1), size - 1)


def pair_kernel(own, recv, me, first_o, mine_o, m1, m2, m3, joined, *, back):
    other, kother = read_msg(recv)
    mine, kmine = read_msg(own)
    first = jnp.logical_xor(bit_of(me, 1), not back)
    t_first, k_first = jnp.where(first, mine, other), jnp.where(first, kmine, kother)
    t_second, k_second = jnp.where(first, other, mine), jnp.where(first, kother, kmine)
    emit_msg(t_first, k_first, first_o)
    emit_msg(k_second * t_first + t_second, k_first * k_second, joined)
    place = place_of(me, 2, 4)
    width = mine_o.shape[1]
    for d, out in enumerate((mine_o, m1, m2, m3)):
        at = pl.ds(pl.multiple_of(jnp.bitwise_xor(place, d) * width, LANES), width)
        emit_msg(joined[0:STATE, at], joined[STATE : STATE + 1, at], out)


def scan_group(own, recvs, place, back):
    read = [read_msg(r) for r in (own, *recvs)]
    totals = in_order([r[0] for r in read], place, back)
    keeps = in_order([r[1] for r in read], place, back)
    prefixes, value, decay = [], jnp.zeros_like(totals[0]), jnp.ones_like(keeps[0])
    for t, k in zip(totals, keeps):
        prefixes.append((value, decay))
        value, decay = k * value + t, decay * k
    return prefixes, value, decay


def own_prefix(prefixes, place, back):
    size = len(prefixes)
    value, decay = prefixes[0]
    for step in range(1, size):
        mine = place == (size - 1 - step if back else step)
        value = jnp.where(mine, prefixes[step][0], value)
        decay = jnp.where(mine, prefixes[step][1], decay)
    return value, decay


def plane_kernel(mine, r1, r2, r3, me, pre_o, *outs, back):
    prefixes, value, decay = scan_group(mine, (r1, r2, r3), place_of(me, 2, 4), back)
    for step, (prefix, kprefix) in enumerate(prefixes):
        emit_msg(prefix, kprefix, pre_o.at[3 - step if back else step])
    for out in outs:
        emit_msg(value, decay, out)


def line_kernel(own, *refs, size, shift, back, carried, final):
    recvs, refs = refs[: size - 1], refs[size - 1 :]
    if carried:
        state, *refs = refs
    if final:
        pre, *refs = refs
    me, *outs = refs
    place = place_of(me, shift, size)
    prefixes, value, decay = scan_group(own, recvs, place, back)
    into, kinto = own_prefix(prefixes, place, back)
    if carried:
        before, kbefore = read_msg(state)
        into, kinto = kbefore * into + before, kbefore * kinto
    if not final:
        emit_msg(into, kinto, outs[0])
        for out in outs[1:]:
            emit_msg(value, decay, out)
        return
    plane = place_of(me, 2, 4)
    for d, out in enumerate(outs):
        prefix, kprefix = read_msg(pre.at[jnp.bitwise_xor(plane, d)])
        out[...] = (kprefix * into + prefix).astype(out.dtype)


def down_kernel(mine, r1, r2, r3, first, me, mine_o, msg_o, whole, *, back):
    place = place_of(me, 2, 4)
    width = mine.shape[1]
    for d, ref in enumerate((mine, r1, r2, r3)):
        at = pl.ds(pl.multiple_of(jnp.bitwise_xor(place, d) * width, LANES), width)
        whole[:, at] = ref[...].astype(F32)
    into = whole[...]
    t_first, k_first = read_msg(first)
    beyond = k_first * into + t_first
    second = jnp.logical_xor(bit_of(me, 1), back)
    mine_o[...] = jnp.where(second, beyond, into)
    msg_o[...] = jnp.where(second, into, beyond).astype(msg_o.dtype)


def join_halves(mine, recv, upper):
    theirs = recv[...].astype(F32)
    own = mine[...]
    return jnp.where(upper, theirs, own), jnp.where(upper, own, theirs)


def exchange(own, msg, me, back, deps=((), (), (), ())):
    count = lax.axis_size("seq")
    kind = msg.dtype
    width = INNER // 2
    quarter = width // 4
    part, message = state_out(quarter), state_out(quarter, kind)
    both = [message] if kind == F32 else [part, message]
    recv = swap(msg, 1)
    first, mine, *msgs = kernel_call(
        partial(pair_kernel, back=back), [state_out(width), part] + [message] * 3,
        (own, recv, me), deps=deps[0], scratch=[pltpu.VMEM(*state_out(width))],
    )
    recvs = [swap(m, 2 * (d + 1)) for d, m in enumerate(msgs)]
    pre, *totals = kernel_call(
        partial(plane_kernel, back=back), [((4, *part[0]), F32)] + both,
        (mine, *recvs, me), deps=deps[1],
    )
    carried = ()
    shift = 8
    while True:
        size = min(4, count // shift)
        recvs = [swap(totals[-1], shift * d) for d in range(1, size)]
        final = shift * size == count
        form = partial(line_kernel, size=size, shift=shift, back=back, carried=bool(carried), final=final)
        shift *= size
        if final:
            break
        state, *totals = kernel_call(form, [part] + both, (totals[0], *recvs, *carried, me))
        carried = (state,)
    mine, *msgs = kernel_call(
        form, [((STATE, quarter), F32)] + [((STATE, quarter), kind)] * 3,
        (totals[0], *recvs, *carried, pre, me), deps=deps[2],
    )
    recvs = [swap(m, 2 * (d + 1)) for d, m in enumerate(msgs)]
    mine, msg = kernel_call(
        partial(down_kernel, back=back), [((STATE, width), F32), ((STATE, width), kind)],
        (mine, *recvs, first, me), deps=deps[3], scratch=[pltpu.VMEM((STATE, width), F32)],
    )
    return mine, swap(msg, 1)


def norm_kernel(h, halo, gain, out):
    for ref, at in ((halo, slice(0, HALO)), (h, slice(HALO, HALO + h.shape[0]))):
        v = ref[...].astype(F32)
        inv = lax.rsqrt(jnp.mean(v * v, axis=-1, keepdims=True) + EPS)
        out[at, :] = (v * inv * gain[0:1, :]).astype(BF16)


def norm_back_kernel(gn, h, g, gain, wide, *refs):
    *others, out, wide_o = refs
    v = h[...].astype(F32)
    grad = gn[...]
    inv = lax.rsqrt(jnp.mean(v * v, axis=-1, keepdims=True) + EPS)
    n = v * inv
    q = grad * gain[0:1, :]
    out[...] = g[...] + inv * (q - n * jnp.mean(q * n, axis=-1, keepdims=True))
    wide_o[0:8, :] = wide[...]
    wide_o[6:7, 0 : v.shape[1]] = jnp.sum(grad * n, axis=0, keepdims=True)
    for other in others:
        wide_o[8:, :] = other[...]


def grads_kernel(gn, normed, mixed, gz, *outs, steps):
    half = INNER // 2
    several, rows = outs[0].shape[0], outs[0].shape[1] // 4
    for k, out in enumerate(outs):

        @pl.when(pl.program_id(0) // steps == k)
        def _(out=out):
            turned = lax.dot_general(gn[...], mixed[...], (((0,), (0,)), ((), ())), preferred_element_type=F32)
            out[:, 2 * rows :, :] = turned.astype(BF16).reshape(several, 2 * rows, half)
            narrow = normed[HALO:, :]
            for q in range(2):
                part = gz[:, q * half : (q + 1) * half]
                turned = lax.dot_general(narrow, part, (((0,), (0,)), ((), ())), preferred_element_type=F32)
                out[:, q * rows : (q + 1) * rows, :] = turned.astype(BF16).reshape(several, rows, half)


def grads_call(gn, normed, mixed, gz, count, parts):
    rows, half = mixed.shape
    wide = 2 * LANES
    several = wide * count // INNER
    steps = count // several // parts
    shape = (several, 4 * half // count, half)

    def share(k):
        return pl.BlockSpec(shape, lambda i: (jnp.clip(i - k * steps, 0, steps - 1), 0, 0))

    return pl.pallas_call(
        partial(grads_kernel, steps=steps),
        grid=(parts * steps,),
        out_shape=[jax.ShapeDtypeStruct((count // parts, *shape[1:]), BF16)] * parts,
        in_specs=[
            pl.BlockSpec((rows, wide), lambda i: (0, i)), pl.BlockSpec((HALO + rows, wide // 2), lambda i: (0, i)),
            pl.BlockSpec(mixed.shape, lambda i: (0, 0)), pl.BlockSpec(gz.shape, lambda i: (0, 0)),
        ],
        out_specs=[share(k) for k in range(parts)],
        compiler_params=pltpu.CompilerParams(vmem_limit_bytes=14 * MB),
        cost_estimate=pl.CostEstimate(flops=8 * rows * half * half, bytes_accessed=10 * MB, transcendentals=0),
    )(gn, normed, mixed, gz)


def own_rows_kernel(gp, spilled, gz, out, gz_o):
    gz_o[...] = gz[...]
    end = out.shape[0] - HALO
    out[0:end, :] = gp[HALO : HALO + end, :]
    out[end:, :] = (gp[HALO + end :, :].astype(F32) + spilled[...].astype(F32)).astype(BF16)


def shares_kernel(*refs, split):
    terms, (in_o, out_o) = refs[:-2], refs[-2:]
    layers_n, rows = in_o.shape[:2]
    half = INNER // 2
    at = 0
    for layer in range(layers_n):
        sums = []
        for size in split[layer]:
            total = terms[at][...].astype(F32)
            for term in terms[at + 1 : at + size]:
                total = total + term[...].astype(F32)
            sums.append(total)
            at += size
        pack, side = sums
        in_o[layer, :, 0:half] = pack[0:rows]
        in_o[layer, :, half:INNER] = pack[rows : 2 * rows]
        in_o[layer, :, INNER:] = side[:, :SIDE]
        out_o[layer] = pack[2 * rows :]


def triangle(rows, lower):
    r = lax.broadcasted_iota(jnp.int32, (rows, rows), 0)
    c = lax.broadcasted_iota(jnp.int32, (rows, rows), 1)
    return r >= c if lower else r <= c


def conv_state_kernel(pc, cw, hp, mk, me, left_o, right_o, bc_o, dt_o, log_o, own_o, msg_o, xw, *low, precise):
    rows = mk.shape[0]
    marks = mk[...]
    raw = pc[HALO:, CONV_CH:WIDE].astype(F32) + hp[0:1, :]
    soft = jnp.maximum(raw, 0.0) + jnp.log1p(jnp.exp(-jnp.abs(raw)))
    dt = jnp.where(lanes_of(rows) < HEADS, soft, 0.0)
    log = dot(triangle(rows, True).astype(F32), dt * hp[1:2, :], EXACT)
    last = log[rows - 1 : rows, :]
    weight = marks[:, 4:5] * jnp.exp(last - log) * dt
    dt_o[...] = dt
    log_o[...] = log
    b_cols = None
    for j in range(CONV_CH // LANES):
        ext = pc[:, tile(j)].astype(F32)
        out = cw[4:5, tile(j)] + cw[3:4, tile(j)] * ext[HALO:, :]
        for k in range(CONV_K - 1):
            out = out + cw[k : k + 1, tile(j)] * ext[LEAD + k : LEAD + k + rows, :] * marks[:, k : k + 1]
        part, at = parted(j, (left_o, right_o, bc_o))
        part[:, at] = out
        if j < PAIRS:
            high, rest = halves(silu(out) * spread(weight, j))
            xw[:, tile(j)] = high
            if precise:
                low[0][:, tile(j)] = rest
        elif j == PAIRS:
            b_cols, b_rest = halves(silu(out).T)
    total = dot(b_cols, xw[...])
    if precise:
        total = total + (dot(b_rest, xw[...]) + dot(b_cols, low[0][...]))
    keep = spread_row(jnp.exp(last) * marks[rows - 1 : rows, 3:4])
    emit_halves(total, keep, bit_of(me, 1), own_o, msg_o)


def mask_bias(mk, sr, rows):
    same = mk[:, 5:6] == sr[0:1, :]
    return jnp.where(jnp.logical_and(triangle(rows, True), same), 0.0, FAR)


def within_kernel(conv, bc, dt, log, hp, mk, sr, y_o, xdt, lcol, lrow, *lower, precise, first):
    rows = mk.shape[0]
    pairs = PAIRS // 2
    scores = fine(dot_t, silu(bc[:, tile(1)]), silu(bc[:, tile(0)]))
    bias = mask_bias(mk, sr, rows)
    dtv, logv = dt[...], log[...]
    lrow[...] = logv.T
    for j in range(pairs):
        x = silu(conv[:, tile(j)])
        high, rest = halves(x * spread(dtv, first + j))
        xdt[:, tile(j)] = high
        if precise:
            lower[0][:, tile(j)] = rest
        y_o[:, tile(j)] = x * spread(hp[2:3, :], first + j)
    for h in range(2 * pairs):
        lcol[h] = jnp.broadcast_to(logv[:, 2 * first + h : 2 * first + h + 1], (rows, LANES))
    low = lanes_of(rows) < HEAD_DIM

    def pair(j, _):
        at = pl.ds(pl.multiple_of(j * LANES, LANES), LANES)
        xp = xdt[:, at]
        res = []
        for q in range(2):
            col = lcol[2 * j + q]
            row = lrow[pl.ds(2 * (first + j) + q, 1), :]
            span = jnp.concatenate([col] * (rows // LANES), axis=1) - row
            mix = scores * jnp.exp(span + bias)
            if precise:
                high, rest = halves(mix)
                res.append(dot(high, xp) + (dot(rest, xp) + dot(high, lower[0][:, at])))
            else:
                res.append(dot(mix.astype(BF16), xp))
        y_o[:, at] += jnp.where(low, res[0], res[1])
        return 0

    lax.fori_loop(0, pairs, pair, 0)


def post_kernel(*refs, places, relative, spans, aligned):
    if spans:
        pack, *refs = refs
        *refs, gated, zbuf, obuf, sems = refs
        parts = len(spans) - 1
        refs, raw = [*refs[:-parts], gated], refs[-parts:]
    else:
        z_low, z_high, out_w, *refs = refs
    normed, h, yw, yw2, mine, recv, bc, log, mk, gg, me, z, y_o, gn_o, st_o, st2_o, h_o, *rel_o, gated = refs
    rows = mk.shape[0]
    wide = 2 * LANES
    half = INNER // 2
    own = normed[HALO:, :]
    flying = []

    def moved(source, target):
        copy = pltpu.make_async_copy(source, target, sems.at[len(flying)])
        flying.append(copy)
        copy.start()
        return copy

    def apart(buffer, base, k):
        return moved(buffer.at[:, spans[k] - base : spans[k + 1] - base, :], raw[k])

    if spans:
        coming = [moved(pack.at[:, spans[0] : spans[2], :], zbuf), moved(pack.at[:, spans[2] : spans[3], :], obuf)]
        coming[0].wait()
        leaving = [apart(zbuf, 0, 0), apart(zbuf, 0, 1)]

    def project(i, _):
        for q in range(2):
            at = pl.ds(pl.multiple_of(i * wide, wide), wide)
            if spans:
                part = zbuf[:, spans[q] : spans[q + 1], at]
                part = part.reshape(-1, part.shape[-1])
            else:
                part = (z_low, z_high)[q][:, at]
            z[:, pl.ds(pl.multiple_of(q * half + i * wide, wide), wide)] = dot(own, part).astype(BF16)
        return 0

    lax.fori_loop(0, half // wide, project, 0)
    if spans:
        for copy in leaving:
            copy.wait()
        more = len(spans) > 4
        if more:
            second = moved(pack.at[:, spans[3] : spans[5], :], zbuf)
        coming[1].wait()
        leaving = [apart(obuf, spans[2], 2)]
    low, high = join_halves(mine, recv, bit_of(me, 1))
    st_o[...] = low.astype(BF16)
    st2_o[...] = high.astype(BF16)
    c = silu(bc[:, tile(1)])
    inflow = jnp.exp(log[...]) * mk[:, 3:4]
    total = jnp.zeros((rows, LANES), F32)
    for j in range(PAIRS):
        part = (yw if j < PAIRS // 2 else yw2)[:, tile(j % (PAIRS // 2))]
        state = (low if j < PAIRS // 2 else high)[:, tile(j % (PAIRS // 2))]
        y = part + fine(dot, c, state) * spread(inflow, j)
        y_o[:, tile(j)] = y
        v = y * silu(z[:, tile(j)].astype(F32))
        gated[:, tile(j)] = v
        total = total + v * v
    inv = lax.rsqrt(jnp.sum(total, axis=-1, keepdims=True) / INNER + EPS)
    for j in range(PAIRS):
        gn_o[:, tile(j)] = (gated[:, tile(j)] * inv * gg[0:1, tile(j)]).astype(BF16)

    if spans and more:
        second.wait()
        leaving += [apart(zbuf, spans[3], 3), apart(zbuf, spans[3], 4)]

    def output(i, _):
        at = pl.ds(pl.multiple_of(i * wide, wide), wide)
        if spans:
            part = obuf[:, :, at]
            part = part.reshape(-1, part.shape[-1])
        else:
            part = out_w[:, at]
        h_o[:, at] = h[:, at].astype(F32) + dot(gn_o[...], part)
        return 0

    lax.fori_loop(0, h.shape[1] // wide, output, 0)
    if spans and more:
        leaving[0].wait()
        last = obuf.at[:, : spans[6] - spans[5], :]
        moved(pack.at[:, spans[5] : spans[6], :], last).wait()
        leaving = leaving[1:] + [moved(last, raw[5])]
    if rel_o:
        lower = lanes_of(rows) < HEAD_DIM
        for j in range(PAIRS):
            base = me[0] if relative else jnp.int32(0)
            sources = [jnp.bitwise_xor(base, jnp.int32(int(places[2 * j + q]))) for q in range(2)]
            upper = jnp.bitwise_and(sources[0], 1) == 1
            tiles = []
            for src in sources:
                at = pl.multiple_of(lax.shift_right_logical(src, 1) * LANES, LANES)
                tiles.append(gn_o[:, pl.ds(at, LANES)].astype(F32))
            left = jnp.where(upper, pltpu.roll(tiles[0], HEAD_DIM, 1), tiles[0])
            right = jnp.where(upper, tiles[1], pltpu.roll(tiles[1], HEAD_DIM, 1))
            rel_o[0][:, tile(j)] = jnp.where(lower, left, right).astype(BF16)
    if spans:
        for copy in leaving:
            copy.wait()


def post_back_kernel(ggn, y, z, gg, left, right, bc, log, mk, me, gy_o, gy2_o, gz_o, gate_o, skip_o, own_o, msg_o, ge):
    rows = mk.shape[0]
    logv = log[...]
    inflow = jnp.exp(logv) * mk[:, 3:4]
    total = jnp.zeros((rows, LANES), F32)
    cross = jnp.zeros((rows, LANES), F32)
    for j in range(PAIRS):
        v = y[:, tile(j)] * silu(z[:, tile(j)].astype(F32))
        total = total + v * v
        cross = cross + v * ggn[:, tile(j)] * gg[0:1, tile(j)]
    inv = lax.rsqrt(jnp.sum(total, axis=-1, keepdims=True) / INNER + EPS)
    mean = jnp.sum(cross, axis=-1, keepdims=True) * inv / INNER
    skips = jnp.zeros((8, LANES), F32)
    for j in range(PAIRS):
        zf = z[:, tile(j)].astype(F32)
        s = sigmoid(zf)
        sz = zf * s
        yv = y[:, tile(j)]
        n = yv * sz * inv
        up = ggn[:, tile(j)]
        gga = inv * (up * gg[0:1, tile(j)] - n * mean)
        gy = gga * sz
        gz_o[:, tile(j)] = (gga * yv * (s * (1.0 + zf * (1.0 - s)))).astype(BF16)
        part, at = parted(j, (gy_o, gy2_o))
        part[:, at] = gy.astype(BF16)
        ge[:, tile(j)] = (gy * spread(inflow, j)).astype(BF16)
        gate_o[:, tile(j)] = jnp.broadcast_to(jnp.sum(up * n, axis=0, keepdims=True), (8, LANES))
        part, at = parted(j, (left, right))
        through = jnp.sum(gy * silu(part[:, at]), axis=0, keepdims=True)
        skips = skips + head_sums(jnp.broadcast_to(through, (8, LANES)), j)
    skip_o[...] = skips
    c_cols = silu(bc[:, tile(1)]).T.astype(BF16)
    state = dot(c_cols, ge[...])
    keep = spread_row(jnp.exp(logv[rows - 1 : rows, :]) * mk[rows - 1 : rows, 3:4])
    emit_halves(state, keep, bit_of(me, 1), own_o, msg_o)


def within_back_kernel(
    conv, bc, dt, log, gy, st, mk, sr, gxdt_o, gb_o, gc_o, gl_o, xdt, ge, lcol, lrow, gscore, lsum, csum, *, first
):
    rows = mk.shape[0]
    pairs = PAIRS // 2
    bf, cf = silu(bc[:, tile(0)]), silu(bc[:, tile(1)])
    b, c = bf.astype(BF16), cf.astype(BF16)
    scores = fine(dot_t, bf, cf)
    same = mk[:, 5:6] == sr[0:1, :]
    bias = jnp.where(jnp.logical_and(triangle(rows, False), same), 0.0, FAR)
    dtv, logv = dt[...], log[...]
    lrow[...] = logv.T
    inflow = jnp.exp(logv) * mk[:, 3:4]
    flow = jnp.zeros((rows, LANES), F32)
    for j in range(pairs):
        xdt[:, tile(j)] = (silu(conv[:, tile(j)]) * spread(dtv, first + j)).astype(BF16)
        gyv = gy[:, tile(j)].astype(F32) * spread(inflow, first + j)
        ge[:, tile(j)] = gyv.astype(BF16)
        flow = flow + head_sums(gyv * dot(c, st[:, tile(j)]), first + j)
    for h in range(2 * pairs):
        lcol[h] = jnp.broadcast_to(logv[:, 2 * first + h : 2 * first + h + 1], (rows, LANES))
    lanes = lanes_of(rows)
    low = lanes < HEAD_DIM
    gscore[...] = jnp.zeros_like(gscore)
    csum[...] = jnp.zeros_like(csum)
    lsum[...] = jnp.zeros_like(lsum)

    def pair(j, _):
        at = pl.ds(pl.multiple_of(j * LANES, LANES), LANES)
        xp, gp = xdt[:, at], gy[:, at]
        res = []
        for q in range(2):
            h = 2 * (first + j) + q
            span = lrow[pl.ds(h, 1), :] - jnp.concatenate([lcol[2 * j + q]] * (rows // LANES), axis=1)
            decay = jnp.exp(span + bias)
            mix = scores * decay
            own = jnp.where(low if q == 0 else jnp.logical_not(low), gp, jnp.zeros_like(gp))
            gmix = dot_t(xp, own)
            gscore[...] += gmix * decay
            term = gmix * mix
            lsum[pl.ds(h, 1), :] = jnp.sum(term, axis=0, keepdims=True)
            csum[...] += jnp.where(lanes == h, jnp.sum(term, axis=1, keepdims=True), 0.0)
            res.append(dot(mix.astype(BF16), gp))
        gxdt_o[:, at] = jnp.where(low, res[0], res[1])
        return 0

    lax.fori_loop(0, pairs, pair, 0)
    gs = gscore[...]
    gb_o[...] = dot(gs.astype(BF16), c)
    gc_o[...] = dot(gs.T.astype(BF16), b) + dot_t(ge[...], st[...])
    gl_o[...] = lsum[...].T - csum[...] + flow


def mixer_back_kernel(
    gxdt2, gy2, right, pc, cw, gxdt, gbi, gci, gli, gbi2, gci2, gli2, mine, recv, gy, left, bc, dt, log, st, st2,
    hp, mk, gate, skip, me, gp_o, wide_o, gb16, xe, acc,
):
    rows = mk.shape[0]
    marks = mk[...]
    low, high = join_halves(mine, recv, bit_of(me, 1))
    half = INNER // 2
    kg = jnp.zeros((8, LANES), F32)
    for part, value in ((0, low), (half, high)):
        gb16[:, part : part + half] = value.astype(BF16)
        rowsum = jnp.sum(value * (st if part == 0 else st2)[...].astype(F32), axis=0, keepdims=True)
        for j in range(PAIRS // 2):
            pair = part // LANES + j
            kg = kg + head_sums(jnp.broadcast_to(rowsum[:, tile(j)], (8, LANES)), pair)
    dtv, logv = dt[...], log[...]
    last = logv[rows - 1 : rows, :]
    b = silu(bc[:, tile(0)]).astype(BF16)
    outflow = marks[:, 4:5] * jnp.exp(last - logv)
    gv = jnp.zeros((rows, LANES), F32)
    gd = jnp.zeros((rows, LANES), F32)

    def conv_back(j, gact, s, out):
        gco = gact * (s * (1.0 + out * (1.0 - s)))
        ext = pc[:, tile(j)].astype(F32)
        acc[...] = jnp.zeros_like(acc)
        for k in range(CONV_K):
            gk = gco if k == CONV_K - 1 else gco * marks[:, k : k + 1]
            wide_o[k : k + 1, tile(j)] = jnp.sum(gk * ext[LEAD + k : LEAD + k + rows, :], axis=0, keepdims=True)
            acc[LEAD + k : LEAD + k + rows, :] += gk * cw[k : k + 1, tile(j)]
        wide_o[4:5, tile(j)] = jnp.sum(gco, axis=0, keepdims=True)
        gp_o[:, tile(j)] = acc[...].astype(BF16)

    wide_o[6:8, :] = jnp.zeros((2, CONV_CH), F32)
    for j in range(PAIRS):
        part, at = parted(j, (left, right))
        out = part[:, at]
        s = sigmoid(out)
        x = out * s
        dtp = spread(dtv, j)
        flow = spread(outflow, j)
        xd = x * dtp
        gxs = dot(b, gb16[:, tile(j)]) * flow
        xe[:, tile(j)] = (xd * flow).astype(BF16)
        gxd = (gxdt if j < PAIRS // 2 else gxdt2)[:, at] + gxs
        gv = gv + head_sums(xd * gxs, j)
        gd = gd + head_sums(x * gxd, j)
        conv_back(j, dtp * gxd + spread(hp[2:3, :], j) * (gy if j < PAIRS // 2 else gy2)[:, at].astype(F32), s, out)
    gb = gbi[...] + gbi2[...] + dot_t(xe[...], gb16[...])
    for j, grad in ((PAIRS, gb), (PAIRS + 1, gci[...] + gci2[...])):
        out = bc[:, tile(j - PAIRS)]
        conv_back(j, grad, sigmoid(out), out)
    keep = jnp.exp(last) * marks[rows - 1 : rows, 3:4]
    edge = jnp.sum(gv, axis=0, keepdims=True) + kg[0:1, :] * keep
    place = lax.broadcasted_iota(jnp.int32, (rows, LANES), 0)
    gl = gli[...] + gli2[...] - gv + jnp.where(place == rows - 1, edge, 0.0)
    ga = dot(triangle(rows, False).astype(F32), gl, EXACT)
    rate = hp[1:2, :]
    raw = pc[HALO:, CONV_CH:WIDE].astype(F32) + hp[0:1, :]
    graw = jnp.where(lanes_of(rows) < HEADS, (ga * rate + gd) * sigmoid(raw), 0.0)
    gp_o[0:HALO, CONV_CH:WIDE] = jnp.zeros((HALO, LANES), BF16)
    gp_o[HALO:, CONV_CH:WIDE] = graw.astype(BF16)
    wide_o[5:6, 0:INNER] = gate[0:1, :]
    place = lanes_of(1)
    heads = jnp.where(place < HEADS, jnp.sum(graw, axis=0, keepdims=True), 0.0)
    for k, row in enumerate((rate * jnp.sum(ga * dtv, axis=0, keepdims=True), skip[0:1, :])):
        heads = heads + jnp.where(place // HEADS == k + 1, pltpu.roll(row, HEADS * (k + 1), 1), 0.0)
    wide_o[5:6, INNER : INNER + LANES] = heads
    wide_o[5:6, INNER + LANES :] = jnp.zeros((1, CONV_CH - INNER - LANES), F32)


def row_of(values, rows=8):
    pad = [(0, rows - values.shape[0]), (0, max(0, LANES - values.shape[1]))]
    return jnp.pad(values.astype(F32), pad)


def per_device(
    hidden, segment_ids, in_weight, out_weight, conv_weight, conv_bias, norm_gain, gate_gain,
    dt_bias, a_log, skip_param, cotangent,
):
    layers_n, in_rows = in_weight.shape[:2]
    out_rows = out_weight.shape[1]
    rows, width = hidden.shape
    count = lax.axis_size("seq")
    me = lax.axis_index("seq")
    me_ref = me.reshape(1).astype(jnp.int32)
    conv_n = conv_bias.shape[1]
    half = INNER // 2
    plane_n = axes_of(count)["z"][1]

    small = jnp.concatenate(
        [conv_weight.reshape(-1), conv_bias.reshape(-1), norm_gain.reshape(-1), gate_gain.reshape(-1)]
    )
    length = small.shape[0]
    small_rows = -(-length // (16 * LANES)) * 16
    small = jnp.pad(small, (0, small_rows * LANES - length)).reshape(small_rows, LANES)
    in_weight_side = jnp.pad(in_weight[0, :, INNER:], ((0, 0), (0, WIDE - SIDE)))
    halo = shifted(hidden[rows - HALO :], 1)
    seg_halo = shifted(segment_ids[rows - HALO :] + 1, 1) - 1
    packs = []
    for layer in range(layers_n):
        parts = [in_weight[layer, :, :half], in_weight[layer, :, half:INNER], out_weight[layer]]
        if layer + 1 < layers_n:
            later = in_weight[layer + 1, :, INNER:]
            parts += [later[:, :half], later[:, half : 2 * half]]
            parts.append(jnp.pad(later[:, 2 * half :], ((0, 0), (0, 3 * half - SIDE))))
        packs.append((jnp.concatenate(parts, axis=0), np.cumsum([0] + [p.shape[0] for p in parts]).tolist()))
    first = Gather(in_weight_side)
    smalls = gather_small(small)
    started = first.line(tuple(pack for pack, _ in packs))
    gathered = [lax.all_gather(after(pack, started), "seq") for pack, _ in packs]
    first.plane()

    seg_pad = jnp.concatenate([seg_halo[LEAD:], segment_ids])
    before = seg_pad[CONV_K - 2]
    columns = [seg_pad[k : k + rows] == segment_ids for k in range(CONV_K - 1)]
    columns += [segment_ids == before, segment_ids == segment_ids[-1], segment_ids]
    marks = jnp.pad(jnp.stack([col.astype(F32) for col in columns], axis=1), ((0, 0), (0, LANES - 6)))
    seg_row = jnp.broadcast_to(segment_ids.astype(F32)[None, :], (8, rows))

    relative, planes = relative_places(count), plane_first(count)
    order = column_order(relative, me, in_rows)
    plane_order = column_order(planes, 0, in_rows)

    place = (jnp.arange(count)[:, None] == (jnp.arange(count) ^ me)[None, :]).astype(BF16)
    smalls = dot(place, smalls.reshape(count, small_rows * LANES))
    sizes = [layers_n * CONV_K * conv_n, layers_n * conv_n, layers_n * in_rows, layers_n * out_rows]
    cuts = np.cumsum([0] + sizes)
    taps, biases, gains, gate_gains = (smalls[:, cuts[i] : cuts[i + 1]] for i in range(4))
    taps = taps.reshape(count, layers_n, CONV_K, conv_n).transpose(1, 2, 0, 3).reshape(layers_n, CONV_K, CONV_CH)
    biases = biases.reshape(count, layers_n, 1, conv_n).transpose(1, 2, 0, 3).reshape(layers_n, 1, CONV_CH)
    conv_rows = jnp.pad(jnp.concatenate([taps, biases], axis=1), ((0, 0), (0, 3), (0, 0)))
    gains = gains.reshape(count, layers_n, in_rows).transpose(1, 0, 2).reshape(layers_n, 1, width)
    gate_gains = gate_gains.reshape(count, layers_n, out_rows).transpose(1, 0, 2).reshape(layers_n, 1, INNER)
    gains = [jnp.broadcast_to(gains[layer], (8, width)) for layer in range(layers_n)]
    gate_gains = [jnp.broadcast_to(gate_gains[layer], (8, INNER)) for layer in range(layers_n)]
    conv_rows = [conv_rows[layer] for layer in range(layers_n)]
    heads = [
        row_of(jnp.stack([dt_bias[layer], -jnp.exp(a_log[layer]), skip_param[layer]])) for layer in range(layers_n)
    ]

    (left, left2), (right, right2) = first.whole((*conv_rows, *gains, *gate_gains, *heads, marks, seg_row, halo, order))

    scratch_wide = pltpu.VMEM((rows, INNER), BF16)
    scratch_half = pltpu.VMEM((rows, INNER // 2), BF16)
    scratch_cols = pltpu.VMEM((HEADS // 2, rows, LANES), F32)
    scratch_rows = pltpu.VMEM((LANES, rows), F32)

    residual = hidden
    saved, sides = [], ()
    for layer in range(layers_n):
        precise = layer + 1 < layers_n
        gain, gate = gains[layer], gate_gains[layer]
        (normed,) = kernel_call(norm_kernel, [((HALO + rows, width), BF16)], (residual, halo, gain))
        if layer == 0:
            normed_rel = dot(normed, order).astype(BF16)
            lower, upper = normed_rel[:, : width // 2], normed_rel[:, width // 2 :]
            parts = [dot(lower, left) + dot(upper, left2), dot(lower, right) + dot(upper, right2)]
        else:
            normed_rel = dot(normed, plane_order).astype(BF16)
            parts = [dot(normed, part) for part in side_parts[:2]]
            parts.append(dot(normed, side_parts[2][:, : WIDE - 2 * half]))
        pc = jnp.concatenate([part.astype(BF16) for part in parts], axis=1)
        hp = heads[layer]
        conv_l, conv_r, bc, dt, log, own, msg = kernel_call(
            partial(conv_state_kernel, precise=precise),
            [((rows, half), F32)] * 2 + [((rows, 2 * STATE), F32)] + [((rows, LANES), F32)] * 2
            + [state_out(half)] * 2,
            (pc, conv_rows[layer], hp, marks, me_ref),
            scratch=[scratch_wide] * (2 if precise else 1), flops=2 * rows * STATE * INNER * 8,
        )
        yw = [
            kernel_call(
                partial(within_kernel, precise=precise, first=part * PAIRS // 2), [((rows, half), F32)],
                ((conv_l, conv_r)[part], bc, dt, log, hp, marks, seg_row),
                scratch=[scratch_half, scratch_cols, scratch_rows] + [scratch_half] * precise,
                flops=2 * rows * rows * half * 16, deps=(own,),
            )[0]
            for part in range(2)
        ]
        mine, recv = exchange(own, msg, me_ref, False, [(), (yw[0],), (yw[1],), ()])
        aligned = out_rows == HEAD_DIM
        places = relative if layer == 0 else planes
        pack, spans = gathered[layer], packs[layer][1]
        weights = [pack[:, a:b].reshape(-1, width) for a, b in zip(spans, spans[1:])]
        outs = [((rows, INNER), BF16), ((rows, INNER), F32), ((rows, INNER), BF16)] + [((STATE, half), BF16)] * 2
        outs += [((rows, width), F32)] + [((rows, INNER), BF16)] * aligned
        form = partial(post_kernel, places=places, relative=layer == 0)
        args = (normed, residual, *yw, mine, recv, bc, log, marks, gate, me_ref)
        scratch = [pltpu.VMEM((rows, INNER), F32)]
        flops = 2 * rows * width * INNER * 2
        if in_rows % HALO:
            z, y, gnormed, state, state2, after_h, *gn_rel = kernel_call(
                partial(form, spans=(), aligned=aligned), outs, (*weights[:3], *args), scratch=scratch, flops=flops
            )
        else:
            z, y, gnormed, state, state2, after_h, *rest = streamed_call(
                partial(form, spans=spans, aligned=aligned), outs, args, flops=flops, streamed=pack,
                scratch=scratch + [pltpu.VMEM((count, 2 * in_rows, width), BF16)] * 2,
                raw=[((count, b - a, width), BF16) for a, b in zip(spans, spans[1:])],
            )
            gn_rel = rest[:aligned]
            weights = [part.reshape(-1, width) for part in rest[aligned:]]
        weights, side_parts = weights[:3], weights[3:]
        if not aligned:
            gn_rel = [dot(gnormed, column_order(places, me if layer == 0 else 0, out_rows)).astype(BF16)]
        saved.append((residual, normed_rel, pc, conv_l, conv_r, bc, dt, log, hp, z, y, gn_rel[0], state, state2, weights, sides))
        sides = side_parts
        residual = after_h
        if layer + 1 < layers_n:
            halo = shifted(residual[rows - HALO :], 1)

    grad = cotangent
    for layer in range(layers_n - 1, -1, -1):
        h, normed_rel, pc, conv_l, conv_r, bc, dt, log, hp, z, y, gn_rel, state, state2, weights, sides = saved[layer]
        z_low, z_high, out_w = weights
        gain, gate = gains[layer], gate_gains[layer]
        mixed = grad.astype(BF16)
        gy, gy2, gz, gate_grad, skip_grad, own, msg = kernel_call(
            post_back_kernel,
            [((rows, half), BF16)] * 2 + [((rows, INNER), BF16), ((8, INNER), F32), ((8, LANES), F32)]
            + [state_out(half), state_out(half, BF16)],
            (dot_t(mixed, out_w), y, z, gate, conv_l, conv_r, bc, log, marks, me_ref),
            scratch=[scratch_wide], flops=2 * rows * STATE * INNER * 8,
        )
        halves_back = [
            kernel_call(
                partial(within_back_kernel, first=part * PAIRS // 2),
                [((rows, half), F32), ((rows, LANES), F32), ((rows, LANES), F32), ((rows, LANES), F32)],
                ((conv_l, conv_r)[part], bc, dt, log, (gy, gy2)[part], (state, state2)[part], marks, seg_row),
                scratch=[
                    scratch_half, scratch_half, scratch_cols, scratch_rows,
                    pltpu.VMEM((rows, rows), F32), scratch_rows, pltpu.VMEM((rows, LANES), F32),
                ],
                flops=2 * rows * rows * half * 32,
            )
            for part in range(2)
        ]
        terms = grads_call(gn_rel, normed_rel, mixed, gz, count, 1 if layer else 2)
        deps = [(), (terms[0],), (halves_back[0][0],), (halves_back[1][0],)]
        late = ()
        if layer:
            planes_sum = scatter_planes(terms[0].reshape(-1, width))
        else:
            pack_share = Shares(*(term.reshape(-1, width) for term in terms))
            late = tuple(far(piece) for piece in pack_share.step())
        if layer + 1 < layers_n:
            deps[3] += (far(above[0]),)
        mine, recv = exchange(own, msg, me_ref, True, deps)

        (gx, *sums), (gx2, *sums2) = halves_back
        gp, wide = kernel_call(
            mixer_back_kernel,
            [((HALO + rows, WIDE), BF16), ((8, CONV_CH), F32)],
            (
                gx2, gy2, conv_r, pc, conv_rows[layer], gx, *sums, *sums2, mine, recv, gy, conv_l, bc, dt, log,
                state, state2, hp, marks, gate_grad, skip_grad, me_ref,
            ),
            scratch=[pltpu.VMEM((STATE, INNER), BF16), scratch_wide, pltpu.VMEM((HALO + rows, LANES), F32)],
            flops=2 * rows * STATE * INNER * 24, deps=late,
        )
        if layer + 1 < layers_n:
            above = (above[0], after(above[1], gp))
        spilled = shifted(gp[:HALO], -1)
        if layer:
            above = (planes_sum, scatter_planes(turned_dot(normed_rel, gp)))
        else:
            side_share = share_terms(normed_rel, gp)
            both = (side_share.terms[0], side_share.send, far(pack_share.terms[1]))
        gp_own, gz = kernel_call(
            own_rows_kernel, [((rows, WIDE), BF16), ((rows, INNER), BF16)], (gp, spilled, gz),
            deps=() if layer else both,
        )
        gn_z = dot_t(gz[:, :half], z_low) + dot_t(gz[:, half:], z_high)
        if layer:
            gn = gn_z
            for k, part in enumerate(sides):
                piece = gp_own[:, k * half : min((k + 1) * half, WIDE)]
                gn = gn + dot_t(piece, part[:, : piece.shape[1]])
        else:
            gp_left, gp_right = gp_own[:, :CUT], gp_own[:, CUT:]
            gn_side = jnp.concatenate(
                [dot_t(gp_left, left) + dot_t(gp_right, right), dot_t(gp_left, left2) + dot_t(gp_right, right2)],
                axis=1,
            )
            gn_high, gn_low = halves(gn_side)
            gn = gn_z + dot_t(gn_high, order) + dot_t(gn_low, order)
        grad, small_grads = kernel_call(
            norm_back_kernel, [((rows, width), F32), ((8 * (layers_n - layer), CONV_CH), F32)],
            (gn, h, grad, gain, wide) + ((small_grads,) if layer + 1 < layers_n else ()),
            deps=() if layer else (far(pack_share.terms[2]),),
        )
    (sums,) = kernel_call(round_kernel, [(small_grads.shape, BF16)], (small_grads,))
    sums = sum_rounds(sums, count // 2, plane_n)
    pieces = pack_share.step((sums,))
    side_share.step(behind=pieces[0])
    side_share.step()
    passed = (*pack_share.terms[1:], side_share.terms[1])
    sums = sum_rounds(sums, plane_n // 2, 1, tuple(far(part) for part in passed))
    terms, split = [*pack_share.terms, *side_share.terms], [(len(pack_share.terms), len(side_share.terms))]
    for part in above:
        terms.append(scatter_lines(part))
    split += [(1, 1)] * (layers_n - 1)
    in_grads, out_grads = kernel_call(
        partial(shares_kernel, split=split),
        [((layers_n, in_rows, INNER + SIDE), F32), ((layers_n, out_rows, width), F32)], terms, deps=(sums,),
    )
    sums = sums.reshape(layers_n, 8, CONV_CH)

    def share(values):
        span = values.shape[-1] // count
        return lax.dynamic_slice_in_dim(values, me * span, span, values.ndim - 1)

    heads = sums[:, 5, INNER : INNER + 3 * HEADS]
    return (
        residual, grad, in_grads, out_grads,
        share(sums[:, :CONV_K]), share(sums[:, CONV_K]), share(sums[:, 6, :width]), share(sums[:, 5, :INNER]),
        heads[:, :HEADS], heads[:, HEADS : 2 * HEADS], heads[:, 2 * HEADS :],
    )


def solution(mesh):
    return jax.shard_map(
        per_device,
        mesh=mesh,
        in_specs=(
            P("seq", None), P("seq"), P(None, "seq", None), P(None, "seq", None), P(None, None, "seq"),
            P(None, "seq"), P(None, "seq"), P(None, "seq"), P(), P(), P(), P("seq", None),
        ),
        out_specs=(
            P("seq", None), P("seq", None), P(None, "seq", None), P(None, "seq", None), P(None, None, "seq"),
            P(None, "seq"), P(None, "seq"), P(None, "seq"), P(), P(), P(),
        ),
        check_vma=False,
    )
```

```python
from functools import partial

import jax
import jax.numpy as jnp
import numpy as np
from jax import lax
from jax.experimental import pallas as pl
from jax.experimental.pallas import tpu as pltpu
from jax.sharding import PartitionSpec as P

HEADS = 32
HEAD_DIM = 64
STATE = 128
CONV_K = 4
INNER = 2048
CONV_CH = 2304
SIDE = CONV_CH + HEADS
WIDE = 2432
CUT = 1280
LANES = 128
PAIRS = HEADS // 2
HALO = 16
LEAD = HALO - (CONV_K - 1)
FAR = -1e30

EPS = 1e-05
F32 = jnp.float32
BF16 = jnp.bfloat16
EXACT = lax.Precision.HIGHEST
MB = 1024 * 1024
CAP = 16 * MB


def axes_of(count):
    side = 4 if count >= 128 else 2
    plane = 2 * side * side
    return {"c": (2, 1), "x": (side, 2), "y": (side, 2 * side), "z": (count // plane, plane)}


def swap(value, flip):
    count = lax.axis_size("seq")
    return lax.ppermute(value, "seq", [(i, i ^ flip) for i in range(count)])


def shifted(shard, by):
    count = lax.axis_size("seq")
    return lax.ppermute(shard, "seq", [(i, i + by) for i in range(count) if 0 <= i + by < count])


def relative_places(count):
    axes = axes_of(count)
    places = np.zeros((1,), np.int32)
    for name in ("c", "y", "x", "z"):
        size, shift = axes[name]
        places = (places[:, None] + np.arange(size, dtype=np.int32)[None, :] * shift).reshape(-1)
    return places


def column_order(places, me, block):
    count = len(places)
    places = jnp.asarray(np.repeat(places, block))
    inner = jnp.asarray(np.tile(np.arange(block, dtype=np.int32), count))
    source = (places ^ me) * block + inner
    return (jnp.arange(count * block)[:, None] == source[None, :]).astype(BF16)


class Gather:

    def __init__(self, shard):
        self.axes = axes_of(lax.axis_size("seq"))
        self.rows = shard.shape[0]
        self.kind = shard.dtype
        self.shard, self.sent = shard, self.send(shard, "z")

    def send(self, value, name):
        size, shift = self.axes[name]
        return [swap(value, d * shift) for d in range(1, size)]

    def outs(self, *lead):
        return [((*lead, self.rows, CUT), self.kind), ((*lead, self.rows, WIDE - CUT), self.kind)]

    def line(self, deps=()):
        everything = slice(None)
        cuts = ((everything, slice(0, CUT)), (everything, slice(CUT, WIDE)))
        pieces = [
            (value, side, cuts[side], d) for side in range(2) for d, value in enumerate([self.shard, *self.sent])
        ]
        self.left, self.right = copies_call(pieces, self.outs(self.axes["z"][0]), deps)
        self.sent = self.send(self.left, "x"), self.send(self.right, "y")
        return self.left

    def plane(self, deps=()):
        sides = ((self.left, *self.sent[0]), (self.right, *self.sent[1]))
        pieces = [(value, side, None, d) for side in range(2) for d, value in enumerate(sides[side])]
        line, across, up = (self.axes[name][0] for name in ("z", "x", "y"))
        outs = [self.outs(across, line)[0], self.outs(up, line)[1]]
        self.left, self.right = copies_call(pieces, outs, deps)
        self.sent = self.send(self.left, "y"), self.send(self.right, "x")
        return self.left

    def whole(self, deps=()):
        line, across, up = (self.axes[name][0] for name in ("z", "x", "y"))
        pieces = [(value, 0, None, d) for d, value in enumerate([self.left, *self.sent[0]])]
        pieces += [
            (value, 1, i, (i, d)) for d, value in enumerate([self.right, *self.sent[1]]) for i in range(up)
        ]
        left, right = copies_call(pieces, self.outs(up, across, line), deps)
        left, right = left.reshape(-1, left.shape[-1]), right.reshape(-1, right.shape[-1])
        return (left, swap(left, 1)), (right, swap(right, 1))


class Shares:

    def __init__(self, keep, send):
        line, plane = axes_of(lax.axis_size("seq"))["z"]
        self.groups = [(plane // 2, 2), (line, plane)]
        shape = (plane // 2, line, keep.shape[0] // (plane // 2 * line), keep.shape[1])
        self.send = send
        self.terms = [keep.reshape(shape), swap(send.reshape(shape), 1)]

    def step(self, deps=(), behind=None):
        size, shift = self.groups.pop(0)
        if deps:
            pieces = list(
                kernel_call(pieces_kernel, [(self.terms[0].shape[1:], BF16)] * size, self.terms, deps=deps)
            )
        else:
            none = 0.0
            if behind is not None:
                none = jnp.minimum(jnp.abs(behind[(0,) * behind.ndim].astype(F32)), 0.0)
            pieces = []
            for d in range(size):
                picked = [t[d].astype(F32) for t in self.terms]
                pieces.append((sum(picked[1:], picked[0]) + none).astype(BF16))
        self.terms = [pieces[0]] + [swap(pieces[d], d * shift) for d in range(1, size)]
        return pieces


def pieces_kernel(*refs):
    size = refs[0].shape[0]
    terms, outs = refs[:-size], refs[-size:]
    for d, out in enumerate(outs):
        total = terms[0][d].astype(F32)
        for term in terms[1:]:
            total = total + term[d].astype(F32)
        out[...] = total.astype(BF16)


def turned_dot(left, right):
    return lax.dot_general(left, right, (((0,), (0,)), ((), ())), preferred_element_type=F32).astype(BF16)


def share_terms(left, right):
    half = left.shape[1] // 2
    return Shares(turned_dot(left[:, :half], right), turned_dot(left[:, half:], right))


def plane_first(count):
    plane = axes_of(count)["z"][1]
    return np.arange(count).reshape(-1, plane).T.reshape(-1)


def scatter_planes(grad):
    count = lax.axis_size("seq")
    plane = axes_of(count)["z"][1]
    groups = np.arange(count).reshape(-1, plane).tolist()
    return lax.psum_scatter(grad, "seq", scatter_dimension=0, tiled=True, axis_index_groups=groups)


def scatter_lines(grad):
    count = lax.axis_size("seq")
    plane = axes_of(count)["z"][1]
    groups = np.arange(count).reshape(-1, plane).T.tolist()
    return lax.psum_scatter(grad, "seq", scatter_dimension=0, tiled=True, axis_index_groups=groups)


def round_kernel(value, out):
    out[...] = value[...].astype(BF16)


def add_kernel(left, right, *outs):
    total = left[...].astype(F32) + right[...].astype(F32)
    for out in outs:
        out[...] = total.astype(out.dtype)


def sum_rounds(value, first, last, deps=()):
    flip = first
    while flip >= last:
        kind = BF16 if flip > 1 else F32
        late, deps = (deps[0], deps[1:]) if deps else ((), ())
        (value,) = kernel_call(add_kernel, [(value.shape, kind)], (value, swap(value, flip)), deps=late)
        flip //= 2
    return value


def gather_small(value, deps):
    flip, rows = 1, value.shape[0]
    while flip < lax.axis_size("seq"):
        late, deps = deps[0], deps[1:] or deps
        first, second = slice(0, flip * rows), slice(flip * rows, 2 * flip * rows)
        pieces = [(value, 0, None, first), (swap(value, flip), 0, None, second)]
        (value,) = copies_call(pieces, [((2 * flip * rows, LANES), value.dtype)], late)
        flip *= 2
    return value


def held_bytes(shape, kind):
    *lead, rows, lanes = (1, *shape) if len(shape) < 2 else shape
    rows, lanes = -(-rows // 16) * 16, -(-lanes // LANES) * LANES
    return int(np.prod(lead, dtype=np.int64)) * rows * lanes * jnp.dtype(kind).itemsize


def room_for(arrays, scratch):
    total = sum(held_bytes(*a) for a in arrays) + sum(held_bytes(r.shape, r.dtype) for r in scratch)
    return total + total // 8 + 3 * MB


def far(array):
    return pltpu.with_memory_space_constraint(array, pltpu.HBM)


def kernel_call(body, outs, args, scratch=(), flops=0, deps=()):
    places = [pltpu.SMEM if a.dtype == jnp.int32 else pltpu.VMEM for a in args] + [pl.ANY] * len(deps)
    known = len(args)

    def run(*refs):
        body(*refs[:known], *refs[known + len(deps) :])

    size = sum(int(np.prod(a.shape)) * a.dtype.itemsize for a in args) + sum(
        int(np.prod(o[0])) * jnp.dtype(o[1]).itemsize for o in outs
    )
    return pl.pallas_call(
        run,
        out_shape=tuple(jax.ShapeDtypeStruct(*o) for o in outs),
        in_specs=[pl.BlockSpec(memory_space=p) for p in places],
        out_specs=tuple(pl.BlockSpec(memory_space=pltpu.VMEM) for _ in outs),
        scratch_shapes=list(scratch),
        compiler_params=pltpu.CompilerParams(vmem_limit_bytes=min(CAP, room_for([(a.shape, a.dtype) for a in args] + list(outs), scratch))
        ),
        cost_estimate=pl.CostEstimate(flops=flops, bytes_accessed=size, transcendentals=0),
    )(*args, *deps)


def streamed_call(body, outs, args, scratch=(), flops=0, streamed=None, raw=()):
    places = [pltpu.SMEM if a.dtype == jnp.int32 else pltpu.VMEM for a in args]
    size = sum(int(np.prod(a.shape)) * a.dtype.itemsize for a in (*args, streamed)) + sum(
        int(np.prod(o[0])) * jnp.dtype(o[1]).itemsize for o in (*outs, *raw)
    )
    return pl.pallas_call(
        body,
        out_shape=tuple(jax.ShapeDtypeStruct(*o) for o in (*outs, *raw)),
        in_specs=[pl.BlockSpec(memory_space=p) for p in (pltpu.HBM, *places)],
        out_specs=tuple(pl.BlockSpec(memory_space=p) for p in [pltpu.VMEM] * len(outs) + [pltpu.HBM] * len(raw)),
        scratch_shapes=[*scratch, pltpu.SemaphoreType.DMA((3 * len(raw),))],
        compiler_params=pltpu.CompilerParams(vmem_limit_bytes=room_for([], scratch) + 8 * MB),
        cost_estimate=pl.CostEstimate(flops=flops, bytes_accessed=size, transcendentals=0),
    )(streamed, *args)


def copies_call(pieces, outs, deps=()):
    arrays = [p[0] for p in pieces]
    known, written = len(arrays), len(outs)

    def run(*refs):
        refs = refs[:known] + refs[known + len(deps) :]
        results, held, (sems, out_sems) = refs[known : known + written], refs[known + written : -2], refs[-2:]
        copies = []
        for k, (_, out, source, target) in enumerate(pieces):
            src = refs[k] if source is None else refs[k].at[source]
            copies.append(pltpu.make_async_copy(src, held[out].at[target], sems.at[k]))
            copies[-1].start()
        for copy in copies:
            copy.wait()
        copies = []
        for k in range(written):
            copies.append(pltpu.make_async_copy(held[k], results[k], out_sems.at[k]))
            copies[-1].start()
        for copy in copies:
            copy.wait()

    size = sum(2 * int(np.prod(o[0])) * jnp.dtype(o[1]).itemsize for o in outs)
    return pl.pallas_call(
        run,
        out_shape=tuple(jax.ShapeDtypeStruct(*o) for o in outs),
        in_specs=[pl.BlockSpec(memory_space=pltpu.HBM)] * known + [pl.BlockSpec(memory_space=pl.ANY)] * len(deps),
        out_specs=tuple(pl.BlockSpec(memory_space=pltpu.HBM) for _ in outs),
        scratch_shapes=[pltpu.VMEM(*o) for o in outs]
        + [pltpu.SemaphoreType.DMA((known,)), pltpu.SemaphoreType.DMA((written,))],
        compiler_params=pltpu.CompilerParams(vmem_limit_bytes=room_for(outs, ())),
        cost_estimate=pl.CostEstimate(flops=0, bytes_accessed=size, transcendentals=0),
    )(*arrays, *deps)


def copy_kernel(value, out):
    out[...] = value[...]


def after(value, *deps):
    return kernel_call(copy_kernel, [(value.shape, value.dtype)], (value,), deps=deps)[0]


def dot(left, right, precision=None):
    return jnp.dot(left, right, precision=precision, preferred_element_type=F32)


def dot_t(left, right):
    return lax.dot_general(left, right, (((1,), (1,)), ((), ())), preferred_element_type=F32)


def halves(value):
    high = value.astype(BF16)
    return high, (value - high.astype(F32)).astype(BF16)


def fine(form, left, right):
    (lh, ll), (rh, rl) = halves(left), halves(right)
    return form(lh, rh) + (form(ll, rh) + form(lh, rl))


def lanes_of(rows):
    return lax.broadcasted_iota(jnp.int32, (rows, LANES), 1)


def spread(values, pair):
    low = lanes_of(values.shape[0]) < HEAD_DIM
    return jnp.where(low, values[:, 2 * pair : 2 * pair + 1], values[:, 2 * pair + 1 : 2 * pair + 2])


def spread_row(row):
    return jnp.concatenate([spread(row, pair) for pair in range(PAIRS)], axis=1)


def head_sums(product, pair):
    rows = lax.broadcasted_iota(jnp.int32, (LANES, LANES), 0)
    cols = lax.broadcasted_iota(jnp.int32, (LANES, LANES), 1)
    pick = (cols == 2 * pair + (rows >= HEAD_DIM).astype(jnp.int32)).astype(BF16)
    high = product.astype(BF16)
    low = (product - high.astype(F32)).astype(BF16)
    return dot(high, pick) + dot(low, pick)


def sigmoid(v):
    return 1.0 / (1.0 + jnp.exp(-v))


def silu(v):
    return v * sigmoid(v)


def parted(j, parts):
    half = PAIRS // 2
    return parts[j // half], tile(j % half)


def tile(pair):
    return slice(pair * LANES, (pair + 1) * LANES)


def pack_row(row):
    first = row.astype(BF16).astype(F32)
    second = (row - first).astype(BF16).astype(F32)
    third = row - first - second
    place = lax.broadcasted_iota(jnp.int32, (16, row.shape[1]), 0)
    packed = jnp.where(place == 0, first, jnp.where(place == 1, second, third))
    return jnp.where(place < 3, packed, 0.0).astype(BF16)


def unpack_row(rows):
    return jnp.sum(rows.astype(F32), axis=0, keepdims=True)


def emit_msg(total, keep, msg_o):
    msg_o[0:STATE, :] = total.astype(msg_o.dtype)
    if msg_o.dtype == F32:
        msg_o[STATE:, :] = jnp.broadcast_to(keep, (msg_o.shape[0] - STATE, keep.shape[1]))
    else:
        msg_o[STATE:, :] = pack_row(keep)


def read_msg(recv):
    if recv.dtype == F32:
        return recv[0:STATE, :], recv[STATE : STATE + 1, :]
    return recv[0:STATE, :].astype(F32), unpack_row(recv[STATE:, :])


def emit_halves(total, keep, upper, own_o, msg_o):
    half = total.shape[1] // 2
    low, high = total[:, :half], total[:, half:]
    klow, khigh = keep[:, :half], keep[:, half:]
    emit_msg(jnp.where(upper, high, low), jnp.where(upper, khigh, klow), own_o)
    emit_msg(jnp.where(upper, low, high), jnp.where(upper, klow, khigh), msg_o)


def bit_of(me, flip):
    return (me[0] & flip) != 0


def state_out(width, kind=F32):
    return ((STATE + (8 if kind == F32 else 16), width), kind)


def in_order(relative, place, back):
    size = len(relative)
    ordered = []
    for step in range(size):
        member = size - 1 - step if back else step
        value = relative[0]
        for d in range(1, size):
            value = jnp.where(jnp.bitwise_xor(place, member) == d, relative[d], value)
        ordered.append(value)
    return ordered


def place_of(me, shift, size):
    return jnp.bitwise_and(lax.shift_right_logical(me[0], shift.bit_length() - 1), size - 1)


def pair_kernel(own, recv, me, first_o, mine_o, m1, m2, m3, joined, *, back):
    other, kother = read_msg(recv)
    mine, kmine = read_msg(own)
    first = jnp.logical_xor(bit_of(me, 1), not back)
    t_first, k_first = jnp.where(first, mine, other), jnp.where(first, kmine, kother)
    t_second, k_second = jnp.where(first, other, mine), jnp.where(first, kother, kmine)
    emit_msg(t_first, k_first, first_o)
    emit_msg(k_second * t_first + t_second, k_first * k_second, joined)
    place = place_of(me, 2, 4)
    width = mine_o.shape[1]
    for d, out in enumerate((mine_o, m1, m2, m3)):
        at = pl.ds(pl.multiple_of(jnp.bitwise_xor(place, d) * width, LANES), width)
        emit_msg(joined[0:STATE, at], joined[STATE : STATE + 1, at], out)


def scan_group(own, recvs, place, back):
    read = [read_msg(r) for r in (own, *recvs)]
    totals = in_order([r[0] for r in read], place, back)
    keeps = in_order([r[1] for r in read], place, back)
    prefixes, value, decay = [], jnp.zeros_like(totals[0]), jnp.ones_like(keeps[0])
    for t, k in zip(totals, keeps):
        prefixes.append((value, decay))
        value, decay = k * value + t, decay * k
    return prefixes, value, decay


def own_prefix(prefixes, place, back):
    size = len(prefixes)
    value, decay = prefixes[0]
    for step in range(1, size):
        mine = place == (size - 1 - step if back else step)
        value = jnp.where(mine, prefixes[step][0], value)
        decay = jnp.where(mine, prefixes[step][1], decay)
    return value, decay


def plane_kernel(mine, r1, r2, r3, me, pre_o, *outs, back):
    prefixes, value, decay = scan_group(mine, (r1, r2, r3), place_of(me, 2, 4), back)
    for step, (prefix, kprefix) in enumerate(prefixes):
        emit_msg(prefix, kprefix, pre_o.at[3 - step if back else step])
    for out in outs:
        emit_msg(value, decay, out)


def line_kernel(own, *refs, size, shift, back, carried, final):
    recvs, refs = refs[: size - 1], refs[size - 1 :]
    if carried:
        state, *refs = refs
    if final:
        pre, *refs = refs
    me, *outs = refs
    place = place_of(me, shift, size)
    prefixes, value, decay = scan_group(own, recvs, place, back)
    into, kinto = own_prefix(prefixes, place, back)
    if carried:
        before, kbefore = read_msg(state)
        into, kinto = kbefore * into + before, kbefore * kinto
    if not final:
        emit_msg(into, kinto, outs[0])
        for out in outs[1:]:
            emit_msg(value, decay, out)
        return
    plane = place_of(me, 2, 4)
    for d, out in enumerate(outs):
        prefix, kprefix = read_msg(pre.at[jnp.bitwise_xor(plane, d)])
        out[...] = (kprefix * into + prefix).astype(out.dtype)


def down_kernel(mine, r1, r2, r3, first, me, mine_o, msg_o, whole, *, back):
    place = place_of(me, 2, 4)
    width = mine.shape[1]
    for d, ref in enumerate((mine, r1, r2, r3)):
        at = pl.ds(pl.multiple_of(jnp.bitwise_xor(place, d) * width, LANES), width)
        whole[:, at] = ref[...].astype(F32)
    into = whole[...]
    t_first, k_first = read_msg(first)
    beyond = k_first * into + t_first
    second = jnp.logical_xor(bit_of(me, 1), back)
    mine_o[...] = jnp.where(second, beyond, into)
    msg_o[...] = jnp.where(second, into, beyond).astype(msg_o.dtype)


def join_halves(mine, recv, upper):
    theirs = recv[...].astype(F32)
    own = mine[...]
    return jnp.where(upper, theirs, own), jnp.where(upper, own, theirs)


def exchange(own, msg, me, back, deps=((), (), (), ())):
    count = lax.axis_size("seq")
    kind = msg.dtype
    width = INNER // 2
    quarter = width // 4
    part, message = state_out(quarter), state_out(quarter, kind)
    both = [message] if kind == F32 else [part, message]
    recv = swap(msg, 1)
    first, mine, *msgs = kernel_call(
        partial(pair_kernel, back=back), [state_out(width), part] + [message] * 3,
        (own, recv, me), deps=deps[0], scratch=[pltpu.VMEM(*state_out(width))],
    )
    recvs = [swap(m, 2 * (d + 1)) for d, m in enumerate(msgs)]
    pre, *totals = kernel_call(
        partial(plane_kernel, back=back), [((4, *part[0]), F32)] + both,
        (mine, *recvs, me), deps=deps[1],
    )
    carried = ()
    shift = 8
    while True:
        size = min(4, count // shift)
        recvs = [swap(totals[-1], shift * d) for d in range(1, size)]
        final = shift * size == count
        form = partial(line_kernel, size=size, shift=shift, back=back, carried=bool(carried), final=final)
        shift *= size
        if final:
            break
        state, *totals = kernel_call(form, [part] + both, (totals[0], *recvs, *carried, me))
        carried = (state,)
    mine, *msgs = kernel_call(
        form, [((STATE, quarter), F32)] + [((STATE, quarter), kind)] * 3,
        (totals[0], *recvs, *carried, pre, me), deps=deps[2],
    )
    recvs = [swap(m, 2 * (d + 1)) for d, m in enumerate(msgs)]
    mine, msg = kernel_call(
        partial(down_kernel, back=back), [((STATE, width), F32), ((STATE, width), kind)],
        (mine, *recvs, first, me), deps=deps[3], scratch=[pltpu.VMEM((STATE, width), F32)],
    )
    return mine, swap(msg, 1)


def norm_kernel(h, halo, gain, out):
    for ref, at in ((halo, slice(0, HALO)), (h, slice(HALO, HALO + h.shape[0]))):
        v = ref[...].astype(F32)
        inv = lax.rsqrt(jnp.mean(v * v, axis=-1, keepdims=True) + EPS)
        out[at, :] = (v * inv * gain[0:1, :]).astype(BF16)


def norm_back_kernel(gn, h, g, gain, wide, *refs):
    *others, out, wide_o = refs
    v = h[...].astype(F32)
    grad = gn[...]
    inv = lax.rsqrt(jnp.mean(v * v, axis=-1, keepdims=True) + EPS)
    n = v * inv
    q = grad * gain[0:1, :]
    out[...] = g[...] + inv * (q - n * jnp.mean(q * n, axis=-1, keepdims=True))
    wide_o[0:8, :] = wide[...]
    wide_o[6:7, 0 : v.shape[1]] = jnp.sum(grad * n, axis=0, keepdims=True)
    for other in others:
        wide_o[8:, :] = other[...]


def grads_kernel(gn, normed, mixed, gz, *outs, steps):
    half = INNER // 2
    several, rows = outs[0].shape[0], outs[0].shape[1] // 4
    for k, out in enumerate(outs):

        @pl.when(pl.program_id(0) // steps == k)
        def _(out=out):
            turned = lax.dot_general(gn[...], mixed[...], (((0,), (0,)), ((), ())), preferred_element_type=F32)
            out[:, 2 * rows :, :] = turned.astype(BF16).reshape(several, 2 * rows, half)
            narrow = normed[HALO:, :]
            for q in range(2):
                part = gz[:, q * half : (q + 1) * half]
                turned = lax.dot_general(narrow, part, (((0,), (0,)), ((), ())), preferred_element_type=F32)
                out[:, q * rows : (q + 1) * rows, :] = turned.astype(BF16).reshape(several, rows, half)


def grads_call(gn, normed, mixed, gz, count, parts):
    rows, half = mixed.shape
    wide = 2 * LANES
    several = wide * count // INNER
    steps = count // several // parts
    shape = (several, 4 * half // count, half)

    def share(k):
        return pl.BlockSpec(shape, lambda i: (jnp.clip(i - k * steps, 0, steps - 1), 0, 0))

    return pl.pallas_call(
        partial(grads_kernel, steps=steps),
        grid=(parts * steps,),
        out_shape=[jax.ShapeDtypeStruct((count // parts, *shape[1:]), BF16)] * parts,
        in_specs=[
            pl.BlockSpec((rows, wide), lambda i: (0, i)), pl.BlockSpec((HALO + rows, wide // 2), lambda i: (0, i)),
            pl.BlockSpec(mixed.shape, lambda i: (0, 0)), pl.BlockSpec(gz.shape, lambda i: (0, 0)),
        ],
        out_specs=[share(k) for k in range(parts)],
        compiler_params=pltpu.CompilerParams(vmem_limit_bytes=14 * MB),
        cost_estimate=pl.CostEstimate(flops=8 * rows * half * half, bytes_accessed=10 * MB, transcendentals=0),
    )(gn, normed, mixed, gz)


def own_rows_kernel(gp, spilled, gz, out, gz_o):
    gz_o[...] = gz[...]
    end = out.shape[0] - HALO
    out[0:end, :] = gp[HALO : HALO + end, :]
    out[end:, :] = (gp[HALO + end :, :].astype(F32) + spilled[...].astype(F32)).astype(BF16)


def shares_kernel(*refs, split):
    terms, (in_o, out_o) = refs[:-2], refs[-2:]
    layers_n, rows = in_o.shape[:2]
    half = INNER // 2
    at = 0
    for layer in range(layers_n):
        sums = []
        for size in split[layer]:
            total = terms[at][...].astype(F32)
            for term in terms[at + 1 : at + size]:
                total = total + term[...].astype(F32)
            sums.append(total)
            at += size
        pack, side = sums
        in_o[layer, :, 0:half] = pack[0:rows]
        in_o[layer, :, half:INNER] = pack[rows : 2 * rows]
        in_o[layer, :, INNER:] = side[:, :SIDE]
        out_o[layer] = pack[2 * rows :]


def triangle(rows, lower):
    r = lax.broadcasted_iota(jnp.int32, (rows, rows), 0)
    c = lax.broadcasted_iota(jnp.int32, (rows, rows), 1)
    return r >= c if lower else r <= c


def conv_state_kernel(pc, cw, hp, mk, me, left_o, right_o, bc_o, dt_o, log_o, own_o, msg_o, xw, *low, precise):
    rows = mk.shape[0]
    marks = mk[...]
    raw = pc[HALO:, CONV_CH:WIDE].astype(F32) + hp[0:1, :]
    soft = jnp.maximum(raw, 0.0) + jnp.log1p(jnp.exp(-jnp.abs(raw)))
    dt = jnp.where(lanes_of(rows) < HEADS, soft, 0.0)
    log = dot(triangle(rows, True).astype(F32), dt * hp[1:2, :], EXACT)
    last = log[rows - 1 : rows, :]
    weight = marks[:, 4:5] * jnp.exp(last - log) * dt
    dt_o[...] = dt
    log_o[...] = log
    b_cols = None
    for j in range(CONV_CH // LANES):
        ext = pc[:, tile(j)].astype(F32)
        out = cw[4:5, tile(j)] + cw[3:4, tile(j)] * ext[HALO:, :]
        for k in range(CONV_K - 1):
            out = out + cw[k : k + 1, tile(j)] * ext[LEAD + k : LEAD + k + rows, :] * marks[:, k : k + 1]
        part, at = parted(j, (left_o, right_o, bc_o))
        part[:, at] = out
        if j < PAIRS:
            high, rest = halves(silu(out) * spread(weight, j))
            xw[:, tile(j)] = high
            if precise:
                low[0][:, tile(j)] = rest
        elif j == PAIRS:
            b_cols, b_rest = halves(silu(out).T)
    total = dot(b_cols, xw[...])
    if precise:
        total = total + (dot(b_rest, xw[...]) + dot(b_cols, low[0][...]))
    keep = spread_row(jnp.exp(last) * marks[rows - 1 : rows, 3:4])
    emit_halves(total, keep, bit_of(me, 1), own_o, msg_o)


def mask_bias(mk, sr, rows):
    same = mk[:, 5:6] == sr[0:1, :]
    return jnp.where(jnp.logical_and(triangle(rows, True), same), 0.0, FAR)


def within_kernel(conv, bc, dt, log, hp, mk, sr, y_o, xdt, lcol, lrow, *lower, precise, first):
    rows = mk.shape[0]
    pairs = PAIRS // 2
    scores = fine(dot_t, silu(bc[:, tile(1)]), silu(bc[:, tile(0)]))
    bias = mask_bias(mk, sr, rows)
    dtv, logv = dt[...], log[...]
    lrow[...] = logv.T
    for j in range(pairs):
        x = silu(conv[:, tile(j)])
        high, rest = halves(x * spread(dtv, first + j))
        xdt[:, tile(j)] = high
        if precise:
            lower[0][:, tile(j)] = rest
        y_o[:, tile(j)] = x * spread(hp[2:3, :], first + j)
    for h in range(2 * pairs):
        lcol[h] = jnp.broadcast_to(logv[:, 2 * first + h : 2 * first + h + 1], (rows, LANES))
    low = lanes_of(rows) < HEAD_DIM

    def pair(j, _):
        at = pl.ds(pl.multiple_of(j * LANES, LANES), LANES)
        xp = xdt[:, at]
        res = []
        for q in range(2):
            col = lcol[2 * j + q]
            row = lrow[pl.ds(2 * (first + j) + q, 1), :]
            span = jnp.concatenate([col] * (rows // LANES), axis=1) - row
            mix = scores * jnp.exp(span + bias)
            if precise:
                high, rest = halves(mix)
                res.append(dot(high, xp) + (dot(rest, xp) + dot(high, lower[0][:, at])))
            else:
                res.append(dot(mix.astype(BF16), xp))
        y_o[:, at] += jnp.where(low, res[0], res[1])
        return 0

    lax.fori_loop(0, pairs, pair, 0)


def post_kernel(*refs, places, relative, spans, aligned):
    if spans:
        pack, *refs = refs
        *refs, gated, zbuf, obuf, sems = refs
        parts = len(spans) - 1
        refs, raw = [*refs[:-parts], gated], refs[-parts:]
    else:
        z_low, z_high, out_w, *refs = refs
    normed, h, yw, yw2, mine, recv, bc, log, mk, gg, me, z, y_o, gn_o, st_o, st2_o, h_o, *rel_o, gated = refs
    rows = mk.shape[0]
    wide = 2 * LANES
    half = INNER // 2
    own = normed[HALO:, :]
    flying = []

    def moved(source, target):
        copy = pltpu.make_async_copy(source, target, sems.at[len(flying)])
        flying.append(copy)
        copy.start()
        return copy

    def apart(buffer, base, k):
        return moved(buffer.at[:, spans[k] - base : spans[k + 1] - base, :], raw[k])

    if spans:
        coming = [moved(pack.at[:, spans[0] : spans[2], :], zbuf), moved(pack.at[:, spans[2] : spans[3], :], obuf)]
        coming[0].wait()
        leaving = [apart(zbuf, 0, 0), apart(zbuf, 0, 1)]

    def project(i, _):
        for q in range(2):
            at = pl.ds(pl.multiple_of(i * wide, wide), wide)
            if spans:
                part = zbuf[:, spans[q] : spans[q + 1], at]
                part = part.reshape(-1, part.shape[-1])
            else:
                part = (z_low, z_high)[q][:, at]
            z[:, pl.ds(pl.multiple_of(q * half + i * wide, wide), wide)] = dot(own, part).astype(BF16)
        return 0

    lax.fori_loop(0, half // wide, project, 0)
    if spans:
        for copy in leaving:
            copy.wait()
        more = len(spans) > 4
        if more:
            second = moved(pack.at[:, spans[3] : spans[5], :], zbuf)
        coming[1].wait()
        leaving = [apart(obuf, spans[2], 2)]
    low, high = join_halves(mine, recv, bit_of(me, 1))
    st_o[...] = low.astype(BF16)
    st2_o[...] = high.astype(BF16)
    c = silu(bc[:, tile(1)])
    inflow = jnp.exp(log[...]) * mk[:, 3:4]
    total = jnp.zeros((rows, LANES), F32)
    for j in range(PAIRS):
        part = (yw if j < PAIRS // 2 else yw2)[:, tile(j % (PAIRS // 2))]
        state = (low if j < PAIRS // 2 else high)[:, tile(j % (PAIRS // 2))]
        y = part + fine(dot, c, state) * spread(inflow, j)
        y_o[:, tile(j)] = y
        v = y * silu(z[:, tile(j)].astype(F32))
        gated[:, tile(j)] = v
        total = total + v * v
    inv = lax.rsqrt(jnp.sum(total, axis=-1, keepdims=True) / INNER + EPS)
    for j in range(PAIRS):
        gn_o[:, tile(j)] = (gated[:, tile(j)] * inv * gg[0:1, tile(j)]).astype(BF16)

    if spans and more:
        second.wait()
        leaving += [apart(zbuf, spans[3], 3), apart(zbuf, spans[3], 4)]

    def output(i, _):
        at = pl.ds(pl.multiple_of(i * wide, wide), wide)
        if spans:
            part = obuf[:, :, at]
            part = part.reshape(-1, part.shape[-1])
        else:
            part = out_w[:, at]
        h_o[:, at] = h[:, at].astype(F32) + dot(gn_o[...], part)
        return 0

    lax.fori_loop(0, h.shape[1] // wide, output, 0)
    if spans and more:
        leaving[0].wait()
        last = obuf.at[:, : spans[6] - spans[5], :]
        moved(pack.at[:, spans[5] : spans[6], :], last).wait()
        leaving = leaving[1:] + [moved(last, raw[5])]
    if rel_o:
        lower = lanes_of(rows) < HEAD_DIM
        for j in range(PAIRS):
            base = me[0] if relative else jnp.int32(0)
            sources = [jnp.bitwise_xor(base, jnp.int32(int(places[2 * j + q]))) for q in range(2)]
            upper = jnp.bitwise_and(sources[0], 1) == 1
            tiles = []
            for src in sources:
                at = pl.multiple_of(lax.shift_right_logical(src, 1) * LANES, LANES)
                tiles.append(gn_o[:, pl.ds(at, LANES)].astype(F32))
            left = jnp.where(upper, pltpu.roll(tiles[0], HEAD_DIM, 1), tiles[0])
            right = jnp.where(upper, tiles[1], pltpu.roll(tiles[1], HEAD_DIM, 1))
            rel_o[0][:, tile(j)] = jnp.where(lower, left, right).astype(BF16)
    if spans:
        for copy in leaving:
            copy.wait()


def post_back_kernel(ggn, y, z, gg, left, right, bc, log, mk, me, gy_o, gy2_o, gz_o, gate_o, skip_o, own_o, msg_o, ge):
    rows = mk.shape[0]
    logv = log[...]
    inflow = jnp.exp(logv) * mk[:, 3:4]
    total = jnp.zeros((rows, LANES), F32)
    cross = jnp.zeros((rows, LANES), F32)
    for j in range(PAIRS):
        v = y[:, tile(j)] * silu(z[:, tile(j)].astype(F32))
        total = total + v * v
        cross = cross + v * ggn[:, tile(j)] * gg[0:1, tile(j)]
    inv = lax.rsqrt(jnp.sum(total, axis=-1, keepdims=True) / INNER + EPS)
    mean = jnp.sum(cross, axis=-1, keepdims=True) * inv / INNER
    skips = jnp.zeros((8, LANES), F32)
    for j in range(PAIRS):
        zf = z[:, tile(j)].astype(F32)
        s = sigmoid(zf)
        sz = zf * s
        yv = y[:, tile(j)]
        n = yv * sz * inv
        up = ggn[:, tile(j)]
        gga = inv * (up * gg[0:1, tile(j)] - n * mean)
        gy = gga * sz
        gz_o[:, tile(j)] = (gga * yv * (s * (1.0 + zf * (1.0 - s)))).astype(BF16)
        part, at = parted(j, (gy_o, gy2_o))
        part[:, at] = gy.astype(BF16)
        ge[:, tile(j)] = (gy * spread(inflow, j)).astype(BF16)
        gate_o[:, tile(j)] = jnp.broadcast_to(jnp.sum(up * n, axis=0, keepdims=True), (8, LANES))
        part, at = parted(j, (left, right))
        through = jnp.sum(gy * silu(part[:, at]), axis=0, keepdims=True)
        skips = skips + head_sums(jnp.broadcast_to(through, (8, LANES)), j)
    skip_o[...] = skips
    c_cols = silu(bc[:, tile(1)]).T.astype(BF16)
    state = dot(c_cols, ge[...])
    keep = spread_row(jnp.exp(logv[rows - 1 : rows, :]) * mk[rows - 1 : rows, 3:4])
    emit_halves(state, keep, bit_of(me, 1), own_o, msg_o)


def within_back_kernel(
    conv, bc, dt, log, gy, st, mk, sr, gxdt_o, gb_o, gc_o, gl_o, xdt, ge, lcol, lrow, gscore, lsum, csum, *, first
):
    rows = mk.shape[0]
    pairs = PAIRS // 2
    bf, cf = silu(bc[:, tile(0)]), silu(bc[:, tile(1)])
    b, c = bf.astype(BF16), cf.astype(BF16)
    scores = fine(dot_t, bf, cf)
    same = mk[:, 5:6] == sr[0:1, :]
    bias = jnp.where(jnp.logical_and(triangle(rows, False), same), 0.0, FAR)
    dtv, logv = dt[...], log[...]
    lrow[...] = logv.T
    inflow = jnp.exp(logv) * mk[:, 3:4]
    flow = jnp.zeros((rows, LANES), F32)
    for j in range(pairs):
        xdt[:, tile(j)] = (silu(conv[:, tile(j)]) * spread(dtv, first + j)).astype(BF16)
        gyv = gy[:, tile(j)].astype(F32) * spread(inflow, first + j)
        ge[:, tile(j)] = gyv.astype(BF16)
        flow = flow + head_sums(gyv * dot(c, st[:, tile(j)]), first + j)
    for h in range(2 * pairs):
        lcol[h] = jnp.broadcast_to(logv[:, 2 * first + h : 2 * first + h + 1], (rows, LANES))
    lanes = lanes_of(rows)
    low = lanes < HEAD_DIM
    gscore[...] = jnp.zeros_like(gscore)
    csum[...] = jnp.zeros_like(csum)
    lsum[...] = jnp.zeros_like(lsum)

    def pair(j, _):
        at = pl.ds(pl.multiple_of(j * LANES, LANES), LANES)
        xp, gp = xdt[:, at], gy[:, at]
        res = []
        for q in range(2):
            h = 2 * (first + j) + q
            span = lrow[pl.ds(h, 1), :] - jnp.concatenate([lcol[2 * j + q]] * (rows // LANES), axis=1)
            decay = jnp.exp(span + bias)
            mix = scores * decay
            own = jnp.where(low if q == 0 else jnp.logical_not(low), gp, jnp.zeros_like(gp))
            gmix = dot_t(xp, own)
            gscore[...] += gmix * decay
            term = gmix * mix
            lsum[pl.ds(h, 1), :] = jnp.sum(term, axis=0, keepdims=True)
            csum[...] += jnp.where(lanes == h, jnp.sum(term, axis=1, keepdims=True), 0.0)
            res.append(dot(mix.astype(BF16), gp))
        gxdt_o[:, at] = jnp.where(low, res[0], res[1])
        return 0

    lax.fori_loop(0, pairs, pair, 0)
    gs = gscore[...]
    gb_o[...] = dot(gs.astype(BF16), c)
    gc_o[...] = dot(gs.T.astype(BF16), b) + dot_t(ge[...], st[...])
    gl_o[...] = lsum[...].T - csum[...] + flow


def mixer_back_kernel(
    gxdt2, gy2, right, pc, cw, gxdt, gbi, gci, gli, gbi2, gci2, gli2, mine, recv, gy, left, bc, dt, log, st, st2,
    hp, mk, gate, skip, me, gp_o, wide_o, gb16, xe, acc,
):
    rows = mk.shape[0]
    marks = mk[...]
    low, high = join_halves(mine, recv, bit_of(me, 1))
    half = INNER // 2
    kg = jnp.zeros((8, LANES), F32)
    for part, value in ((0, low), (half, high)):
        gb16[:, part : part + half] = value.astype(BF16)
        rowsum = jnp.sum(value * (st if part == 0 else st2)[...].astype(F32), axis=0, keepdims=True)
        for j in range(PAIRS // 2):
            pair = part // LANES + j
            kg = kg + head_sums(jnp.broadcast_to(rowsum[:, tile(j)], (8, LANES)), pair)
    dtv, logv = dt[...], log[...]
    last = logv[rows - 1 : rows, :]
    b = silu(bc[:, tile(0)]).astype(BF16)
    outflow = marks[:, 4:5] * jnp.exp(last - logv)
    gv = jnp.zeros((rows, LANES), F32)
    gd = jnp.zeros((rows, LANES), F32)

    def conv_back(j, gact, s, out):
        gco = gact * (s * (1.0 + out * (1.0 - s)))
        ext = pc[:, tile(j)].astype(F32)
        acc[...] = jnp.zeros_like(acc)
        for k in range(CONV_K):
            gk = gco if k == CONV_K - 1 else gco * marks[:, k : k + 1]
            wide_o[k : k + 1, tile(j)] = jnp.sum(gk * ext[LEAD + k : LEAD + k + rows, :], axis=0, keepdims=True)
            acc[LEAD + k : LEAD + k + rows, :] += gk * cw[k : k + 1, tile(j)]
        wide_o[4:5, tile(j)] = jnp.sum(gco, axis=0, keepdims=True)
        gp_o[:, tile(j)] = acc[...].astype(BF16)

    wide_o[6:8, :] = jnp.zeros((2, CONV_CH), F32)
    for j in range(PAIRS):
        part, at = parted(j, (left, right))
        out = part[:, at]
        s = sigmoid(out)
        x = out * s
        dtp = spread(dtv, j)
        flow = spread(outflow, j)
        xd = x * dtp
        gxs = dot(b, gb16[:, tile(j)]) * flow
        xe[:, tile(j)] = (xd * flow).astype(BF16)
        gxd = (gxdt if j < PAIRS // 2 else gxdt2)[:, at] + gxs
        gv = gv + head_sums(xd * gxs, j)
        gd = gd + head_sums(x * gxd, j)
        conv_back(j, dtp * gxd + spread(hp[2:3, :], j) * (gy if j < PAIRS // 2 else gy2)[:, at].astype(F32), s, out)
    gb = gbi[...] + gbi2[...] + dot_t(xe[...], gb16[...])
    for j, grad in ((PAIRS, gb), (PAIRS + 1, gci[...] + gci2[...])):
        out = bc[:, tile(j - PAIRS)]
        conv_back(j, grad, sigmoid(out), out)
    keep = jnp.exp(last) * marks[rows - 1 : rows, 3:4]
    edge = jnp.sum(gv, axis=0, keepdims=True) + kg[0:1, :] * keep
    place = lax.broadcasted_iota(jnp.int32, (rows, LANES), 0)
    gl = gli[...] + gli2[...] - gv + jnp.where(place == rows - 1, edge, 0.0)
    ga = dot(triangle(rows, False).astype(F32), gl, EXACT)
    rate = hp[1:2, :]
    raw = pc[HALO:, CONV_CH:WIDE].astype(F32) + hp[0:1, :]
    graw = jnp.where(lanes_of(rows) < HEADS, (ga * rate + gd) * sigmoid(raw), 0.0)
    gp_o[0:HALO, CONV_CH:WIDE] = jnp.zeros((HALO, LANES), BF16)
    gp_o[HALO:, CONV_CH:WIDE] = graw.astype(BF16)
    wide_o[5:6, 0:INNER] = gate[0:1, :]
    place = lanes_of(1)
    heads = jnp.where(place < HEADS, jnp.sum(graw, axis=0, keepdims=True), 0.0)
    for k, row in enumerate((rate * jnp.sum(ga * dtv, axis=0, keepdims=True), skip[0:1, :])):
        heads = heads + jnp.where(place // HEADS == k + 1, pltpu.roll(row, HEADS * (k + 1), 1), 0.0)
    wide_o[5:6, INNER : INNER + LANES] = heads
    wide_o[5:6, INNER + LANES :] = jnp.zeros((1, CONV_CH - INNER - LANES), F32)


def row_of(values, rows=8):
    pad = [(0, rows - values.shape[0]), (0, max(0, LANES - values.shape[1]))]
    return jnp.pad(values.astype(F32), pad)


def per_device(
    hidden, segment_ids, in_weight, out_weight, conv_weight, conv_bias, norm_gain, gate_gain,
    dt_bias, a_log, skip_param, cotangent,
):
    layers_n, in_rows = in_weight.shape[:2]
    out_rows = out_weight.shape[1]
    rows, width = hidden.shape
    count = lax.axis_size("seq")
    me = lax.axis_index("seq")
    me_ref = me.reshape(1).astype(jnp.int32)
    conv_n = conv_bias.shape[1]
    half = INNER // 2
    plane_n = axes_of(count)["z"][1]

    small = jnp.concatenate(
        [conv_weight.reshape(-1), conv_bias.reshape(-1), norm_gain.reshape(-1), gate_gain.reshape(-1)]
    )
    length = small.shape[0]
    small_rows = -(-length // (16 * LANES)) * 16
    small = jnp.pad(small, (0, small_rows * LANES - length)).reshape(small_rows, LANES)
    in_weight_side = jnp.pad(in_weight[0, :, INNER:], ((0, 0), (0, WIDE - SIDE)))
    halo = shifted(hidden[rows - HALO :], 1)
    seg_halo = shifted(segment_ids[rows - HALO :] + 1, 1) - 1
    packs = []
    for layer in range(layers_n):
        parts = [in_weight[layer, :, :half], in_weight[layer, :, half:INNER], out_weight[layer]]
        if layer + 1 < layers_n:
            later = in_weight[layer + 1, :, INNER:]
            parts += [later[:, :half], later[:, half : 2 * half]]
            parts.append(jnp.pad(later[:, 2 * half :], ((0, 0), (0, 3 * half - SIDE))))
        packs.append((jnp.concatenate(parts, axis=0), np.cumsum([0] + [p.shape[0] for p in parts]).tolist()))
    first = Gather(in_weight_side)
    started = first.line(tuple(pack for pack, _ in packs))
    gathered = [lax.all_gather(after(pack, started), "seq") for pack, _ in packs]
    crossed = first.plane()
    smalls = gather_small(small, [(), (), (started,), (started,), (crossed,)])

    seg_pad = jnp.concatenate([seg_halo[LEAD:], segment_ids])
    before = seg_pad[CONV_K - 2]
    columns = [seg_pad[k : k + rows] == segment_ids for k in range(CONV_K - 1)]
    columns += [segment_ids == before, segment_ids == segment_ids[-1], segment_ids]
    marks = jnp.pad(jnp.stack([col.astype(F32) for col in columns], axis=1), ((0, 0), (0, LANES - 6)))
    seg_row = jnp.broadcast_to(segment_ids.astype(F32)[None, :], (8, rows))

    relative, planes = relative_places(count), plane_first(count)
    order = column_order(relative, me, in_rows)
    plane_order = column_order(planes, 0, in_rows)

    place = (jnp.arange(count)[:, None] == (jnp.arange(count) ^ me)[None, :]).astype(BF16)
    smalls = dot(place, smalls.reshape(count, small_rows * LANES))
    sizes = [layers_n * CONV_K * conv_n, layers_n * conv_n, layers_n * in_rows, layers_n * out_rows]
    cuts = np.cumsum([0] + sizes)
    taps, biases, gains, gate_gains = (smalls[:, cuts[i] : cuts[i + 1]] for i in range(4))
    taps = taps.reshape(count, layers_n, CONV_K, conv_n).transpose(1, 2, 0, 3).reshape(layers_n, CONV_K, CONV_CH)
    biases = biases.reshape(count, layers_n, 1, conv_n).transpose(1, 2, 0, 3).reshape(layers_n, 1, CONV_CH)
    conv_rows = jnp.pad(jnp.concatenate([taps, biases], axis=1), ((0, 0), (0, 3), (0, 0)))
    gains = gains.reshape(count, layers_n, in_rows).transpose(1, 0, 2).reshape(layers_n, 1, width)
    gate_gains = gate_gains.reshape(count, layers_n, out_rows).transpose(1, 0, 2).reshape(layers_n, 1, INNER)
    gains = [jnp.broadcast_to(gains[layer], (8, width)) for layer in range(layers_n)]
    gate_gains = [jnp.broadcast_to(gate_gains[layer], (8, INNER)) for layer in range(layers_n)]
    conv_rows = [conv_rows[layer] for layer in range(layers_n)]
    heads = [
        row_of(jnp.stack([dt_bias[layer], -jnp.exp(a_log[layer]), skip_param[layer]])) for layer in range(layers_n)
    ]

    (left, left2), (right, right2) = first.whole((*conv_rows, *gains, *gate_gains, *heads, marks, seg_row, halo, order))

    scratch_wide = pltpu.VMEM((rows, INNER), BF16)
    scratch_half = pltpu.VMEM((rows, INNER // 2), BF16)
    scratch_cols = pltpu.VMEM((HEADS // 2, rows, LANES), F32)
    scratch_rows = pltpu.VMEM((LANES, rows), F32)

    residual = hidden
    saved, sides = [], ()
    for layer in range(layers_n):
        precise = layer + 1 < layers_n
        gain, gate = gains[layer], gate_gains[layer]
        (normed,) = kernel_call(norm_kernel, [((HALO + rows, width), BF16)], (residual, halo, gain))
        normed_rel = dot(normed, order).astype(BF16)
        if layer == 0:
            lower, upper = normed_rel[:, : width // 2], normed_rel[:, width // 2 :]
            parts = [dot(lower, left) + dot(upper, left2), dot(lower, right) + dot(upper, right2)]
        else:
            parts = [dot(normed, part) for part in side_parts[:2]]
            parts.append(dot(normed, side_parts[2][:, : WIDE - 2 * half]))
        pc = jnp.concatenate([part.astype(BF16) for part in parts], axis=1)
        hp = heads[layer]
        conv_l, conv_r, bc, dt, log, own, msg = kernel_call(
            partial(conv_state_kernel, precise=precise),
            [((rows, half), F32)] * 2 + [((rows, 2 * STATE), F32)] + [((rows, LANES), F32)] * 2
            + [state_out(half)] * 2,
            (pc, conv_rows[layer], hp, marks, me_ref),
            scratch=[scratch_wide] * (2 if precise else 1), flops=2 * rows * STATE * INNER * 8,
        )
        yw = [
            kernel_call(
                partial(within_kernel, precise=precise, first=part * PAIRS // 2), [((rows, half), F32)],
                ((conv_l, conv_r)[part], bc, dt, log, hp, marks, seg_row),
                scratch=[scratch_half, scratch_cols, scratch_rows] + [scratch_half] * precise,
                flops=2 * rows * rows * half * 16, deps=(own,),
            )[0]
            for part in range(2)
        ]
        mine, recv = exchange(own, msg, me_ref, False, [(), (yw[0],), (yw[1],), ()])
        aligned = out_rows == HEAD_DIM
        pack, spans = gathered[layer], packs[layer][1]
        weights = [pack[:, a:b].reshape(-1, width) for a, b in zip(spans, spans[1:])]
        outs = [((rows, INNER), BF16), ((rows, INNER), F32), ((rows, INNER), BF16)] + [((STATE, half), BF16)] * 2
        outs += [((rows, width), F32)] + [((rows, INNER), BF16)] * aligned
        form = partial(post_kernel, places=planes, relative=False)
        args = (normed, residual, *yw, mine, recv, bc, log, marks, gate, me_ref)
        scratch = [pltpu.VMEM((rows, INNER), F32)]
        flops = 2 * rows * width * INNER * 2
        if in_rows % HALO:
            z, y, gnormed, state, state2, after_h, *gn_rel = kernel_call(
                partial(form, spans=(), aligned=aligned), outs, (*weights[:3], *args), scratch=scratch, flops=flops
            )
        else:
            z, y, gnormed, state, state2, after_h, *rest = streamed_call(
                partial(form, spans=spans, aligned=aligned), outs, args, flops=flops, streamed=pack,
                scratch=scratch + [pltpu.VMEM((count, 2 * in_rows, width), BF16)] * 2,
                raw=[((count, b - a, width), BF16) for a, b in zip(spans, spans[1:])],
            )
            gn_rel = rest[:aligned]
            weights = [part.reshape(-1, width) for part in rest[aligned:]]
        weights, side_parts = weights[:3], weights[3:]
        if not aligned:
            gn_rel = [dot(gnormed, column_order(planes, 0, out_rows)).astype(BF16)]
        saved.append((residual, normed, normed_rel, pc, conv_l, conv_r, bc, dt, log, hp, z, y, gn_rel[0], state, state2, weights, sides))
        sides = side_parts
        residual = after_h
        if layer + 1 < layers_n:
            halo = shifted(residual[rows - HALO :], 1)

    grad = cotangent
    pack_sums, side_shares = [None] * layers_n, [None] * layers_n
    for layer in range(layers_n - 1, -1, -1):
        h, normed, normed_rel, pc, conv_l, conv_r, bc, dt, log, hp, z, y, gn_rel, state, state2, weights, sides = saved[layer]
        z_low, z_high, out_w = weights
        gain, gate = gains[layer], gate_gains[layer]
        mixed = grad.astype(BF16)
        gy, gy2, gz, gate_grad, skip_grad, own, msg = kernel_call(
            post_back_kernel,
            [((rows, half), BF16)] * 2 + [((rows, INNER), BF16), ((8, INNER), F32), ((8, LANES), F32)]
            + [state_out(half), state_out(half, BF16)],
            (dot_t(mixed, out_w), y, z, gate, conv_l, conv_r, bc, log, marks, me_ref),
            scratch=[scratch_wide], flops=2 * rows * STATE * INNER * 8,
        )
        halves_back = [
            kernel_call(
                partial(within_back_kernel, first=part * PAIRS // 2),
                [((rows, half), F32), ((rows, LANES), F32), ((rows, LANES), F32), ((rows, LANES), F32)],
                ((conv_l, conv_r)[part], bc, dt, log, (gy, gy2)[part], (state, state2)[part], marks, seg_row),
                scratch=[
                    scratch_half, scratch_half, scratch_cols, scratch_rows,
                    pltpu.VMEM((rows, rows), F32), scratch_rows, pltpu.VMEM((rows, LANES), F32),
                ],
                flops=2 * rows * rows * half * 32,
            )
            for part in range(2)
        ]
        normed_planes = dot(normed, plane_order).astype(BF16)
        (term,) = grads_call(gn_rel, normed_planes, mixed, gz, count, 1)
        pack_sums[layer] = scatter_planes(term.reshape(-1, width))
        deps = [(), (term,), (halves_back[0][0],), (halves_back[1][0],)]
        late = ()
        if layer + 1 < layers_n:
            deps[0] += (far(pack_sums[layer + 1]),)
            late = tuple(far(part) for part in side_shares[layer + 1].terms[1:3])
        mine, recv = exchange(own, msg, me_ref, True, deps)

        (gx, *sums), (gx2, *sums2) = halves_back
        gp, wide = kernel_call(
            mixer_back_kernel,
            [((HALO + rows, WIDE), BF16), ((8, CONV_CH), F32)],
            (
                gx2, gy2, conv_r, pc, conv_rows[layer], gx, *sums, *sums2, mine, recv, gy, conv_l, bc, dt, log,
                state, state2, hp, marks, gate_grad, skip_grad, me_ref,
            ),
            scratch=[pltpu.VMEM((STATE, INNER), BF16), scratch_wide, pltpu.VMEM((HALO + rows, LANES), F32)],
            flops=2 * rows * STATE * INNER * 24, deps=late,
        )
        spilled = shifted(gp[:HALO], -1)
        side_shares[layer] = share_terms(normed_rel, gp)
        both = (side_shares[layer].terms[0], side_shares[layer].send)
        if layer:
            pieces = tuple(side_shares[layer].step())
        else:
            pieces = tuple(side_shares[layer].step())
            for share in side_shares[1:]:
                share.step(behind=pieces[0])
        gp_own, gz = kernel_call(
            own_rows_kernel, [((rows, WIDE), BF16), ((rows, INNER), BF16)], (gp, spilled, gz),
            deps=both if layer else (far(pieces[0]),),
        )
        gn_z = dot_t(gz[:, :half], z_low) + dot_t(gz[:, half:], z_high)
        if layer:
            gn = gn_z
            for k, part in enumerate(sides):
                piece = gp_own[:, k * half : min((k + 1) * half, WIDE)]
                gn = gn + dot_t(piece, part[:, : piece.shape[1]])
        else:
            gp_left, gp_right = gp_own[:, :CUT], gp_own[:, CUT:]
            gn_side = jnp.concatenate(
                [dot_t(gp_left, left) + dot_t(gp_right, right), dot_t(gp_left, left2) + dot_t(gp_right, right2)],
                axis=1,
            )
            gn_high, gn_low = halves(gn_side)
            gn = gn_z + dot_t(gn_high, order) + dot_t(gn_low, order)
        grad, small_grads = kernel_call(
            norm_back_kernel, [((rows, width), F32), ((8 * (layers_n - layer), CONV_CH), F32)],
            (gn, h, grad, gain, wide) + ((small_grads,) if layer + 1 < layers_n else ()),
            deps=tuple(
                far(part)
                for part in (pieces if layer else (pack_sums[0], *[t for v in side_shares[1:] for t in v.terms[1:]]))
            ),
        )
    (sums,) = kernel_call(round_kernel, [(small_grads.shape, BF16)], (small_grads,))
    sums = sum_rounds(sums, count // 2, plane_n)
    side_shares[0].step()
    sums = sum_rounds(sums, plane_n // 2, 1, [(far(part),) for part in side_shares[0].terms[1:]])
    terms, split = [], []
    for layer in range(layers_n):
        terms += [scatter_lines(pack_sums[layer]), *side_shares[layer].terms]
        split.append((1, len(side_shares[layer].terms)))
    in_grads, out_grads = kernel_call(
        partial(shares_kernel, split=split),
        [((layers_n, in_rows, INNER + SIDE), F32), ((layers_n, out_rows, width), F32)], terms, deps=(sums,),
    )
    sums = sums.reshape(layers_n, 8, CONV_CH)

    def share(values):
        span = values.shape[-1] // count
        return lax.dynamic_slice_in_dim(values, me * span, span, values.ndim - 1)

    heads = sums[:, 5, INNER : INNER + 3 * HEADS]
    return (
        residual, grad, in_grads, out_grads,
        share(sums[:, :CONV_K]), share(sums[:, CONV_K]), share(sums[:, 6, :width]), share(sums[:, 5, :INNER]),
        heads[:, :HEADS], heads[:, HEADS : 2 * HEADS], heads[:, 2 * HEADS :],
    )


def solution(mesh):
    return jax.shard_map(
        per_device,
        mesh=mesh,
        in_specs=(
            P("seq", None), P("seq"), P(None, "seq", None), P(None, "seq", None), P(None, None, "seq"),
            P(None, "seq"), P(None, "seq"), P(None, "seq"), P(), P(), P(), P("seq", None),
        ),
        out_specs=(
            P("seq", None), P("seq", None), P(None, "seq", None), P(None, "seq", None), P(None, None, "seq"),
            P(None, "seq"), P(None, "seq"), P(None, "seq"), P(), P(), P(),
        ),
        check_vma=False,
    )
```

```python
from functools import partial

import jax
import jax.numpy as jnp
import numpy as np
from jax import lax
from jax.experimental import pallas as pl
from jax.experimental.pallas import tpu as pltpu
from jax.sharding import PartitionSpec as P

HEADS = 32
HEAD_DIM = 64
STATE = 128
CONV_K = 4
INNER = 2048
CONV_CH = 2304
SIDE = CONV_CH + HEADS
WIDE = 2432
CUT = 1280
LANES = 128
PAIRS = HEADS // 2
HALO = 16
LEAD = HALO - (CONV_K - 1)
FAR = -1e30

EPS = 1e-05
F32 = jnp.float32
BF16 = jnp.bfloat16
EXACT = lax.Precision.HIGHEST
MB = 1024 * 1024
CAP = 16 * MB


def axes_of(count):
    side = 4 if count >= 128 else 2
    plane = 2 * side * side
    return {"c": (2, 1), "x": (side, 2), "y": (side, 2 * side), "z": (count // plane, plane)}


def swap(value, flip):
    count = lax.axis_size("seq")
    return lax.ppermute(value, "seq", [(i, i ^ flip) for i in range(count)])


def shifted(shard, by):
    count = lax.axis_size("seq")
    return lax.ppermute(shard, "seq", [(i, i + by) for i in range(count) if 0 <= i + by < count])


def relative_places(count):
    axes = axes_of(count)
    places = np.zeros((1,), np.int32)
    for name in ("c", "y", "x", "z"):
        size, shift = axes[name]
        places = (places[:, None] + np.arange(size, dtype=np.int32)[None, :] * shift).reshape(-1)
    return places


def column_order(places, me, block):
    count = len(places)
    places = jnp.asarray(np.repeat(places, block))
    inner = jnp.asarray(np.tile(np.arange(block, dtype=np.int32), count))
    source = (places ^ me) * block + inner
    return (jnp.arange(count * block)[:, None] == source[None, :]).astype(BF16)


class Gather:

    def __init__(self, shard):
        self.axes = axes_of(lax.axis_size("seq"))
        self.rows = shard.shape[0]
        self.kind = shard.dtype
        self.shard, self.sent = shard, self.send(shard, "z")

    def send(self, value, name):
        size, shift = self.axes[name]
        return [swap(value, d * shift) for d in range(1, size)]

    def outs(self, *lead):
        return [((*lead, self.rows, CUT), self.kind), ((*lead, self.rows, WIDE - CUT), self.kind)]

    def line(self, deps=()):
        everything = slice(None)
        cuts = ((everything, slice(0, CUT)), (everything, slice(CUT, WIDE)))
        pieces = [
            (value, side, cuts[side], d) for side in range(2) for d, value in enumerate([self.shard, *self.sent])
        ]
        self.left, self.right = copies_call(pieces, self.outs(self.axes["z"][0]), deps)
        self.sent = self.send(self.left, "x"), self.send(self.right, "y")
        return self.left

    def plane(self, deps=()):
        sides = ((self.left, *self.sent[0]), (self.right, *self.sent[1]))
        pieces = [(value, side, None, d) for side in range(2) for d, value in enumerate(sides[side])]
        line, across, up = (self.axes[name][0] for name in ("z", "x", "y"))
        outs = [self.outs(across, line)[0], self.outs(up, line)[1]]
        self.left, self.right = copies_call(pieces, outs, deps)
        self.sent = self.send(self.left, "y"), self.send(self.right, "x")
        return self.left

    def whole(self, deps=()):
        line, across, up = (self.axes[name][0] for name in ("z", "x", "y"))
        pieces = [(value, 0, None, d) for d, value in enumerate([self.left, *self.sent[0]])]
        pieces += [
            (value, 1, i, (i, d)) for d, value in enumerate([self.right, *self.sent[1]]) for i in range(up)
        ]
        left, right = copies_call(pieces, self.outs(up, across, line), deps)
        left, right = left.reshape(-1, left.shape[-1]), right.reshape(-1, right.shape[-1])
        return (left, swap(left, 1)), (right, swap(right, 1))


class Shares:

    def __init__(self, keep, send):
        line, plane = axes_of(lax.axis_size("seq"))["z"]
        self.groups = [(plane // 2, 2), (line, plane)]
        shape = (plane // 2, line, keep.shape[0] // (plane // 2 * line), keep.shape[1])
        self.send = send
        self.terms = [keep.reshape(shape), swap(send.reshape(shape), 1)]

    def step(self, deps=(), behind=None):
        size, shift = self.groups.pop(0)
        if deps:
            pieces = list(
                kernel_call(pieces_kernel, [(self.terms[0].shape[1:], BF16)] * size, self.terms, deps=deps)
            )
        else:
            none = 0.0
            if behind is not None:
                none = held_back(behind)
            pieces = []
            for d in range(size):
                picked = [t[d].astype(F32) for t in self.terms]
                pieces.append((sum(picked[1:], picked[0]) + none).astype(BF16))
        self.terms = [pieces[0]] + [swap(pieces[d], d * shift) for d in range(1, size)]
        return pieces


def pieces_kernel(*refs):
    size = refs[0].shape[0]
    terms, outs = refs[:-size], refs[-size:]
    for d, out in enumerate(outs):
        total = terms[0][d].astype(F32)
        for term in terms[1:]:
            total = total + term[d].astype(F32)
        out[...] = total.astype(BF16)


def turned_dot(left, right):
    return lax.dot_general(left, right, (((0,), (0,)), ((), ())), preferred_element_type=F32).astype(BF16)


def share_terms(left, right):
    half = left.shape[1] // 2
    return Shares(turned_dot(left[:, :half], right), turned_dot(left[:, half:], right))


def plane_first(count):
    plane = axes_of(count)["z"][1]
    return np.arange(count).reshape(-1, plane).T.reshape(-1)


def scatter_planes(grad):
    count = lax.axis_size("seq")
    plane = axes_of(count)["z"][1]
    groups = np.arange(count).reshape(-1, plane).tolist()
    return lax.psum_scatter(grad, "seq", scatter_dimension=0, tiled=True, axis_index_groups=groups)


def held_back(behind):
    return jnp.minimum(jnp.abs(behind[(0,) * behind.ndim].astype(F32)), 0.0)


def line_terms(grad):
    line, plane = axes_of(lax.axis_size("seq"))["z"]
    place = lax.axis_index("seq") // plane
    parts = grad.reshape(line, -1, grad.shape[1])
    pieces = [lax.dynamic_index_in_dim(parts, place ^ d, 0, False) for d in range(line)]
    return [pieces[0]] + [swap(pieces[d], d * plane) for d in range(1, line)]


def round_kernel(value, out):
    out[...] = value[...].astype(BF16)


def add_kernel(left, right, *outs):
    total = left[...].astype(F32) + right[...].astype(F32)
    for out in outs:
        out[...] = total.astype(out.dtype)


def sum_rounds(value, first, last, deps=()):
    flip = first
    while flip >= last:
        kind = BF16 if flip > 1 else F32
        late, deps = (deps[0], deps[1:]) if deps else ((), ())
        (value,) = kernel_call(add_kernel, [(value.shape, kind)], (value, swap(value, flip)), deps=late)
        flip //= 2
    return value


def gather_small(value, deps):
    flip, rows = 1, value.shape[0]
    while flip < lax.axis_size("seq"):
        late, deps = deps[0], deps[1:] or deps
        first, second = slice(0, flip * rows), slice(flip * rows, 2 * flip * rows)
        pieces = [(value, 0, None, first), (swap(value, flip), 0, None, second)]
        (value,) = copies_call(pieces, [((2 * flip * rows, LANES), value.dtype)], late)
        flip *= 2
    return value


def held_bytes(shape, kind):
    *lead, rows, lanes = (1, *shape) if len(shape) < 2 else shape
    rows, lanes = -(-rows // 16) * 16, -(-lanes // LANES) * LANES
    return int(np.prod(lead, dtype=np.int64)) * rows * lanes * jnp.dtype(kind).itemsize


def room_for(arrays, scratch):
    total = sum(held_bytes(*a) for a in arrays) + sum(held_bytes(r.shape, r.dtype) for r in scratch)
    return total + total // 8 + 3 * MB


def far(array):
    return pltpu.with_memory_space_constraint(array, pltpu.HBM)


def kernel_call(body, outs, args, scratch=(), flops=0, deps=()):
    places = [pltpu.SMEM if a.dtype == jnp.int32 else pltpu.VMEM for a in args] + [pl.ANY] * len(deps)
    known = len(args)

    def run(*refs):
        body(*refs[:known], *refs[known + len(deps) :])

    size = sum(int(np.prod(a.shape)) * a.dtype.itemsize for a in args) + sum(
        int(np.prod(o[0])) * jnp.dtype(o[1]).itemsize for o in outs
    )
    return pl.pallas_call(
        run,
        out_shape=tuple(jax.ShapeDtypeStruct(*o) for o in outs),
        in_specs=[pl.BlockSpec(memory_space=p) for p in places],
        out_specs=tuple(pl.BlockSpec(memory_space=pltpu.VMEM) for _ in outs),
        scratch_shapes=list(scratch),
        compiler_params=pltpu.CompilerParams(vmem_limit_bytes=min(CAP, room_for([(a.shape, a.dtype) for a in args] + list(outs), scratch))
        ),
        cost_estimate=pl.CostEstimate(flops=flops, bytes_accessed=size, transcendentals=0),
    )(*args, *deps)


def streamed_call(body, outs, args, scratch=(), flops=0, streamed=None, raw=()):
    places = [pltpu.SMEM if a.dtype == jnp.int32 else pltpu.VMEM for a in args]
    size = sum(int(np.prod(a.shape)) * a.dtype.itemsize for a in (*args, streamed)) + sum(
        int(np.prod(o[0])) * jnp.dtype(o[1]).itemsize for o in (*outs, *raw)
    )
    return pl.pallas_call(
        body,
        out_shape=tuple(jax.ShapeDtypeStruct(*o) for o in (*outs, *raw)),
        in_specs=[pl.BlockSpec(memory_space=p) for p in (pltpu.HBM, *places)],
        out_specs=tuple(pl.BlockSpec(memory_space=p) for p in [pltpu.VMEM] * len(outs) + [pltpu.HBM] * len(raw)),
        scratch_shapes=[*scratch, pltpu.SemaphoreType.DMA((3 * len(raw),))],
        compiler_params=pltpu.CompilerParams(vmem_limit_bytes=room_for([], scratch) + 8 * MB),
        cost_estimate=pl.CostEstimate(flops=flops, bytes_accessed=size, transcendentals=0),
    )(streamed, *args)


def copies_call(pieces, outs, deps=()):
    arrays = [p[0] for p in pieces]
    known, written = len(arrays), len(outs)

    def run(*refs):
        refs = refs[:known] + refs[known + len(deps) :]
        results, held, (sems, out_sems) = refs[known : known + written], refs[known + written : -2], refs[-2:]
        copies = []
        for k, (_, out, source, target) in enumerate(pieces):
            src = refs[k] if source is None else refs[k].at[source]
            copies.append(pltpu.make_async_copy(src, held[out].at[target], sems.at[k]))
            copies[-1].start()
        for copy in copies:
            copy.wait()
        copies = []
        for k in range(written):
            copies.append(pltpu.make_async_copy(held[k], results[k], out_sems.at[k]))
            copies[-1].start()
        for copy in copies:
            copy.wait()

    size = sum(2 * int(np.prod(o[0])) * jnp.dtype(o[1]).itemsize for o in outs)
    return pl.pallas_call(
        run,
        out_shape=tuple(jax.ShapeDtypeStruct(*o) for o in outs),
        in_specs=[pl.BlockSpec(memory_space=pltpu.HBM)] * known + [pl.BlockSpec(memory_space=pl.ANY)] * len(deps),
        out_specs=tuple(pl.BlockSpec(memory_space=pltpu.HBM) for _ in outs),
        scratch_shapes=[pltpu.VMEM(*o) for o in outs]
        + [pltpu.SemaphoreType.DMA((known,)), pltpu.SemaphoreType.DMA((written,))],
        compiler_params=pltpu.CompilerParams(vmem_limit_bytes=room_for(outs, ())),
        cost_estimate=pl.CostEstimate(flops=0, bytes_accessed=size, transcendentals=0),
    )(*arrays, *deps)


def copy_kernel(value, out):
    out[...] = value[...]


def after(value, *deps):
    return kernel_call(copy_kernel, [(value.shape, value.dtype)], (value,), deps=deps)[0]


def dot(left, right, precision=None):
    return jnp.dot(left, right, precision=precision, preferred_element_type=F32)


def dot_t(left, right):
    return lax.dot_general(left, right, (((1,), (1,)), ((), ())), preferred_element_type=F32)


def halves(value):
    high = value.astype(BF16)
    return high, (value - high.astype(F32)).astype(BF16)


def fine(form, left, right):
    (lh, ll), (rh, rl) = halves(left), halves(right)
    return form(lh, rh) + (form(ll, rh) + form(lh, rl))


def lanes_of(rows):
    return lax.broadcasted_iota(jnp.int32, (rows, LANES), 1)


def spread(values, pair):
    low = lanes_of(values.shape[0]) < HEAD_DIM
    return jnp.where(low, values[:, 2 * pair : 2 * pair + 1], values[:, 2 * pair + 1 : 2 * pair + 2])


def spread_row(row):
    return jnp.concatenate([spread(row, pair) for pair in range(PAIRS)], axis=1)


def head_sums(product, pair):
    rows = lax.broadcasted_iota(jnp.int32, (LANES, LANES), 0)
    cols = lax.broadcasted_iota(jnp.int32, (LANES, LANES), 1)
    pick = (cols == 2 * pair + (rows >= HEAD_DIM).astype(jnp.int32)).astype(BF16)
    high = product.astype(BF16)
    low = (product - high.astype(F32)).astype(BF16)
    return dot(high, pick) + dot(low, pick)


def sigmoid(v):
    return 1.0 / (1.0 + jnp.exp(-v))


def silu(v):
    return v * sigmoid(v)


def parted(j, parts):
    half = PAIRS // 2
    return parts[j // half], tile(j % half)


def tile(pair):
    return slice(pair * LANES, (pair + 1) * LANES)


def pack_row(row):
    first = row.astype(BF16).astype(F32)
    second = (row - first).astype(BF16).astype(F32)
    third = row - first - second
    place = lax.broadcasted_iota(jnp.int32, (16, row.shape[1]), 0)
    packed = jnp.where(place == 0, first, jnp.where(place == 1, second, third))
    return jnp.where(place < 3, packed, 0.0).astype(BF16)


def unpack_row(rows):
    return jnp.sum(rows.astype(F32), axis=0, keepdims=True)


def emit_msg(total, keep, msg_o):
    msg_o[0:STATE, :] = total.astype(msg_o.dtype)
    if msg_o.dtype == F32:
        msg_o[STATE:, :] = jnp.broadcast_to(keep, (msg_o.shape[0] - STATE, keep.shape[1]))
    else:
        msg_o[STATE:, :] = pack_row(keep)


def read_msg(recv):
    if recv.dtype == F32:
        return recv[0:STATE, :], recv[STATE : STATE + 1, :]
    return recv[0:STATE, :].astype(F32), unpack_row(recv[STATE:, :])


def emit_halves(total, keep, upper, own_o, msg_o):
    half = total.shape[1] // 2
    low, high = total[:, :half], total[:, half:]
    klow, khigh = keep[:, :half], keep[:, half:]
    emit_msg(jnp.where(upper, high, low), jnp.where(upper, khigh, klow), own_o)
    emit_msg(jnp.where(upper, low, high), jnp.where(upper, klow, khigh), msg_o)


def bit_of(me, flip):
    return (me[0] & flip) != 0


def state_out(width, kind=F32):
    return ((STATE + (8 if kind == F32 else 16), width), kind)


def in_order(relative, place, back):
    size = len(relative)
    ordered = []
    for step in range(size):
        member = size - 1 - step if back else step
        value = relative[0]
        for d in range(1, size):
            value = jnp.where(jnp.bitwise_xor(place, member) == d, relative[d], value)
        ordered.append(value)
    return ordered


def place_of(me, shift, size):
    return jnp.bitwise_and(lax.shift_right_logical(me[0], shift.bit_length() - 1), size - 1)


def pair_kernel(own, recv, me, first_o, mine_o, m1, m2, m3, joined, *, back):
    other, kother = read_msg(recv)
    mine, kmine = read_msg(own)
    first = jnp.logical_xor(bit_of(me, 1), not back)
    t_first, k_first = jnp.where(first, mine, other), jnp.where(first, kmine, kother)
    t_second, k_second = jnp.where(first, other, mine), jnp.where(first, kother, kmine)
    emit_msg(t_first, k_first, first_o)
    emit_msg(k_second * t_first + t_second, k_first * k_second, joined)
    place = place_of(me, 2, 4)
    width = mine_o.shape[1]
    for d, out in enumerate((mine_o, m1, m2, m3)):
        at = pl.ds(pl.multiple_of(jnp.bitwise_xor(place, d) * width, LANES), width)
        emit_msg(joined[0:STATE, at], joined[STATE : STATE + 1, at], out)


def scan_group(own, recvs, place, back):
    read = [read_msg(r) for r in (own, *recvs)]
    totals = in_order([r[0] for r in read], place, back)
    keeps = in_order([r[1] for r in read], place, back)
    prefixes, value, decay = [], jnp.zeros_like(totals[0]), jnp.ones_like(keeps[0])
    for t, k in zip(totals, keeps):
        prefixes.append((value, decay))
        value, decay = k * value + t, decay * k
    return prefixes, value, decay


def own_prefix(prefixes, place, back):
    size = len(prefixes)
    value, decay = prefixes[0]
    for step in range(1, size):
        mine = place == (size - 1 - step if back else step)
        value = jnp.where(mine, prefixes[step][0], value)
        decay = jnp.where(mine, prefixes[step][1], decay)
    return value, decay


def plane_kernel(mine, r1, r2, r3, me, pre_o, *outs, back):
    prefixes, value, decay = scan_group(mine, (r1, r2, r3), place_of(me, 2, 4), back)
    for step, (prefix, kprefix) in enumerate(prefixes):
        emit_msg(prefix, kprefix, pre_o.at[3 - step if back else step])
    for out in outs:
        emit_msg(value, decay, out)


def line_kernel(own, *refs, size, shift, back, carried, final):
    recvs, refs = refs[: size - 1], refs[size - 1 :]
    if carried:
        state, *refs = refs
    if final:
        pre, *refs = refs
    me, *outs = refs
    place = place_of(me, shift, size)
    prefixes, value, decay = scan_group(own, recvs, place, back)
    into, kinto = own_prefix(prefixes, place, back)
    if carried:
        before, kbefore = read_msg(state)
        into, kinto = kbefore * into + before, kbefore * kinto
    if not final:
        emit_msg(into, kinto, outs[0])
        for out in outs[1:]:
            emit_msg(value, decay, out)
        return
    plane = place_of(me, 2, 4)
    for d, out in enumerate(outs):
        prefix, kprefix = read_msg(pre.at[jnp.bitwise_xor(plane, d)])
        out[...] = (kprefix * into + prefix).astype(out.dtype)


def down_kernel(mine, r1, r2, r3, first, me, mine_o, msg_o, whole, *, back):
    place = place_of(me, 2, 4)
    width = mine.shape[1]
    for d, ref in enumerate((mine, r1, r2, r3)):
        at = pl.ds(pl.multiple_of(jnp.bitwise_xor(place, d) * width, LANES), width)
        whole[:, at] = ref[...].astype(F32)
    into = whole[...]
    t_first, k_first = read_msg(first)
    beyond = k_first * into + t_first
    second = jnp.logical_xor(bit_of(me, 1), back)
    mine_o[...] = jnp.where(second, beyond, into)
    msg_o[...] = jnp.where(second, into, beyond).astype(msg_o.dtype)


def join_halves(mine, recv, upper):
    theirs = recv[...].astype(F32)
    own = mine[...]
    return jnp.where(upper, theirs, own), jnp.where(upper, own, theirs)


def exchange(own, msg, me, back, deps=((), (), (), ())):
    count = lax.axis_size("seq")
    kind = msg.dtype
    width = INNER // 2
    quarter = width // 4
    part, message = state_out(quarter), state_out(quarter, kind)
    both = [message] if kind == F32 else [part, message]
    recv = swap(msg, 1)
    first, mine, *msgs = kernel_call(
        partial(pair_kernel, back=back), [state_out(width), part] + [message] * 3,
        (own, recv, me), deps=deps[0], scratch=[pltpu.VMEM(*state_out(width))],
    )
    recvs = [swap(m, 2 * (d + 1)) for d, m in enumerate(msgs)]
    pre, *totals = kernel_call(
        partial(plane_kernel, back=back), [((4, *part[0]), F32)] + both,
        (mine, *recvs, me), deps=deps[1],
    )
    carried = ()
    shift = 8
    while True:
        size = min(4, count // shift)
        recvs = [swap(totals[-1], shift * d) for d in range(1, size)]
        final = shift * size == count
        form = partial(line_kernel, size=size, shift=shift, back=back, carried=bool(carried), final=final)
        shift *= size
        if final:
            break
        state, *totals = kernel_call(form, [part] + both, (totals[0], *recvs, *carried, me))
        carried = (state,)
    mine, *msgs = kernel_call(
        form, [((STATE, quarter), F32)] + [((STATE, quarter), kind)] * 3,
        (totals[0], *recvs, *carried, pre, me), deps=deps[2],
    )
    recvs = [swap(m, 2 * (d + 1)) for d, m in enumerate(msgs)]
    mine, msg = kernel_call(
        partial(down_kernel, back=back), [((STATE, width), F32), ((STATE, width), kind)],
        (mine, *recvs, first, me), deps=deps[3], scratch=[pltpu.VMEM((STATE, width), F32)],
    )
    return mine, swap(msg, 1)


def norm_kernel(h, halo, gain, out):
    for ref, at in ((halo, slice(0, HALO)), (h, slice(HALO, HALO + h.shape[0]))):
        v = ref[...].astype(F32)
        inv = lax.rsqrt(jnp.mean(v * v, axis=-1, keepdims=True) + EPS)
        out[at, :] = (v * inv * gain[0:1, :]).astype(BF16)


def norm_back_kernel(gn, h, g, gain, wide, *refs):
    *others, out, wide_o = refs
    v = h[...].astype(F32)
    grad = gn[...]
    inv = lax.rsqrt(jnp.mean(v * v, axis=-1, keepdims=True) + EPS)
    n = v * inv
    q = grad * gain[0:1, :]
    out[...] = g[...] + inv * (q - n * jnp.mean(q * n, axis=-1, keepdims=True))
    wide_o[0:8, :] = wide[...]
    wide_o[6:7, 0 : v.shape[1]] = jnp.sum(grad * n, axis=0, keepdims=True)
    for other in others:
        wide_o[8:, :] = other[...]


def grads_kernel(gn, normed, mixed, gz, *outs, steps):
    half = INNER // 2
    several, rows = outs[0].shape[0], outs[0].shape[1] // 4
    for k, out in enumerate(outs):

        @pl.when(pl.program_id(0) // steps == k)
        def _(out=out):
            turned = lax.dot_general(gn[...], mixed[...], (((0,), (0,)), ((), ())), preferred_element_type=F32)
            out[:, 2 * rows :, :] = turned.astype(BF16).reshape(several, 2 * rows, half)
            narrow = normed[HALO:, :]
            for q in range(2):
                part = gz[:, q * half : (q + 1) * half]
                turned = lax.dot_general(narrow, part, (((0,), (0,)), ((), ())), preferred_element_type=F32)
                out[:, q * rows : (q + 1) * rows, :] = turned.astype(BF16).reshape(several, rows, half)


def grads_call(gn, normed, mixed, gz, count, parts):
    rows, half = mixed.shape
    wide = 2 * LANES
    several = wide * count // INNER
    steps = count // several // parts
    shape = (several, 4 * half // count, half)

    def share(k):
        return pl.BlockSpec(shape, lambda i: (jnp.clip(i - k * steps, 0, steps - 1), 0, 0))

    return pl.pallas_call(
        partial(grads_kernel, steps=steps),
        grid=(parts * steps,),
        out_shape=[pltpu.HBM((count // parts, *shape[1:]), BF16)] * parts,
        in_specs=[
            pl.BlockSpec((rows, wide), lambda i: (0, i)), pl.BlockSpec((HALO + rows, wide // 2), lambda i: (0, i)),
            pl.BlockSpec(mixed.shape, lambda i: (0, 0)), pl.BlockSpec(gz.shape, lambda i: (0, 0)),
        ],
        out_specs=[share(k) for k in range(parts)],
        compiler_params=pltpu.CompilerParams(vmem_limit_bytes=14 * MB),
        cost_estimate=pl.CostEstimate(flops=8 * rows * half * half, bytes_accessed=10 * MB, transcendentals=0),
    )(gn, normed, mixed, gz)


def own_rows_kernel(gp, spilled, gz, out, gz_o):
    gz_o[...] = gz[...]
    end = out.shape[0] - HALO
    out[0:end, :] = gp[HALO : HALO + end, :]
    out[end:, :] = (gp[HALO + end :, :].astype(F32) + spilled[...].astype(F32)).astype(BF16)


def triangle(rows, lower):
    r = lax.broadcasted_iota(jnp.int32, (rows, rows), 0)
    c = lax.broadcasted_iota(jnp.int32, (rows, rows), 1)
    return r >= c if lower else r <= c


def conv_state_kernel(pc, cw, hp, mk, me, left_o, right_o, bc_o, dt_o, log_o, own_o, msg_o, xw, *low, precise):
    rows = mk.shape[0]
    marks = mk[...]
    raw = pc[HALO:, CONV_CH:WIDE].astype(F32) + hp[0:1, :]
    soft = jnp.maximum(raw, 0.0) + jnp.log1p(jnp.exp(-jnp.abs(raw)))
    dt = jnp.where(lanes_of(rows) < HEADS, soft, 0.0)
    log = dot(triangle(rows, True).astype(F32), dt * hp[1:2, :], EXACT)
    last = log[rows - 1 : rows, :]
    weight = marks[:, 4:5] * jnp.exp(last - log) * dt
    dt_o[...] = dt
    log_o[...] = log
    b_cols = None
    for j in range(CONV_CH // LANES):
        ext = pc[:, tile(j)].astype(F32)
        out = cw[4:5, tile(j)] + cw[3:4, tile(j)] * ext[HALO:, :]
        for k in range(CONV_K - 1):
            out = out + cw[k : k + 1, tile(j)] * ext[LEAD + k : LEAD + k + rows, :] * marks[:, k : k + 1]
        part, at = parted(j, (left_o, right_o, bc_o))
        part[:, at] = out
        if j < PAIRS:
            high, rest = halves(silu(out) * spread(weight, j))
            xw[:, tile(j)] = high
            if precise:
                low[0][:, tile(j)] = rest
        elif j == PAIRS:
            b_cols, b_rest = halves(silu(out).T)
    total = dot(b_cols, xw[...])
    if precise:
        total = total + (dot(b_rest, xw[...]) + dot(b_cols, low[0][...]))
    keep = spread_row(jnp.exp(last) * marks[rows - 1 : rows, 3:4])
    emit_halves(total, keep, bit_of(me, 1), own_o, msg_o)


def mask_bias(mk, sr, rows):
    same = mk[:, 5:6] == sr[0:1, :]
    return jnp.where(jnp.logical_and(triangle(rows, True), same), 0.0, FAR)


def within_kernel(conv, bc, dt, log, hp, mk, sr, y_o, xdt, lcol, lrow, *lower, precise, first):
    rows = mk.shape[0]
    pairs = PAIRS // 2
    scores = fine(dot_t, silu(bc[:, tile(1)]), silu(bc[:, tile(0)]))
    bias = mask_bias(mk, sr, rows)
    dtv, logv = dt[...], log[...]
    lrow[...] = logv.T
    for j in range(pairs):
        x = silu(conv[:, tile(j)])
        high, rest = halves(x * spread(dtv, first + j))
        xdt[:, tile(j)] = high
        if precise:
            lower[0][:, tile(j)] = rest
        y_o[:, tile(j)] = x * spread(hp[2:3, :], first + j)
    for h in range(2 * pairs):
        lcol[h] = jnp.broadcast_to(logv[:, 2 * first + h : 2 * first + h + 1], (rows, LANES))
    low = lanes_of(rows) < HEAD_DIM

    def pair(j, _):
        at = pl.ds(pl.multiple_of(j * LANES, LANES), LANES)
        xp = xdt[:, at]
        res = []
        for q in range(2):
            col = lcol[2 * j + q]
            row = lrow[pl.ds(2 * (first + j) + q, 1), :]
            span = jnp.concatenate([col] * (rows // LANES), axis=1) - row
            mix = scores * jnp.exp(span + bias)
            if precise:
                high, rest = halves(mix)
                res.append(dot(high, xp) + (dot(rest, xp) + dot(high, lower[0][:, at])))
            else:
                res.append(dot(mix.astype(BF16), xp))
        y_o[:, at] += jnp.where(low, res[0], res[1])
        return 0

    lax.fori_loop(0, pairs, pair, 0)


def post_kernel(*refs, places, relative, spans, aligned):
    if spans:
        pack, *refs = refs
        *refs, gated, zbuf, obuf, sems = refs
        parts = len(spans) - 1
        refs, raw = [*refs[:-parts], gated], refs[-parts:]
    else:
        z_low, z_high, out_w, *refs = refs
    normed, h, yw, yw2, mine, recv, bc, log, mk, gg, me, z, y_o, gn_o, st_o, st2_o, h_o, *rel_o, gated = refs
    rows = mk.shape[0]
    wide = 2 * LANES
    half = INNER // 2
    own = normed[HALO:, :]
    flying = []

    def moved(source, target):
        copy = pltpu.make_async_copy(source, target, sems.at[len(flying)])
        flying.append(copy)
        copy.start()
        return copy

    def apart(buffer, base, k):
        return moved(buffer.at[:, spans[k] - base : spans[k + 1] - base, :], raw[k])

    if spans:
        coming = [moved(pack.at[:, spans[0] : spans[2], :], zbuf), moved(pack.at[:, spans[2] : spans[3], :], obuf)]
        coming[0].wait()
        leaving = [apart(zbuf, 0, 0), apart(zbuf, 0, 1)]

    def project(i, _):
        for q in range(2):
            at = pl.ds(pl.multiple_of(i * wide, wide), wide)
            if spans:
                part = zbuf[:, spans[q] : spans[q + 1], at]
                part = part.reshape(-1, part.shape[-1])
            else:
                part = (z_low, z_high)[q][:, at]
            z[:, pl.ds(pl.multiple_of(q * half + i * wide, wide), wide)] = dot(own, part).astype(BF16)
        return 0

    lax.fori_loop(0, half // wide, project, 0)
    if spans:
        for copy in leaving:
            copy.wait()
        more = len(spans) > 4
        if more:
            second = moved(pack.at[:, spans[3] : spans[5], :], zbuf)
        coming[1].wait()
        leaving = [apart(obuf, spans[2], 2)]
    low, high = join_halves(mine, recv, bit_of(me, 1))
    st_o[...] = low.astype(BF16)
    st2_o[...] = high.astype(BF16)
    c = silu(bc[:, tile(1)])
    inflow = jnp.exp(log[...]) * mk[:, 3:4]
    total = jnp.zeros((rows, LANES), F32)
    for j in range(PAIRS):
        part = (yw if j < PAIRS // 2 else yw2)[:, tile(j % (PAIRS // 2))]
        state = (low if j < PAIRS // 2 else high)[:, tile(j % (PAIRS // 2))]
        y = part + fine(dot, c, state) * spread(inflow, j)
        y_o[:, tile(j)] = y
        v = y * silu(z[:, tile(j)].astype(F32))
        gated[:, tile(j)] = v
        total = total + v * v
    inv = lax.rsqrt(jnp.sum(total, axis=-1, keepdims=True) / INNER + EPS)
    for j in range(PAIRS):
        gn_o[:, tile(j)] = (gated[:, tile(j)] * inv * gg[0:1, tile(j)]).astype(BF16)

    if spans and more:
        second.wait()
        leaving += [apart(zbuf, spans[3], 3), apart(zbuf, spans[3], 4)]

    def output(i, _):
        at = pl.ds(pl.multiple_of(i * wide, wide), wide)
        if spans:
            part = obuf[:, :, at]
            part = part.reshape(-1, part.shape[-1])
        else:
            part = out_w[:, at]
        h_o[:, at] = h[:, at].astype(F32) + dot(gn_o[...], part)
        return 0

    lax.fori_loop(0, h.shape[1] // wide, output, 0)
    if spans and more:
        leaving[0].wait()
        last = obuf.at[:, : spans[6] - spans[5], :]
        moved(pack.at[:, spans[5] : spans[6], :], last).wait()
        leaving = leaving[1:] + [moved(last, raw[5])]
    if rel_o:
        lower = lanes_of(rows) < HEAD_DIM
        for j in range(PAIRS):
            base = me[0] if relative else jnp.int32(0)
            sources = [jnp.bitwise_xor(base, jnp.int32(int(places[2 * j + q]))) for q in range(2)]
            upper = jnp.bitwise_and(sources[0], 1) == 1
            tiles = []
            for src in sources:
                at = pl.multiple_of(lax.shift_right_logical(src, 1) * LANES, LANES)
                tiles.append(gn_o[:, pl.ds(at, LANES)].astype(F32))
            left = jnp.where(upper, pltpu.roll(tiles[0], HEAD_DIM, 1), tiles[0])
            right = jnp.where(upper, tiles[1], pltpu.roll(tiles[1], HEAD_DIM, 1))
            rel_o[0][:, tile(j)] = jnp.where(lower, left, right).astype(BF16)
    if spans:
        for copy in leaving:
            copy.wait()


def post_back_kernel(ggn, y, z, gg, left, right, bc, log, mk, me, gy_o, gy2_o, gz_o, gate_o, skip_o, own_o, msg_o, ge):
    rows = mk.shape[0]
    logv = log[...]
    inflow = jnp.exp(logv) * mk[:, 3:4]
    total = jnp.zeros((rows, LANES), F32)
    cross = jnp.zeros((rows, LANES), F32)
    for j in range(PAIRS):
        v = y[:, tile(j)] * silu(z[:, tile(j)].astype(F32))
        total = total + v * v
        cross = cross + v * ggn[:, tile(j)] * gg[0:1, tile(j)]
    inv = lax.rsqrt(jnp.sum(total, axis=-1, keepdims=True) / INNER + EPS)
    mean = jnp.sum(cross, axis=-1, keepdims=True) * inv / INNER
    skips = jnp.zeros((8, LANES), F32)
    for j in range(PAIRS):
        zf = z[:, tile(j)].astype(F32)
        s = sigmoid(zf)
        sz = zf * s
        yv = y[:, tile(j)]
        n = yv * sz * inv
        up = ggn[:, tile(j)]
        gga = inv * (up * gg[0:1, tile(j)] - n * mean)
        gy = gga * sz
        gz_o[:, tile(j)] = (gga * yv * (s * (1.0 + zf * (1.0 - s)))).astype(BF16)
        part, at = parted(j, (gy_o, gy2_o))
        part[:, at] = gy.astype(BF16)
        ge[:, tile(j)] = (gy * spread(inflow, j)).astype(BF16)
        gate_o[:, tile(j)] = jnp.broadcast_to(jnp.sum(up * n, axis=0, keepdims=True), (8, LANES))
        part, at = parted(j, (left, right))
        through = jnp.sum(gy * silu(part[:, at]), axis=0, keepdims=True)
        skips = skips + head_sums(jnp.broadcast_to(through, (8, LANES)), j)
    skip_o[...] = skips
    c_cols = silu(bc[:, tile(1)]).T.astype(BF16)
    state = dot(c_cols, ge[...])
    keep = spread_row(jnp.exp(logv[rows - 1 : rows, :]) * mk[rows - 1 : rows, 3:4])
    emit_halves(state, keep, bit_of(me, 1), own_o, msg_o)


def within_back_kernel(
    conv, bc, dt, log, gy, st, mk, sr, gxdt_o, gb_o, gc_o, gl_o, xdt, ge, lcol, lrow, gscore, lsum, csum, *, first
):
    rows = mk.shape[0]
    pairs = PAIRS // 2
    bf, cf = silu(bc[:, tile(0)]), silu(bc[:, tile(1)])
    b, c = bf.astype(BF16), cf.astype(BF16)
    scores = fine(dot_t, bf, cf)
    same = mk[:, 5:6] == sr[0:1, :]
    bias = jnp.where(jnp.logical_and(triangle(rows, False), same), 0.0, FAR)
    dtv, logv = dt[...], log[...]
    lrow[...] = logv.T
    inflow = jnp.exp(logv) * mk[:, 3:4]
    flow = jnp.zeros((rows, LANES), F32)
    for j in range(pairs):
        xdt[:, tile(j)] = (silu(conv[:, tile(j)]) * spread(dtv, first + j)).astype(BF16)
        gyv = gy[:, tile(j)].astype(F32) * spread(inflow, first + j)
        ge[:, tile(j)] = gyv.astype(BF16)
        flow = flow + head_sums(gyv * dot(c, st[:, tile(j)]), first + j)
    for h in range(2 * pairs):
        lcol[h] = jnp.broadcast_to(logv[:, 2 * first + h : 2 * first + h + 1], (rows, LANES))
    lanes = lanes_of(rows)
    low = lanes < HEAD_DIM
    gscore[...] = jnp.zeros_like(gscore)
    csum[...] = jnp.zeros_like(csum)
    lsum[...] = jnp.zeros_like(lsum)

    def pair(j, _):
        at = pl.ds(pl.multiple_of(j * LANES, LANES), LANES)
        xp, gp = xdt[:, at], gy[:, at]
        res = []
        for q in range(2):
            h = 2 * (first + j) + q
            span = lrow[pl.ds(h, 1), :] - jnp.concatenate([lcol[2 * j + q]] * (rows // LANES), axis=1)
            decay = jnp.exp(span + bias)
            mix = scores * decay
            own = jnp.where(low if q == 0 else jnp.logical_not(low), gp, jnp.zeros_like(gp))
            gmix = dot_t(xp, own)
            gscore[...] += gmix * decay
            term = gmix * mix
            lsum[pl.ds(h, 1), :] = jnp.sum(term, axis=0, keepdims=True)
            csum[...] += jnp.where(lanes == h, jnp.sum(term, axis=1, keepdims=True), 0.0)
            res.append(dot(mix.astype(BF16), gp))
        gxdt_o[:, at] = jnp.where(low, res[0], res[1])
        return 0

    lax.fori_loop(0, pairs, pair, 0)
    gs = gscore[...]
    gb_o[...] = dot(gs.astype(BF16), c)
    gc_o[...] = dot(gs.T.astype(BF16), b) + dot_t(ge[...], st[...])
    gl_o[...] = lsum[...].T - csum[...] + flow


def mixer_back_kernel(
    gxdt2, gy2, right, pc, cw, gxdt, gbi, gci, gli, gbi2, gci2, gli2, mine, recv, gy, left, bc, dt, log, st, st2,
    hp, mk, gate, skip, me, gp_o, wide_o, gb16, xe, acc,
):
    rows = mk.shape[0]
    marks = mk[...]
    low, high = join_halves(mine, recv, bit_of(me, 1))
    half = INNER // 2
    kg = jnp.zeros((8, LANES), F32)
    for part, value in ((0, low), (half, high)):
        gb16[:, part : part + half] = value.astype(BF16)
        rowsum = jnp.sum(value * (st if part == 0 else st2)[...].astype(F32), axis=0, keepdims=True)
        for j in range(PAIRS // 2):
            pair = part // LANES + j
            kg = kg + head_sums(jnp.broadcast_to(rowsum[:, tile(j)], (8, LANES)), pair)
    dtv, logv = dt[...], log[...]
    last = logv[rows - 1 : rows, :]
    b = silu(bc[:, tile(0)]).astype(BF16)
    outflow = marks[:, 4:5] * jnp.exp(last - logv)
    gv = jnp.zeros((rows, LANES), F32)
    gd = jnp.zeros((rows, LANES), F32)

    def conv_back(j, gact, s, out):
        gco = gact * (s * (1.0 + out * (1.0 - s)))
        ext = pc[:, tile(j)].astype(F32)
        acc[...] = jnp.zeros_like(acc)
        for k in range(CONV_K):
            gk = gco if k == CONV_K - 1 else gco * marks[:, k : k + 1]
            wide_o[k : k + 1, tile(j)] = jnp.sum(gk * ext[LEAD + k : LEAD + k + rows, :], axis=0, keepdims=True)
            acc[LEAD + k : LEAD + k + rows, :] += gk * cw[k : k + 1, tile(j)]
        wide_o[4:5, tile(j)] = jnp.sum(gco, axis=0, keepdims=True)
        gp_o[:, tile(j)] = acc[...].astype(BF16)

    wide_o[6:8, :] = jnp.zeros((2, CONV_CH), F32)
    for j in range(PAIRS):
        part, at = parted(j, (left, right))
        out = part[:, at]
        s = sigmoid(out)
        x = out * s
        dtp = spread(dtv, j)
        flow = spread(outflow, j)
        xd = x * dtp
        gxs = dot(b, gb16[:, tile(j)]) * flow
        xe[:, tile(j)] = (xd * flow).astype(BF16)
        gxd = (gxdt if j < PAIRS // 2 else gxdt2)[:, at] + gxs
        gv = gv + head_sums(xd * gxs, j)
        gd = gd + head_sums(x * gxd, j)
        conv_back(j, dtp * gxd + spread(hp[2:3, :], j) * (gy if j < PAIRS // 2 else gy2)[:, at].astype(F32), s, out)
    gb = gbi[...] + gbi2[...] + dot_t(xe[...], gb16[...])
    for j, grad in ((PAIRS, gb), (PAIRS + 1, gci[...] + gci2[...])):
        out = bc[:, tile(j - PAIRS)]
        conv_back(j, grad, sigmoid(out), out)
    keep = jnp.exp(last) * marks[rows - 1 : rows, 3:4]
    edge = jnp.sum(gv, axis=0, keepdims=True) + kg[0:1, :] * keep
    place = lax.broadcasted_iota(jnp.int32, (rows, LANES), 0)
    gl = gli[...] + gli2[...] - gv + jnp.where(place == rows - 1, edge, 0.0)
    ga = dot(triangle(rows, False).astype(F32), gl, EXACT)
    rate = hp[1:2, :]
    raw = pc[HALO:, CONV_CH:WIDE].astype(F32) + hp[0:1, :]
    graw = jnp.where(lanes_of(rows) < HEADS, (ga * rate + gd) * sigmoid(raw), 0.0)
    gp_o[0:HALO, CONV_CH:WIDE] = jnp.zeros((HALO, LANES), BF16)
    gp_o[HALO:, CONV_CH:WIDE] = graw.astype(BF16)
    wide_o[5:6, 0:INNER] = gate[0:1, :]
    place = lanes_of(1)
    heads = jnp.where(place < HEADS, jnp.sum(graw, axis=0, keepdims=True), 0.0)
    for k, row in enumerate((rate * jnp.sum(ga * dtv, axis=0, keepdims=True), skip[0:1, :])):
        heads = heads + jnp.where(place // HEADS == k + 1, pltpu.roll(row, HEADS * (k + 1), 1), 0.0)
    wide_o[5:6, INNER : INNER + LANES] = heads
    wide_o[5:6, INNER + LANES :] = jnp.zeros((1, CONV_CH - INNER - LANES), F32)


def row_of(values, rows=8):
    pad = [(0, rows - values.shape[0]), (0, max(0, LANES - values.shape[1]))]
    return jnp.pad(values.astype(F32), pad)


def per_device(
    hidden, segment_ids, in_weight, out_weight, conv_weight, conv_bias, norm_gain, gate_gain,
    dt_bias, a_log, skip_param, cotangent,
):
    layers_n, in_rows = in_weight.shape[:2]
    out_rows = out_weight.shape[1]
    rows, width = hidden.shape
    count = lax.axis_size("seq")
    me = lax.axis_index("seq")
    me_ref = me.reshape(1).astype(jnp.int32)
    conv_n = conv_bias.shape[1]
    half = INNER // 2
    plane_n = axes_of(count)["z"][1]

    small = jnp.concatenate(
        [conv_weight.reshape(-1), conv_bias.reshape(-1), norm_gain.reshape(-1), gate_gain.reshape(-1)]
    )
    length = small.shape[0]
    small_rows = -(-length // (16 * LANES)) * 16
    small = jnp.pad(small, (0, small_rows * LANES - length)).reshape(small_rows, LANES)
    in_weight_side = jnp.pad(in_weight[0, :, INNER:], ((0, 0), (0, WIDE - SIDE)))
    halo = shifted(hidden[rows - HALO :], 1)
    seg_halo = shifted(segment_ids[rows - HALO :] + 1, 1) - 1
    packs = []
    for layer in range(layers_n):
        parts = [in_weight[layer, :, :half], in_weight[layer, :, half:INNER], out_weight[layer]]
        if layer + 1 < layers_n:
            later = in_weight[layer + 1, :, INNER:]
            parts += [later[:, :half], later[:, half : 2 * half]]
            parts.append(jnp.pad(later[:, 2 * half :], ((0, 0), (0, 3 * half - SIDE))))
        packs.append((jnp.concatenate(parts, axis=0), np.cumsum([0] + [p.shape[0] for p in parts]).tolist()))
    first = Gather(in_weight_side)
    started = first.line(tuple(pack for pack, _ in packs[1:]))
    gathered = [lax.all_gather(after(pack, started) if layer else pack, "seq") for layer, (pack, _) in enumerate(packs)]
    crossed = first.plane()
    smalls = gather_small(small, [(), (), (started,), (started,), (crossed,)])

    seg_pad = jnp.concatenate([seg_halo[LEAD:], segment_ids])
    before = seg_pad[CONV_K - 2]
    columns = [seg_pad[k : k + rows] == segment_ids for k in range(CONV_K - 1)]
    columns += [segment_ids == before, segment_ids == segment_ids[-1], segment_ids]
    marks = jnp.pad(jnp.stack([col.astype(F32) for col in columns], axis=1), ((0, 0), (0, LANES - 6)))
    seg_row = jnp.broadcast_to(segment_ids.astype(F32)[None, :], (8, rows))

    relative, planes = relative_places(count), plane_first(count)
    order = column_order(relative, me, in_rows)
    plane_order = column_order(planes, 0, in_rows)

    place = (jnp.arange(count)[:, None] == (jnp.arange(count) ^ me)[None, :]).astype(BF16)
    smalls = dot(place, smalls.reshape(count, small_rows * LANES))
    sizes = [layers_n * CONV_K * conv_n, layers_n * conv_n, layers_n * in_rows, layers_n * out_rows]
    cuts = np.cumsum([0] + sizes)
    taps, biases, gains, gate_gains = (smalls[:, cuts[i] : cuts[i + 1]] for i in range(4))
    taps = taps.reshape(count, layers_n, CONV_K, conv_n).transpose(1, 2, 0, 3).reshape(layers_n, CONV_K, CONV_CH)
    biases = biases.reshape(count, layers_n, 1, conv_n).transpose(1, 2, 0, 3).reshape(layers_n, 1, CONV_CH)
    conv_rows = jnp.pad(jnp.concatenate([taps, biases], axis=1), ((0, 0), (0, 3), (0, 0)))
    gains = gains.reshape(count, layers_n, in_rows).transpose(1, 0, 2).reshape(layers_n, 1, width)
    gate_gains = gate_gains.reshape(count, layers_n, out_rows).transpose(1, 0, 2).reshape(layers_n, 1, INNER)
    gains = [jnp.broadcast_to(gains[layer], (8, width)) for layer in range(layers_n)]
    gate_gains = [jnp.broadcast_to(gate_gains[layer], (8, INNER)) for layer in range(layers_n)]
    conv_rows = [conv_rows[layer] for layer in range(layers_n)]
    heads = [
        row_of(jnp.stack([dt_bias[layer], -jnp.exp(a_log[layer]), skip_param[layer]])) for layer in range(layers_n)
    ]

    (left, left2), (right, right2) = first.whole((*conv_rows, *gains, *gate_gains, *heads, marks, seg_row, halo, order))

    scratch_wide = pltpu.VMEM((rows, INNER), BF16)
    scratch_half = pltpu.VMEM((rows, INNER // 2), BF16)
    scratch_cols = pltpu.VMEM((HEADS // 2, rows, LANES), F32)
    scratch_rows = pltpu.VMEM((LANES, rows), F32)

    residual = hidden
    saved, sides = [], ()
    for layer in range(layers_n):
        precise = layer + 1 < layers_n
        gain, gate = gains[layer], gate_gains[layer]
        (normed,) = kernel_call(norm_kernel, [((HALO + rows, width), BF16)], (residual, halo, gain))
        normed_rel = dot(normed, order).astype(BF16)
        if layer == 0:
            lower, upper = normed_rel[:, : width // 2], normed_rel[:, width // 2 :]
            parts = [dot(lower, left) + dot(upper, left2), dot(lower, right) + dot(upper, right2)]
        else:
            parts = [dot(normed, part) for part in side_parts[:2]]
            parts.append(dot(normed, side_parts[2][:, : WIDE - 2 * half]))
        pc = jnp.concatenate([part.astype(BF16) for part in parts], axis=1)
        hp = heads[layer]
        conv_l, conv_r, bc, dt, log, own, msg = kernel_call(
            partial(conv_state_kernel, precise=precise),
            [((rows, half), F32)] * 2 + [((rows, 2 * STATE), F32)] + [((rows, LANES), F32)] * 2
            + [state_out(half)] * 2,
            (pc, conv_rows[layer], hp, marks, me_ref),
            scratch=[scratch_wide] * (2 if precise else 1), flops=2 * rows * STATE * INNER * 8,
        )
        yw = [
            kernel_call(
                partial(within_kernel, precise=precise, first=part * PAIRS // 2), [((rows, half), F32)],
                ((conv_l, conv_r)[part], bc, dt, log, hp, marks, seg_row),
                scratch=[scratch_half, scratch_cols, scratch_rows] + [scratch_half] * precise,
                flops=2 * rows * rows * half * 16, deps=(own,),
            )[0]
            for part in range(2)
        ]
        mine, recv = exchange(own, msg, me_ref, False, [(), (yw[0],), (yw[1],), ()])
        aligned = out_rows == HEAD_DIM
        pack, spans = gathered[layer], packs[layer][1]
        weights = [pack[:, a:b].reshape(-1, width) for a, b in zip(spans, spans[1:])]
        outs = [((rows, INNER), BF16), ((rows, INNER), F32), ((rows, INNER), BF16)] + [((STATE, half), BF16)] * 2
        outs += [((rows, width), F32)] + [((rows, INNER), BF16)] * aligned
        form = partial(post_kernel, places=planes, relative=False)
        args = (normed, residual, *yw, mine, recv, bc, log, marks, gate, me_ref)
        scratch = [pltpu.VMEM((rows, INNER), F32)]
        flops = 2 * rows * width * INNER * 2
        if in_rows % HALO:
            z, y, gnormed, state, state2, after_h, *gn_rel = kernel_call(
                partial(form, spans=(), aligned=aligned), outs, (*weights[:3], *args), scratch=scratch, flops=flops
            )
        else:
            z, y, gnormed, state, state2, after_h, *rest = streamed_call(
                partial(form, spans=spans, aligned=aligned), outs, args, flops=flops, streamed=pack,
                scratch=scratch + [pltpu.VMEM((count, 2 * in_rows, width), BF16)] * 2,
                raw=[((count, b - a, width), BF16) for a, b in zip(spans, spans[1:])],
            )
            gn_rel = rest[:aligned]
            weights = [part.reshape(-1, width) for part in rest[aligned:]]
        weights, side_parts = weights[:3], weights[3:]
        if not aligned:
            gn_rel = [dot(gnormed, column_order(planes, 0, out_rows)).astype(BF16)]
        saved.append((residual, normed, normed_rel, pc, conv_l, conv_r, bc, dt, log, hp, z, y, gn_rel[0], state, state2, weights, sides))
        sides = side_parts
        residual = after_h
        if layer + 1 < layers_n:
            halo = shifted(residual[rows - HALO :], 1)

    grad = cotangent
    pack_sums, pack_terms, side_shares = ([None] * layers_n for _ in range(3))
    for layer in range(layers_n - 1, -1, -1):
        h, normed, normed_rel, pc, conv_l, conv_r, bc, dt, log, hp, z, y, gn_rel, state, state2, weights, sides = saved[layer]
        z_low, z_high, out_w = weights
        gain, gate = gains[layer], gate_gains[layer]
        mixed = grad.astype(BF16)
        gy, gy2, gz, gate_grad, skip_grad, own, msg = kernel_call(
            post_back_kernel,
            [((rows, half), BF16)] * 2 + [((rows, INNER), BF16), ((8, INNER), F32), ((8, LANES), F32)]
            + [state_out(half), state_out(half, BF16)],
            (dot_t(mixed, out_w), y, z, gate, conv_l, conv_r, bc, log, marks, me_ref),
            scratch=[scratch_wide], flops=2 * rows * STATE * INNER * 8,
        )
        halves_back = [
            kernel_call(
                partial(within_back_kernel, first=part * PAIRS // 2),
                [((rows, half), F32), ((rows, LANES), F32), ((rows, LANES), F32), ((rows, LANES), F32)],
                ((conv_l, conv_r)[part], bc, dt, log, (gy, gy2)[part], (state, state2)[part], marks, seg_row),
                scratch=[
                    scratch_half, scratch_half, scratch_cols, scratch_rows,
                    pltpu.VMEM((rows, rows), F32), scratch_rows, pltpu.VMEM((rows, LANES), F32),
                ],
                flops=2 * rows * rows * half * 32,
            )
            for part in range(2)
        ]
        normed_planes = dot(normed, plane_order).astype(BF16)
        (term,) = grads_call(gn_rel, normed_planes, mixed, gz, count, 1)
        pack_sums[layer] = scatter_planes(term.reshape(-1, width))
        pack_terms[layer] = line_terms(pack_sums[layer])
        deps = [(), (far(term),), (halves_back[0][0],), (halves_back[1][0],)]
        late = ()
        if layer + 1 < layers_n:
            deps[0] += (far(pack_sums[layer + 1]),)
            late = tuple(far(part) for part in side_shares[layer + 1].terms[1:3])
        mine, recv = exchange(own, msg, me_ref, True, deps)

        (gx, *sums), (gx2, *sums2) = halves_back
        gp, wide = kernel_call(
            mixer_back_kernel,
            [((HALO + rows, WIDE), BF16), ((8, CONV_CH), F32)],
            (
                gx2, gy2, conv_r, pc, conv_rows[layer], gx, *sums, *sums2, mine, recv, gy, conv_l, bc, dt, log,
                state, state2, hp, marks, gate_grad, skip_grad, me_ref,
            ),
            scratch=[pltpu.VMEM((STATE, INNER), BF16), scratch_wide, pltpu.VMEM((HALO + rows, LANES), F32)],
            flops=2 * rows * STATE * INNER * 24, deps=late,
        )
        spilled = shifted(gp[:HALO], -1)
        side_shares[layer] = share_terms(normed_rel, gp)
        both = (side_shares[layer].terms[0], side_shares[layer].send)
        if layer:
            pieces = tuple(side_shares[layer].step())
        else:
            pieces = tuple(side_shares[layer].step())
        gp_own, gz = kernel_call(
            own_rows_kernel, [((rows, WIDE), BF16), ((rows, INNER), BF16)], (gp, spilled, gz),
            deps=both if layer else (far(pieces[0]), *[far(t) for above in pack_terms[1:] for t in above[1:]]),
        )
        if not layer:
            for share in side_shares[1:]:
                share.step(behind=gp_own)
        gn_z = dot_t(gz[:, :half], z_low) + dot_t(gz[:, half:], z_high)
        if layer:
            gn = gn_z
            for k, part in enumerate(sides):
                piece = gp_own[:, k * half : min((k + 1) * half, WIDE)]
                gn = gn + dot_t(piece, part[:, : piece.shape[1]])
        else:
            gp_left, gp_right = gp_own[:, :CUT], gp_own[:, CUT:]
            gn_side = jnp.concatenate(
                [dot_t(gp_left, left) + dot_t(gp_right, right), dot_t(gp_left, left2) + dot_t(gp_right, right2)],
                axis=1,
            )
            gn_high, gn_low = halves(gn_side)
            gn = gn_z + dot_t(gn_high, order) + dot_t(gn_low, order)
        grad, small_grads = kernel_call(
            norm_back_kernel, [((rows, width), F32), ((8 * (layers_n - layer), CONV_CH), F32)],
            (gn, h, grad, gain, wide) + ((small_grads,) if layer + 1 < layers_n else ()),
            deps=tuple(
                far(part)
                for part in (pieces if layer else (pack_sums[0], *[t for v in side_shares[1:] for t in v.terms[1:]]))
            ),
        )
    (sums,) = kernel_call(round_kernel, [(small_grads.shape, BF16)], (small_grads,))
    sums = sum_rounds(sums, count // 2, plane_n)
    pieces = side_shares[0].step()
    late = [(far(part),) for part in side_shares[0].terms[1:]]
    late[0] += tuple(far(part) for part in pack_terms[0][1:])
    sums = sum_rounds(sums, plane_n // 2, 1, late)
    in_grads, out_grads = [], []
    for layer in range(layers_n):
        pack, side = (
            sum((t.astype(F32) for t in terms[1:]), terms[0].astype(F32))
            for terms in (pack_terms[layer], side_shares[layer].terms)
        )
        if layer == 0:
            pack = pack + held_back(pieces[1])
        in_grads.append(jnp.concatenate([pack[:in_rows], pack[in_rows : 2 * in_rows], side[:, :SIDE]], axis=1))
        out_grads.append(pack[2 * in_rows :])
    in_grads, out_grads = jnp.stack(in_grads), jnp.stack(out_grads)
    sums = sums.reshape(layers_n, 8, CONV_CH)

    def share(values):
        span = values.shape[-1] // count
        return lax.dynamic_slice_in_dim(values, me * span, span, values.ndim - 1)

    heads = sums[:, 5, INNER : INNER + 3 * HEADS]
    return (
        residual, grad, in_grads, out_grads,
        share(sums[:, :CONV_K]), share(sums[:, CONV_K]), share(sums[:, 6, :width]), share(sums[:, 5, :INNER]),
        heads[:, :HEADS], heads[:, HEADS : 2 * HEADS], heads[:, 2 * HEADS :],
    )


def solution(mesh):
    return jax.shard_map(
        per_device,
        mesh=mesh,
        in_specs=(
            P("seq", None), P("seq"), P(None, "seq", None), P(None, "seq", None), P(None, None, "seq"),
            P(None, "seq"), P(None, "seq"), P(None, "seq"), P(), P(), P(), P("seq", None),
        ),
        out_specs=(
            P("seq", None), P("seq", None), P(None, "seq", None), P(None, "seq", None), P(None, None, "seq"),
            P(None, "seq"), P(None, "seq"), P(None, "seq"), P(), P(), P(),
        ),
        check_vma=False,
    )
```

```python
from functools import partial

import jax
import jax.numpy as jnp
import numpy as np
from jax import lax
from jax.experimental import pallas as pl
from jax.experimental.pallas import tpu as pltpu
from jax.sharding import PartitionSpec as P

HEADS = 32
HEAD_DIM = 64
STATE = 128
CONV_K = 4
INNER = 2048
CONV_CH = 2304
SIDE = CONV_CH + HEADS
WIDE = 2432
CUT = 1280
LANES = 128
PAIRS = HEADS // 2
HALO = 16
LEAD = HALO - (CONV_K - 1)
FAR = -1e30

EPS = 1e-05
F32 = jnp.float32
BF16 = jnp.bfloat16
EXACT = lax.Precision.HIGHEST
MB = 1024 * 1024
CAP = 16 * MB


def axes_of(count):
    side = 4 if count >= 128 else 2
    plane = 2 * side * side
    return {"c": (2, 1), "x": (side, 2), "y": (side, 2 * side), "z": (count // plane, plane)}


def swap(value, flip):
    count = lax.axis_size("seq")
    return lax.ppermute(value, "seq", [(i, i ^ flip) for i in range(count)])


def shifted(shard, by):
    count = lax.axis_size("seq")
    return lax.ppermute(shard, "seq", [(i, i + by) for i in range(count) if 0 <= i + by < count])


def relative_places(count):
    axes = axes_of(count)
    places = np.zeros((1,), np.int32)
    for name in ("c", "y", "x", "z"):
        size, shift = axes[name]
        places = (places[:, None] + np.arange(size, dtype=np.int32)[None, :] * shift).reshape(-1)
    return places


def column_order(places, me, block):
    count = len(places)
    places = jnp.asarray(np.repeat(places, block))
    inner = jnp.asarray(np.tile(np.arange(block, dtype=np.int32), count))
    source = (places ^ me) * block + inner
    return (jnp.arange(count * block)[:, None] == source[None, :]).astype(BF16)


class Gather:

    def __init__(self, shard):
        self.axes = axes_of(lax.axis_size("seq"))
        self.rows = shard.shape[0]
        self.kind = shard.dtype
        self.shard, self.sent = shard, self.send(shard, "z")

    def send(self, value, name):
        size, shift = self.axes[name]
        return [swap(value, d * shift) for d in range(1, size)]

    def outs(self, *lead):
        return [((*lead, self.rows, CUT), self.kind), ((*lead, self.rows, WIDE - CUT), self.kind)]

    def line(self, deps=()):
        everything = slice(None)
        cuts = ((everything, slice(0, CUT)), (everything, slice(CUT, WIDE)))
        pieces = [
            (value, side, cuts[side], d) for side in range(2) for d, value in enumerate([self.shard, *self.sent])
        ]
        self.left, self.right = copies_call(pieces, self.outs(self.axes["z"][0]), deps)
        self.sent = self.send(self.left, "x"), self.send(self.right, "y")
        return self.left

    def plane(self, deps=()):
        sides = ((self.left, *self.sent[0]), (self.right, *self.sent[1]))
        pieces = [(value, side, None, d) for side in range(2) for d, value in enumerate(sides[side])]
        line, across, up = (self.axes[name][0] for name in ("z", "x", "y"))
        outs = [self.outs(across, line)[0], self.outs(up, line)[1]]
        self.left, self.right = copies_call(pieces, outs, deps)
        self.sent = self.send(self.left, "y"), self.send(self.right, "x")
        return self.left

    def whole(self, deps=()):
        line, across, up = (self.axes[name][0] for name in ("z", "x", "y"))
        pieces = [(value, 0, None, d) for d, value in enumerate([self.left, *self.sent[0]])]
        pieces += [
            (value, 1, i, (i, d)) for d, value in enumerate([self.right, *self.sent[1]]) for i in range(up)
        ]
        left, right = copies_call(pieces, self.outs(up, across, line), deps)
        left, right = left.reshape(-1, left.shape[-1]), right.reshape(-1, right.shape[-1])
        return (left, swap(left, 1)), (right, swap(right, 1))


class Shares:

    def __init__(self, keep, send):
        line, plane = axes_of(lax.axis_size("seq"))["z"]
        self.groups = [(plane // 2, 2), (line, plane)]
        shape = (plane // 2, line, keep.shape[0] // (plane // 2 * line), keep.shape[1])
        self.send = send
        self.terms = [keep.reshape(shape), swap(send.reshape(shape), 1)]

    def step(self, deps=(), behind=None):
        size, shift = self.groups.pop(0)
        if deps:
            pieces = list(
                kernel_call(pieces_kernel, [(self.terms[0].shape[1:], BF16)] * size, self.terms, deps=deps)
            )
        else:
            none = 0.0
            if behind is not None:
                none = held_back(behind)
            pieces = []
            for d in range(size):
                picked = [t[d].astype(F32) for t in self.terms]
                pieces.append((sum(picked[1:], picked[0]) + none).astype(BF16))
        self.terms = [pieces[0]] + [swap(pieces[d], d * shift) for d in range(1, size)]
        return pieces


def pieces_kernel(*refs):
    size = refs[0].shape[0]
    terms, outs = refs[:-size], refs[-size:]
    for d, out in enumerate(outs):
        total = terms[0][d].astype(F32)
        for term in terms[1:]:
            total = total + term[d].astype(F32)
        out[...] = total.astype(BF16)


def turned_dot(left, right):
    return lax.dot_general(left, right, (((0,), (0,)), ((), ())), preferred_element_type=F32).astype(BF16)


def share_terms(left, right):
    half = left.shape[1] // 2
    return Shares(turned_dot(left[:, :half], right), turned_dot(left[:, half:], right))


def plane_first(count):
    plane = axes_of(count)["z"][1]
    return np.arange(count).reshape(-1, plane).T.reshape(-1)


def scatter_planes(grad):
    count = lax.axis_size("seq")
    plane = axes_of(count)["z"][1]
    groups = np.arange(count).reshape(-1, plane).tolist()
    return lax.psum_scatter(grad, "seq", scatter_dimension=0, tiled=True, axis_index_groups=groups)


def held_back(behind):
    return jnp.minimum(jnp.abs(behind[(0,) * behind.ndim].astype(F32)), 0.0)


def line_terms(grad):
    line, plane = axes_of(lax.axis_size("seq"))["z"]
    place = lax.axis_index("seq") // plane
    parts = grad.reshape(line, -1, grad.shape[1])
    pieces = [lax.dynamic_index_in_dim(parts, place ^ d, 0, False) for d in range(line)]
    return [pieces[0]] + [swap(pieces[d], d * plane) for d in range(1, line)]


def round_kernel(value, out):
    out[...] = value[...].astype(BF16)


def add_kernel(left, right, *outs):
    total = left[...].astype(F32) + right[...].astype(F32)
    for out in outs:
        out[...] = total.astype(out.dtype)


def sum_rounds(value, first, last, deps=()):
    flip = first
    while flip >= last:
        kind = BF16 if flip > 1 else F32
        late, deps = (deps[0], deps[1:]) if deps else ((), ())
        (value,) = kernel_call(add_kernel, [(value.shape, kind)], (value, swap(value, flip)), deps=late)
        flip //= 2
    return value


def gather_small(value, deps):
    flip, rows = 1, value.shape[0]
    while flip < lax.axis_size("seq"):
        late, deps = deps[0], deps[1:] or deps
        first, second = slice(0, flip * rows), slice(flip * rows, 2 * flip * rows)
        pieces = [(value, 0, None, first), (swap(value, flip), 0, None, second)]
        (value,) = copies_call(pieces, [((2 * flip * rows, LANES), value.dtype)], late)
        flip *= 2
    return value


def held_bytes(shape, kind):
    *lead, rows, lanes = (1, *shape) if len(shape) < 2 else shape
    rows, lanes = -(-rows // 16) * 16, -(-lanes // LANES) * LANES
    return int(np.prod(lead, dtype=np.int64)) * rows * lanes * jnp.dtype(kind).itemsize


def room_for(arrays, scratch):
    total = sum(held_bytes(*a) for a in arrays) + sum(held_bytes(r.shape, r.dtype) for r in scratch)
    return total + total // 8 + 3 * MB


def far(array):
    return pltpu.with_memory_space_constraint(array, pltpu.HBM)


def kernel_call(body, outs, args, scratch=(), flops=0, deps=()):
    places = [pltpu.SMEM if a.dtype == jnp.int32 else pltpu.VMEM for a in args] + [pl.ANY] * len(deps)
    known = len(args)

    def run(*refs):
        body(*refs[:known], *refs[known + len(deps) :])

    size = sum(int(np.prod(a.shape)) * a.dtype.itemsize for a in args) + sum(
        int(np.prod(o[0])) * jnp.dtype(o[1]).itemsize for o in outs
    )
    return pl.pallas_call(
        run,
        out_shape=tuple(jax.ShapeDtypeStruct(*o) for o in outs),
        in_specs=[pl.BlockSpec(memory_space=p) for p in places],
        out_specs=tuple(pl.BlockSpec(memory_space=pltpu.VMEM) for _ in outs),
        scratch_shapes=list(scratch),
        compiler_params=pltpu.CompilerParams(vmem_limit_bytes=min(CAP, room_for([(a.shape, a.dtype) for a in args] + list(outs), scratch))
        ),
        cost_estimate=pl.CostEstimate(flops=flops, bytes_accessed=size, transcendentals=0),
    )(*args, *deps)


def streamed_call(body, outs, args, scratch=(), flops=0, streamed=None, raw=()):
    places = [pltpu.SMEM if a.dtype == jnp.int32 else pltpu.VMEM for a in args]
    size = sum(int(np.prod(a.shape)) * a.dtype.itemsize for a in (*args, streamed)) + sum(
        int(np.prod(o[0])) * jnp.dtype(o[1]).itemsize for o in (*outs, *raw)
    )
    return pl.pallas_call(
        body,
        out_shape=tuple(jax.ShapeDtypeStruct(*o) for o in (*outs, *raw)),
        in_specs=[pl.BlockSpec(memory_space=p) for p in (pltpu.HBM, *places)],
        out_specs=tuple(pl.BlockSpec(memory_space=p) for p in [pltpu.VMEM] * len(outs) + [pltpu.HBM] * len(raw)),
        scratch_shapes=[*scratch, pltpu.SemaphoreType.DMA((3 * len(raw),))],
        compiler_params=pltpu.CompilerParams(vmem_limit_bytes=room_for([], scratch) + 8 * MB),
        cost_estimate=pl.CostEstimate(flops=flops, bytes_accessed=size, transcendentals=0),
    )(streamed, *args)


def copies_call(pieces, outs, deps=()):
    arrays = [p[0] for p in pieces]
    known, written = len(arrays), len(outs)

    def run(*refs):
        refs = refs[:known] + refs[known + len(deps) :]
        results, held, (sems, out_sems) = refs[known : known + written], refs[known + written : -2], refs[-2:]
        copies = []
        for k, (_, out, source, target) in enumerate(pieces):
            src = refs[k] if source is None else refs[k].at[source]
            copies.append(pltpu.make_async_copy(src, held[out].at[target], sems.at[k]))
            copies[-1].start()
        for copy in copies:
            copy.wait()
        copies = []
        for k in range(written):
            copies.append(pltpu.make_async_copy(held[k], results[k], out_sems.at[k]))
            copies[-1].start()
        for copy in copies:
            copy.wait()

    size = sum(2 * int(np.prod(o[0])) * jnp.dtype(o[1]).itemsize for o in outs)
    return pl.pallas_call(
        run,
        out_shape=tuple(jax.ShapeDtypeStruct(*o) for o in outs),
        in_specs=[pl.BlockSpec(memory_space=pltpu.HBM)] * known + [pl.BlockSpec(memory_space=pl.ANY)] * len(deps),
        out_specs=tuple(pl.BlockSpec(memory_space=pltpu.HBM) for _ in outs),
        scratch_shapes=[pltpu.VMEM(*o) for o in outs]
        + [pltpu.SemaphoreType.DMA((known,)), pltpu.SemaphoreType.DMA((written,))],
        compiler_params=pltpu.CompilerParams(vmem_limit_bytes=room_for(outs, ())),
        cost_estimate=pl.CostEstimate(flops=0, bytes_accessed=size, transcendentals=0),
    )(*arrays, *deps)


def copy_kernel(value, out):
    out[...] = value[...]


def after(value, *deps):
    return kernel_call(copy_kernel, [(value.shape, value.dtype)], (value,), deps=deps)[0]


def dot(left, right, precision=None):
    return jnp.dot(left, right, precision=precision, preferred_element_type=F32)


def dot_t(left, right):
    return lax.dot_general(left, right, (((1,), (1,)), ((), ())), preferred_element_type=F32)


def halves(value):
    high = value.astype(BF16)
    return high, (value - high.astype(F32)).astype(BF16)


def fine(form, left, right):
    (lh, ll), (rh, rl) = halves(left), halves(right)
    return form(lh, rh) + (form(ll, rh) + form(lh, rl))


def lanes_of(rows):
    return lax.broadcasted_iota(jnp.int32, (rows, LANES), 1)


def spread(values, pair):
    low = lanes_of(values.shape[0]) < HEAD_DIM
    return jnp.where(low, values[:, 2 * pair : 2 * pair + 1], values[:, 2 * pair + 1 : 2 * pair + 2])


def spread_row(row):
    return jnp.concatenate([spread(row, pair) for pair in range(PAIRS)], axis=1)


def head_sums(product, pair):
    rows = lax.broadcasted_iota(jnp.int32, (LANES, LANES), 0)
    cols = lax.broadcasted_iota(jnp.int32, (LANES, LANES), 1)
    pick = (cols == 2 * pair + (rows >= HEAD_DIM).astype(jnp.int32)).astype(BF16)
    high = product.astype(BF16)
    low = (product - high.astype(F32)).astype(BF16)
    return dot(high, pick) + dot(low, pick)


def sigmoid(v):
    return 1.0 / (1.0 + jnp.exp(-v))


def silu(v):
    return v * sigmoid(v)


def parted(j, parts):
    half = PAIRS // 2
    return parts[j // half], tile(j % half)


def tile(pair):
    return slice(pair * LANES, (pair + 1) * LANES)


def pack_row(row):
    first = row.astype(BF16).astype(F32)
    second = (row - first).astype(BF16).astype(F32)
    third = row - first - second
    place = lax.broadcasted_iota(jnp.int32, (16, row.shape[1]), 0)
    packed = jnp.where(place == 0, first, jnp.where(place == 1, second, third))
    return jnp.where(place < 3, packed, 0.0).astype(BF16)


def unpack_row(rows):
    return jnp.sum(rows.astype(F32), axis=0, keepdims=True)


def emit_msg(total, keep, msg_o):
    msg_o[0:STATE, :] = total.astype(msg_o.dtype)
    if msg_o.dtype == F32:
        msg_o[STATE:, :] = jnp.broadcast_to(keep, (msg_o.shape[0] - STATE, keep.shape[1]))
    else:
        msg_o[STATE:, :] = pack_row(keep)


def read_msg(recv):
    if recv.dtype == F32:
        return recv[0:STATE, :], recv[STATE : STATE + 1, :]
    return recv[0:STATE, :].astype(F32), unpack_row(recv[STATE:, :])


def emit_halves(total, keep, upper, own_o, msg_o):
    half = total.shape[1] // 2
    low, high = total[:, :half], total[:, half:]
    klow, khigh = keep[:, :half], keep[:, half:]
    emit_msg(jnp.where(upper, high, low), jnp.where(upper, khigh, klow), own_o)
    emit_msg(jnp.where(upper, low, high), jnp.where(upper, klow, khigh), msg_o)


def bit_of(me, flip):
    return (me[0] & flip) != 0


def state_out(width, kind=F32):
    return ((STATE + (8 if kind == F32 else 16), width), kind)


def in_order(relative, place, back):
    size = len(relative)
    ordered = []
    for step in range(size):
        member = size - 1 - step if back else step
        value = relative[0]
        for d in range(1, size):
            value = jnp.where(jnp.bitwise_xor(place, member) == d, relative[d], value)
        ordered.append(value)
    return ordered


def place_of(me, shift, size):
    return jnp.bitwise_and(lax.shift_right_logical(me[0], shift.bit_length() - 1), size - 1)


def pair_kernel(own, recv, me, first_o, mine_o, m1, m2, m3, joined, *, back):
    other, kother = read_msg(recv)
    mine, kmine = read_msg(own)
    first = jnp.logical_xor(bit_of(me, 1), not back)
    t_first, k_first = jnp.where(first, mine, other), jnp.where(first, kmine, kother)
    t_second, k_second = jnp.where(first, other, mine), jnp.where(first, kother, kmine)
    emit_msg(t_first, k_first, first_o)
    emit_msg(k_second * t_first + t_second, k_first * k_second, joined)
    place = place_of(me, 2, 4)
    width = mine_o.shape[1]
    for d, out in enumerate((mine_o, m1, m2, m3)):
        at = pl.ds(pl.multiple_of(jnp.bitwise_xor(place, d) * width, LANES), width)
        emit_msg(joined[0:STATE, at], joined[STATE : STATE + 1, at], out)


def scan_group(own, recvs, place, back):
    read = [read_msg(r) for r in (own, *recvs)]
    totals = in_order([r[0] for r in read], place, back)
    keeps = in_order([r[1] for r in read], place, back)
    prefixes, value, decay = [], jnp.zeros_like(totals[0]), jnp.ones_like(keeps[0])
    for t, k in zip(totals, keeps):
        prefixes.append((value, decay))
        value, decay = k * value + t, decay * k
    return prefixes, value, decay


def own_prefix(prefixes, place, back):
    size = len(prefixes)
    value, decay = prefixes[0]
    for step in range(1, size):
        mine = place == (size - 1 - step if back else step)
        value = jnp.where(mine, prefixes[step][0], value)
        decay = jnp.where(mine, prefixes[step][1], decay)
    return value, decay


def plane_kernel(mine, r1, r2, r3, me, pre_o, *outs, back):
    prefixes, value, decay = scan_group(mine, (r1, r2, r3), place_of(me, 2, 4), back)
    for step, (prefix, kprefix) in enumerate(prefixes):
        emit_msg(prefix, kprefix, pre_o.at[3 - step if back else step])
    for out in outs:
        emit_msg(value, decay, out)


def line_kernel(own, *refs, size, shift, back, carried, final):
    recvs, refs = refs[: size - 1], refs[size - 1 :]
    if carried:
        state, *refs = refs
    if final:
        pre, *refs = refs
    me, *outs = refs
    place = place_of(me, shift, size)
    prefixes, value, decay = scan_group(own, recvs, place, back)
    into, kinto = own_prefix(prefixes, place, back)
    if carried:
        before, kbefore = read_msg(state)
        into, kinto = kbefore * into + before, kbefore * kinto
    if not final:
        emit_msg(into, kinto, outs[0])
        for out in outs[1:]:
            emit_msg(value, decay, out)
        return
    plane = place_of(me, 2, 4)
    for d, out in enumerate(outs):
        prefix, kprefix = read_msg(pre.at[jnp.bitwise_xor(plane, d)])
        out[...] = (kprefix * into + prefix).astype(out.dtype)


def down_kernel(mine, r1, r2, r3, first, me, mine_o, msg_o, whole, *, back):
    place = place_of(me, 2, 4)
    width = mine.shape[1]
    for d, ref in enumerate((mine, r1, r2, r3)):
        at = pl.ds(pl.multiple_of(jnp.bitwise_xor(place, d) * width, LANES), width)
        whole[:, at] = ref[...].astype(F32)
    into = whole[...]
    t_first, k_first = read_msg(first)
    beyond = k_first * into + t_first
    second = jnp.logical_xor(bit_of(me, 1), back)
    mine_o[...] = jnp.where(second, beyond, into)
    msg_o[...] = jnp.where(second, into, beyond).astype(msg_o.dtype)


def join_halves(mine, recv, upper):
    theirs = recv[...].astype(F32)
    own = mine[...]
    return jnp.where(upper, theirs, own), jnp.where(upper, own, theirs)


def exchange(own, msg, me, back, deps=((), (), (), ())):
    count = lax.axis_size("seq")
    kind = msg.dtype
    width = INNER // 2
    quarter = width // 4
    part, message = state_out(quarter), state_out(quarter, kind)
    both = [message] if kind == F32 else [part, message]
    recv = swap(msg, 1)
    first, mine, *msgs = kernel_call(
        partial(pair_kernel, back=back), [state_out(width), part] + [message] * 3,
        (own, recv, me), deps=deps[0], scratch=[pltpu.VMEM(*state_out(width))],
    )
    recvs = [swap(m, 2 * (d + 1)) for d, m in enumerate(msgs)]
    pre, *totals = kernel_call(
        partial(plane_kernel, back=back), [((4, *part[0]), F32)] + both,
        (mine, *recvs, me), deps=deps[1],
    )
    carried = ()
    shift = 8
    while True:
        size = min(4, count // shift)
        recvs = [swap(totals[-1], shift * d) for d in range(1, size)]
        final = shift * size == count
        form = partial(line_kernel, size=size, shift=shift, back=back, carried=bool(carried), final=final)
        shift *= size
        if final:
            break
        state, *totals = kernel_call(form, [part] + both, (totals[0], *recvs, *carried, me))
        carried = (state,)
    mine, *msgs = kernel_call(
        form, [((STATE, quarter), F32)] + [((STATE, quarter), kind)] * 3,
        (totals[0], *recvs, *carried, pre, me), deps=deps[2],
    )
    recvs = [swap(m, 2 * (d + 1)) for d, m in enumerate(msgs)]
    mine, msg = kernel_call(
        partial(down_kernel, back=back), [((STATE, width), F32), ((STATE, width), kind)],
        (mine, *recvs, first, me), deps=deps[3], scratch=[pltpu.VMEM((STATE, width), F32)],
    )
    return mine, swap(msg, 1)


def norm_kernel(h, halo, gain, out):
    for ref, at in ((halo, slice(0, HALO)), (h, slice(HALO, HALO + h.shape[0]))):
        v = ref[...].astype(F32)
        inv = lax.rsqrt(jnp.mean(v * v, axis=-1, keepdims=True) + EPS)
        out[at, :] = (v * inv * gain[0:1, :]).astype(BF16)


def norm_back_kernel(gn, h, g, gain, wide, *refs):
    *others, out, wide_o = refs
    v = h[...].astype(F32)
    grad = gn[...]
    inv = lax.rsqrt(jnp.mean(v * v, axis=-1, keepdims=True) + EPS)
    n = v * inv
    q = grad * gain[0:1, :]
    out[...] = g[...] + inv * (q - n * jnp.mean(q * n, axis=-1, keepdims=True))
    wide_o[0:8, :] = wide[...]
    wide_o[6:7, 0 : v.shape[1]] = jnp.sum(grad * n, axis=0, keepdims=True)
    for other in others:
        wide_o[8:, :] = other[...]


def grads_kernel(gn, normed, mixed, gz, *outs, steps):
    half = INNER // 2
    several, rows = outs[0].shape[0], outs[0].shape[1] // 4
    for k, out in enumerate(outs):

        @pl.when(pl.program_id(0) // steps == k)
        def _(out=out):
            turned = lax.dot_general(gn[...], mixed[...], (((0,), (0,)), ((), ())), preferred_element_type=F32)
            out[:, 2 * rows :, :] = turned.astype(BF16).reshape(several, 2 * rows, half)
            narrow = normed[HALO:, :]
            for q in range(2):
                part = gz[:, q * half : (q + 1) * half]
                turned = lax.dot_general(narrow, part, (((0,), (0,)), ((), ())), preferred_element_type=F32)
                out[:, q * rows : (q + 1) * rows, :] = turned.astype(BF16).reshape(several, rows, half)


def grads_call(gn, normed, mixed, gz, count, parts):
    rows, half = mixed.shape
    wide = 2 * LANES
    several = wide * count // INNER
    steps = count // several // parts
    shape = (several, 4 * half // count, half)

    def share(k):
        return pl.BlockSpec(shape, lambda i: (jnp.clip(i - k * steps, 0, steps - 1), 0, 0))

    return pl.pallas_call(
        partial(grads_kernel, steps=steps),
        grid=(parts * steps,),
        out_shape=[pltpu.HBM((count // parts, *shape[1:]), BF16)] * parts,
        in_specs=[
            pl.BlockSpec((rows, wide), lambda i: (0, i)), pl.BlockSpec((HALO + rows, wide // 2), lambda i: (0, i)),
            pl.BlockSpec(mixed.shape, lambda i: (0, 0)), pl.BlockSpec(gz.shape, lambda i: (0, 0)),
        ],
        out_specs=[share(k) for k in range(parts)],
        compiler_params=pltpu.CompilerParams(vmem_limit_bytes=14 * MB),
        cost_estimate=pl.CostEstimate(flops=8 * rows * half * half, bytes_accessed=10 * MB, transcendentals=0),
    )(gn, normed, mixed, gz)


def own_rows_kernel(gp, spilled, gz, out, gz_o):
    gz_o[...] = gz[...]
    end = out.shape[0] - HALO
    out[0:end, :] = gp[HALO : HALO + end, :]
    out[end:, :] = (gp[HALO + end :, :].astype(F32) + spilled[...].astype(F32)).astype(BF16)


def triangle(rows, lower):
    r = lax.broadcasted_iota(jnp.int32, (rows, rows), 0)
    c = lax.broadcasted_iota(jnp.int32, (rows, rows), 1)
    return r >= c if lower else r <= c


def conv_state_kernel(pc, cw, hp, mk, me, left_o, right_o, bc_o, dt_o, log_o, own_o, msg_o, xw, *low, precise):
    rows = mk.shape[0]
    marks = mk[...]
    raw = pc[HALO:, CONV_CH:WIDE].astype(F32) + hp[0:1, :]
    soft = jnp.maximum(raw, 0.0) + jnp.log1p(jnp.exp(-jnp.abs(raw)))
    dt = jnp.where(lanes_of(rows) < HEADS, soft, 0.0)
    log = dot(triangle(rows, True).astype(F32), dt * hp[1:2, :], EXACT)
    last = log[rows - 1 : rows, :]
    weight = marks[:, 4:5] * jnp.exp(last - log) * dt
    dt_o[...] = dt
    log_o[...] = log
    b_cols = None
    for j in range(CONV_CH // LANES):
        ext = pc[:, tile(j)].astype(F32)
        out = cw[4:5, tile(j)] + cw[3:4, tile(j)] * ext[HALO:, :]
        for k in range(CONV_K - 1):
            out = out + cw[k : k + 1, tile(j)] * ext[LEAD + k : LEAD + k + rows, :] * marks[:, k : k + 1]
        part, at = parted(j, (left_o, right_o, bc_o))
        part[:, at] = out
        if j < PAIRS:
            high, rest = halves(silu(out) * spread(weight, j))
            xw[:, tile(j)] = high
            if precise:
                low[0][:, tile(j)] = rest
        elif j == PAIRS:
            b_cols, b_rest = halves(silu(out).T)
    total = dot(b_cols, xw[...])
    if precise:
        total = total + (dot(b_rest, xw[...]) + dot(b_cols, low[0][...]))
    keep = spread_row(jnp.exp(last) * marks[rows - 1 : rows, 3:4])
    emit_halves(total, keep, bit_of(me, 1), own_o, msg_o)


def mask_bias(mk, sr, rows):
    same = mk[:, 5:6] == sr[0:1, :]
    return jnp.where(jnp.logical_and(triangle(rows, True), same), 0.0, FAR)


def within_kernel(conv, bc, dt, log, hp, mk, sr, y_o, xdt, lcol, lrow, *lower, precise, first):
    rows = mk.shape[0]
    pairs = PAIRS // 2
    scores = fine(dot_t, silu(bc[:, tile(1)]), silu(bc[:, tile(0)]))
    bias = mask_bias(mk, sr, rows)
    dtv, logv = dt[...], log[...]
    lrow[...] = logv.T
    for j in range(pairs):
        x = silu(conv[:, tile(j)])
        high, rest = halves(x * spread(dtv, first + j))
        xdt[:, tile(j)] = high
        if precise:
            lower[0][:, tile(j)] = rest
        y_o[:, tile(j)] = x * spread(hp[2:3, :], first + j)
    for h in range(2 * pairs):
        lcol[h] = jnp.broadcast_to(logv[:, 2 * first + h : 2 * first + h + 1], (rows, LANES))
    low = lanes_of(rows) < HEAD_DIM

    def pair(j, _):
        at = pl.ds(pl.multiple_of(j * LANES, LANES), LANES)
        xp = xdt[:, at]
        res = []
        for q in range(2):
            col = lcol[2 * j + q]
            row = lrow[pl.ds(2 * (first + j) + q, 1), :]
            span = jnp.concatenate([col] * (rows // LANES), axis=1) - row
            mix = scores * jnp.exp(span + bias)
            if precise:
                high, rest = halves(mix)
                res.append(dot(high, xp) + (dot(rest, xp) + dot(high, lower[0][:, at])))
            else:
                res.append(dot(mix.astype(BF16), xp))
        y_o[:, at] += jnp.where(low, res[0], res[1])
        return 0

    lax.fori_loop(0, pairs, pair, 0)


def post_kernel(*refs, places, relative, spans, aligned):
    if spans:
        pack, *refs = refs
        *refs, gated, zbuf, obuf, sems = refs
        parts = len(spans) - 1
        refs, raw = [*refs[:-parts], gated], refs[-parts:]
    else:
        z_low, z_high, out_w, *refs = refs
    normed, h, yw, yw2, mine, recv, bc, log, mk, gg, me, z, y_o, gn_o, st_o, st2_o, h_o, *rel_o, gated = refs
    rows = mk.shape[0]
    wide = 2 * LANES
    half = INNER // 2
    own = normed[HALO:, :]
    flying = []

    def moved(source, target):
        copy = pltpu.make_async_copy(source, target, sems.at[len(flying)])
        flying.append(copy)
        copy.start()
        return copy

    def apart(buffer, base, k):
        return moved(buffer.at[:, spans[k] - base : spans[k + 1] - base, :], raw[k])

    if spans:
        coming = [moved(pack.at[:, spans[0] : spans[2], :], zbuf), moved(pack.at[:, spans[2] : spans[3], :], obuf)]
        coming[0].wait()
        leaving = [apart(zbuf, 0, 0), apart(zbuf, 0, 1)]

    def project(i, _):
        for q in range(2):
            at = pl.ds(pl.multiple_of(i * wide, wide), wide)
            if spans:
                part = zbuf[:, spans[q] : spans[q + 1], at]
                part = part.reshape(-1, part.shape[-1])
            else:
                part = (z_low, z_high)[q][:, at]
            z[:, pl.ds(pl.multiple_of(q * half + i * wide, wide), wide)] = dot(own, part).astype(BF16)
        return 0

    lax.fori_loop(0, half // wide, project, 0)
    if spans:
        for copy in leaving:
            copy.wait()
        more = len(spans) > 4
        if more:
            second = moved(pack.at[:, spans[3] : spans[5], :], zbuf)
        coming[1].wait()
        leaving = [apart(obuf, spans[2], 2)]
    low, high = join_halves(mine, recv, bit_of(me, 1))
    st_o[...] = low.astype(BF16)
    st2_o[...] = high.astype(BF16)
    c = silu(bc[:, tile(1)])
    inflow = jnp.exp(log[...]) * mk[:, 3:4]
    total = jnp.zeros((rows, LANES), F32)
    for j in range(PAIRS):
        part = (yw if j < PAIRS // 2 else yw2)[:, tile(j % (PAIRS // 2))]
        state = (low if j < PAIRS // 2 else high)[:, tile(j % (PAIRS // 2))]
        y = part + fine(dot, c, state) * spread(inflow, j)
        y_o[:, tile(j)] = y
        v = y * silu(z[:, tile(j)].astype(F32))
        gated[:, tile(j)] = v
        total = total + v * v
    inv = lax.rsqrt(jnp.sum(total, axis=-1, keepdims=True) / INNER + EPS)
    for j in range(PAIRS):
        gn_o[:, tile(j)] = (gated[:, tile(j)] * inv * gg[0:1, tile(j)]).astype(BF16)

    if spans and more:
        second.wait()
        leaving += [apart(zbuf, spans[3], 3), apart(zbuf, spans[3], 4)]

    def output(i, _):
        at = pl.ds(pl.multiple_of(i * wide, wide), wide)
        if spans:
            part = obuf[:, :, at]
            part = part.reshape(-1, part.shape[-1])
        else:
            part = out_w[:, at]
        h_o[:, at] = h[:, at].astype(F32) + dot(gn_o[...], part)
        return 0

    lax.fori_loop(0, h.shape[1] // wide, output, 0)
    if spans and more:
        leaving[0].wait()
        last = obuf.at[:, : spans[6] - spans[5], :]
        moved(pack.at[:, spans[5] : spans[6], :], last).wait()
        leaving = leaving[1:] + [moved(last, raw[5])]
    if rel_o:
        lower = lanes_of(rows) < HEAD_DIM
        for j in range(PAIRS):
            base = me[0] if relative else jnp.int32(0)
            sources = [jnp.bitwise_xor(base, jnp.int32(int(places[2 * j + q]))) for q in range(2)]
            upper = jnp.bitwise_and(sources[0], 1) == 1
            tiles = []
            for src in sources:
                at = pl.multiple_of(lax.shift_right_logical(src, 1) * LANES, LANES)
                tiles.append(gn_o[:, pl.ds(at, LANES)].astype(F32))
            left = jnp.where(upper, pltpu.roll(tiles[0], HEAD_DIM, 1), tiles[0])
            right = jnp.where(upper, tiles[1], pltpu.roll(tiles[1], HEAD_DIM, 1))
            rel_o[0][:, tile(j)] = jnp.where(lower, left, right).astype(BF16)
    if spans:
        for copy in leaving:
            copy.wait()


def post_back_kernel(ggn, y, z, gg, left, right, bc, log, mk, me, gy_o, gy2_o, gz_o, gate_o, skip_o, own_o, msg_o, ge):
    rows = mk.shape[0]
    logv = log[...]
    inflow = jnp.exp(logv) * mk[:, 3:4]
    total = jnp.zeros((rows, LANES), F32)
    cross = jnp.zeros((rows, LANES), F32)
    for j in range(PAIRS):
        v = y[:, tile(j)] * silu(z[:, tile(j)].astype(F32))
        total = total + v * v
        cross = cross + v * ggn[:, tile(j)] * gg[0:1, tile(j)]
    inv = lax.rsqrt(jnp.sum(total, axis=-1, keepdims=True) / INNER + EPS)
    mean = jnp.sum(cross, axis=-1, keepdims=True) * inv / INNER
    skips = jnp.zeros((8, LANES), F32)
    for j in range(PAIRS):
        zf = z[:, tile(j)].astype(F32)
        s = sigmoid(zf)
        sz = zf * s
        yv = y[:, tile(j)]
        n = yv * sz * inv
        up = ggn[:, tile(j)]
        gga = inv * (up * gg[0:1, tile(j)] - n * mean)
        gy = gga * sz
        gz_o[:, tile(j)] = (gga * yv * (s * (1.0 + zf * (1.0 - s)))).astype(BF16)
        part, at = parted(j, (gy_o, gy2_o))
        part[:, at] = gy.astype(BF16)
        ge[:, tile(j)] = (gy * spread(inflow, j)).astype(BF16)
        gate_o[:, tile(j)] = jnp.broadcast_to(jnp.sum(up * n, axis=0, keepdims=True), (8, LANES))
        part, at = parted(j, (left, right))
        through = jnp.sum(gy * silu(part[:, at]), axis=0, keepdims=True)
        skips = skips + head_sums(jnp.broadcast_to(through, (8, LANES)), j)
    skip_o[...] = skips
    c_cols = silu(bc[:, tile(1)]).T.astype(BF16)
    state = dot(c_cols, ge[...])
    keep = spread_row(jnp.exp(logv[rows - 1 : rows, :]) * mk[rows - 1 : rows, 3:4])
    emit_halves(state, keep, bit_of(me, 1), own_o, msg_o)


def within_back_kernel(
    conv, bc, dt, log, gy, st, mk, sr, gxdt_o, gb_o, gc_o, gl_o, xdt, ge, lcol, lrow, gscore, lsum, csum, *, first
):
    rows = mk.shape[0]
    pairs = PAIRS // 2
    bf, cf = silu(bc[:, tile(0)]), silu(bc[:, tile(1)])
    b, c = bf.astype(BF16), cf.astype(BF16)
    scores = fine(dot_t, bf, cf)
    same = mk[:, 5:6] == sr[0:1, :]
    bias = jnp.where(jnp.logical_and(triangle(rows, False), same), 0.0, FAR)
    dtv, logv = dt[...], log[...]
    lrow[...] = logv.T
    inflow = jnp.exp(logv) * mk[:, 3:4]
    flow = jnp.zeros((rows, LANES), F32)
    for j in range(pairs):
        xdt[:, tile(j)] = (silu(conv[:, tile(j)]) * spread(dtv, first + j)).astype(BF16)
        gyv = gy[:, tile(j)].astype(F32) * spread(inflow, first + j)
        ge[:, tile(j)] = gyv.astype(BF16)
        flow = flow + head_sums(gyv * dot(c, st[:, tile(j)]), first + j)
    for h in range(2 * pairs):
        lcol[h] = jnp.broadcast_to(logv[:, 2 * first + h : 2 * first + h + 1], (rows, LANES))
    lanes = lanes_of(rows)
    low = lanes < HEAD_DIM
    gscore[...] = jnp.zeros_like(gscore)
    csum[...] = jnp.zeros_like(csum)
    lsum[...] = jnp.zeros_like(lsum)

    def pair(j, _):
        at = pl.ds(pl.multiple_of(j * LANES, LANES), LANES)
        xp, gp = xdt[:, at], gy[:, at]
        res = []
        for q in range(2):
            h = 2 * (first + j) + q
            span = lrow[pl.ds(h, 1), :] - jnp.concatenate([lcol[2 * j + q]] * (rows // LANES), axis=1)
            decay = jnp.exp(span + bias)
            mix = scores * decay
            own = jnp.where(low if q == 0 else jnp.logical_not(low), gp, jnp.zeros_like(gp))
            gmix = dot_t(xp, own)
            gscore[...] += gmix * decay
            term = gmix * mix
            lsum[pl.ds(h, 1), :] = jnp.sum(term, axis=0, keepdims=True)
            csum[...] += jnp.where(lanes == h, jnp.sum(term, axis=1, keepdims=True), 0.0)
            res.append(dot(mix.astype(BF16), gp))
        gxdt_o[:, at] = jnp.where(low, res[0], res[1])
        return 0

    lax.fori_loop(0, pairs, pair, 0)
    gs = gscore[...]
    gb_o[...] = dot(gs.astype(BF16), c)
    gc_o[...] = dot(gs.T.astype(BF16), b) + dot_t(ge[...], st[...])
    gl_o[...] = lsum[...].T - csum[...] + flow


def mixer_back_kernel(
    gxdt2, gy2, right, pc, cw, gxdt, gbi, gci, gli, gbi2, gci2, gli2, mine, recv, gy, left, bc, dt, log, st, st2,
    hp, mk, gate, skip, me, gp_o, wide_o, gb16, xe, acc,
):
    rows = mk.shape[0]
    marks = mk[...]
    low, high = join_halves(mine, recv, bit_of(me, 1))
    half = INNER // 2
    kg = jnp.zeros((8, LANES), F32)
    for part, value in ((0, low), (half, high)):
        gb16[:, part : part + half] = value.astype(BF16)
        rowsum = jnp.sum(value * (st if part == 0 else st2)[...].astype(F32), axis=0, keepdims=True)
        for j in range(PAIRS // 2):
            pair = part // LANES + j
            kg = kg + head_sums(jnp.broadcast_to(rowsum[:, tile(j)], (8, LANES)), pair)
    dtv, logv = dt[...], log[...]
    last = logv[rows - 1 : rows, :]
    b = silu(bc[:, tile(0)]).astype(BF16)
    outflow = marks[:, 4:5] * jnp.exp(last - logv)
    gv = jnp.zeros((rows, LANES), F32)
    gd = jnp.zeros((rows, LANES), F32)

    def conv_back(j, gact, s, out):
        gco = gact * (s * (1.0 + out * (1.0 - s)))
        ext = pc[:, tile(j)].astype(F32)
        acc[...] = jnp.zeros_like(acc)
        for k in range(CONV_K):
            gk = gco if k == CONV_K - 1 else gco * marks[:, k : k + 1]
            wide_o[k : k + 1, tile(j)] = jnp.sum(gk * ext[LEAD + k : LEAD + k + rows, :], axis=0, keepdims=True)
            acc[LEAD + k : LEAD + k + rows, :] += gk * cw[k : k + 1, tile(j)]
        wide_o[4:5, tile(j)] = jnp.sum(gco, axis=0, keepdims=True)
        gp_o[:, tile(j)] = acc[...].astype(BF16)

    wide_o[6:8, :] = jnp.zeros((2, CONV_CH), F32)
    for j in range(PAIRS):
        part, at = parted(j, (left, right))
        out = part[:, at]
        s = sigmoid(out)
        x = out * s
        dtp = spread(dtv, j)
        flow = spread(outflow, j)
        xd = x * dtp
        gxs = dot(b, gb16[:, tile(j)]) * flow
        xe[:, tile(j)] = (xd * flow).astype(BF16)
        gxd = (gxdt if j < PAIRS // 2 else gxdt2)[:, at] + gxs
        gv = gv + head_sums(xd * gxs, j)
        gd = gd + head_sums(x * gxd, j)
        conv_back(j, dtp * gxd + spread(hp[2:3, :], j) * (gy if j < PAIRS // 2 else gy2)[:, at].astype(F32), s, out)
    gb = gbi[...] + gbi2[...] + dot_t(xe[...], gb16[...])
    for j, grad in ((PAIRS, gb), (PAIRS + 1, gci[...] + gci2[...])):
        out = bc[:, tile(j - PAIRS)]
        conv_back(j, grad, sigmoid(out), out)
    keep = jnp.exp(last) * marks[rows - 1 : rows, 3:4]
    edge = jnp.sum(gv, axis=0, keepdims=True) + kg[0:1, :] * keep
    place = lax.broadcasted_iota(jnp.int32, (rows, LANES), 0)
    gl = gli[...] + gli2[...] - gv + jnp.where(place == rows - 1, edge, 0.0)
    ga = dot(triangle(rows, False).astype(F32), gl, EXACT)
    rate = hp[1:2, :]
    raw = pc[HALO:, CONV_CH:WIDE].astype(F32) + hp[0:1, :]
    graw = jnp.where(lanes_of(rows) < HEADS, (ga * rate + gd) * sigmoid(raw), 0.0)
    gp_o[0:HALO, CONV_CH:WIDE] = jnp.zeros((HALO, LANES), BF16)
    gp_o[HALO:, CONV_CH:WIDE] = graw.astype(BF16)
    wide_o[5:6, 0:INNER] = gate[0:1, :]
    place = lanes_of(1)
    heads = jnp.where(place < HEADS, jnp.sum(graw, axis=0, keepdims=True), 0.0)
    for k, row in enumerate((rate * jnp.sum(ga * dtv, axis=0, keepdims=True), skip[0:1, :])):
        heads = heads + jnp.where(place // HEADS == k + 1, pltpu.roll(row, HEADS * (k + 1), 1), 0.0)
    wide_o[5:6, INNER : INNER + LANES] = heads
    wide_o[5:6, INNER + LANES :] = jnp.zeros((1, CONV_CH - INNER - LANES), F32)


def row_of(values, rows=8):
    pad = [(0, rows - values.shape[0]), (0, max(0, LANES - values.shape[1]))]
    return jnp.pad(values.astype(F32), pad)


def per_device(
    hidden, segment_ids, in_weight, out_weight, conv_weight, conv_bias, norm_gain, gate_gain,
    dt_bias, a_log, skip_param, cotangent,
):
    layers_n, in_rows = in_weight.shape[:2]
    out_rows = out_weight.shape[1]
    rows, width = hidden.shape
    count = lax.axis_size("seq")
    me = lax.axis_index("seq")
    me_ref = me.reshape(1).astype(jnp.int32)
    conv_n = conv_bias.shape[1]
    half = INNER // 2
    plane_n = axes_of(count)["z"][1]

    small = jnp.concatenate(
        [conv_weight.reshape(-1), conv_bias.reshape(-1), norm_gain.reshape(-1), gate_gain.reshape(-1)]
    )
    length = small.shape[0]
    small_rows = -(-length // (16 * LANES)) * 16
    small = jnp.pad(small, (0, small_rows * LANES - length)).reshape(small_rows, LANES)
    in_weight_side = jnp.pad(in_weight[0, :, INNER:], ((0, 0), (0, WIDE - SIDE)))
    halo = shifted(hidden[rows - HALO :], 1)
    seg_halo = shifted(segment_ids[rows - HALO :] + 1, 1) - 1
    packs = []
    for layer in range(layers_n):
        parts = [in_weight[layer, :, :half], in_weight[layer, :, half:INNER], out_weight[layer]]
        if layer + 1 < layers_n:
            later = in_weight[layer + 1, :, INNER:]
            parts += [later[:, :half], later[:, half : 2 * half]]
            parts.append(jnp.pad(later[:, 2 * half :], ((0, 0), (0, 3 * half - SIDE))))
        packs.append((jnp.concatenate(parts, axis=0), np.cumsum([0] + [p.shape[0] for p in parts]).tolist()))
    first = Gather(in_weight_side)
    started = first.line(tuple(far(pack) for pack, _ in packs[1:]))
    gathered = [lax.all_gather(after(pack, started) if layer else pack, "seq") for layer, (pack, _) in enumerate(packs)]
    crossed = first.plane()
    smalls = gather_small(small, [(), (), (started,), (started,), (crossed,)])

    seg_pad = jnp.concatenate([seg_halo[LEAD:], segment_ids])
    before = seg_pad[CONV_K - 2]
    columns = [seg_pad[k : k + rows] == segment_ids for k in range(CONV_K - 1)]
    columns += [segment_ids == before, segment_ids == segment_ids[-1], segment_ids]
    marks = jnp.pad(jnp.stack([col.astype(F32) for col in columns], axis=1), ((0, 0), (0, LANES - 6)))
    seg_row = jnp.broadcast_to(segment_ids.astype(F32)[None, :], (8, rows))

    relative, planes = relative_places(count), plane_first(count)
    order = column_order(relative, me, in_rows)
    plane_order = column_order(planes, 0, in_rows)

    place = (jnp.arange(count)[:, None] == (jnp.arange(count) ^ me)[None, :]).astype(BF16)
    smalls = dot(place, smalls.reshape(count, small_rows * LANES))
    sizes = [layers_n * CONV_K * conv_n, layers_n * conv_n, layers_n * in_rows, layers_n * out_rows]
    cuts = np.cumsum([0] + sizes)
    taps, biases, gains, gate_gains = (smalls[:, cuts[i] : cuts[i + 1]] for i in range(4))
    taps = taps.reshape(count, layers_n, CONV_K, conv_n).transpose(1, 2, 0, 3).reshape(layers_n, CONV_K, CONV_CH)
    biases = biases.reshape(count, layers_n, 1, conv_n).transpose(1, 2, 0, 3).reshape(layers_n, 1, CONV_CH)
    conv_rows = jnp.pad(jnp.concatenate([taps, biases], axis=1), ((0, 0), (0, 3), (0, 0)))
    gains = gains.reshape(count, layers_n, in_rows).transpose(1, 0, 2).reshape(layers_n, 1, width)
    gate_gains = gate_gains.reshape(count, layers_n, out_rows).transpose(1, 0, 2).reshape(layers_n, 1, INNER)
    gains = [jnp.broadcast_to(gains[layer], (8, width)) for layer in range(layers_n)]
    gate_gains = [jnp.broadcast_to(gate_gains[layer], (8, INNER)) for layer in range(layers_n)]
    conv_rows = [conv_rows[layer] for layer in range(layers_n)]
    heads = [
        row_of(jnp.stack([dt_bias[layer], -jnp.exp(a_log[layer]), skip_param[layer]])) for layer in range(layers_n)
    ]

    (left, left2), (right, right2) = first.whole((*conv_rows, *gains, *gate_gains, *heads, marks, seg_row, halo, order))

    scratch_wide = pltpu.VMEM((rows, INNER), BF16)
    scratch_half = pltpu.VMEM((rows, INNER // 2), BF16)
    scratch_cols = pltpu.VMEM((HEADS // 2, rows, LANES), F32)
    scratch_rows = pltpu.VMEM((LANES, rows), F32)

    residual = hidden
    saved, sides = [], ()
    for layer in range(layers_n):
        precise = layer + 1 < layers_n
        gain, gate = gains[layer], gate_gains[layer]
        (normed,) = kernel_call(norm_kernel, [((HALO + rows, width), BF16)], (residual, halo, gain))
        normed_rel = dot(normed, order).astype(BF16)
        if layer == 0:
            lower, upper = normed_rel[:, : width // 2], normed_rel[:, width // 2 :]
            parts = [dot(lower, left) + dot(upper, left2), dot(lower, right) + dot(upper, right2)]
        else:
            parts = [dot(normed, part) for part in side_parts[:2]]
            parts.append(dot(normed, side_parts[2][:, : WIDE - 2 * half]))
        pc = jnp.concatenate([part.astype(BF16) for part in parts], axis=1)
        hp = heads[layer]
        conv_l, conv_r, bc, dt, log, own, msg = kernel_call(
            partial(conv_state_kernel, precise=precise),
            [((rows, half), F32)] * 2 + [((rows, 2 * STATE), F32)] + [((rows, LANES), F32)] * 2
            + [state_out(half)] * 2,
            (pc, conv_rows[layer], hp, marks, me_ref),
            scratch=[scratch_wide] * (2 if precise else 1), flops=2 * rows * STATE * INNER * 8,
        )
        yw = [
            kernel_call(
                partial(within_kernel, precise=precise, first=part * PAIRS // 2), [((rows, half), F32)],
                ((conv_l, conv_r)[part], bc, dt, log, hp, marks, seg_row),
                scratch=[scratch_half, scratch_cols, scratch_rows] + [scratch_half] * precise,
                flops=2 * rows * rows * half * 16,
            )[0]
            for part in range(2)
        ]
        mine, recv = exchange(own, msg, me_ref, False, [(), (yw[0],), (yw[1],), ()])
        aligned = out_rows == HEAD_DIM
        pack, spans = gathered[layer], packs[layer][1]
        weights = [pack[:, a:b].reshape(-1, width) for a, b in zip(spans, spans[1:])]
        outs = [((rows, INNER), BF16), ((rows, INNER), F32), ((rows, INNER), BF16)] + [((STATE, half), BF16)] * 2
        outs += [((rows, width), F32)] + [((rows, INNER), BF16)] * aligned
        form = partial(post_kernel, places=planes, relative=False)
        args = (normed, residual, *yw, mine, recv, bc, log, marks, gate, me_ref)
        scratch = [pltpu.VMEM((rows, INNER), F32)]
        flops = 2 * rows * width * INNER * 2
        if in_rows % HALO:
            z, y, gnormed, state, state2, after_h, *gn_rel = kernel_call(
                partial(form, spans=(), aligned=aligned), outs, (*weights[:3], *args), scratch=scratch, flops=flops
            )
        else:
            z, y, gnormed, state, state2, after_h, *rest = streamed_call(
                partial(form, spans=spans, aligned=aligned), outs, args, flops=flops, streamed=pack,
                scratch=scratch + [pltpu.VMEM((count, 2 * in_rows, width), BF16)] * 2,
                raw=[((count, b - a, width), BF16) for a, b in zip(spans, spans[1:])],
            )
            gn_rel = rest[:aligned]
            weights = [part.reshape(-1, width) for part in rest[aligned:]]
        weights, side_parts = weights[:3], weights[3:]
        if not aligned:
            gn_rel = [dot(gnormed, column_order(planes, 0, out_rows)).astype(BF16)]
        saved.append((residual, normed, normed_rel, pc, conv_l, conv_r, bc, dt, log, hp, z, y, gn_rel[0], state, state2, weights, sides))
        sides = side_parts
        residual = after_h
        if layer + 1 < layers_n:
            halo = shifted(residual[rows - HALO :], 1)

    grad = cotangent
    pack_sums, pack_terms, side_shares = ([None] * layers_n for _ in range(3))
    for layer in range(layers_n - 1, -1, -1):
        h, normed, normed_rel, pc, conv_l, conv_r, bc, dt, log, hp, z, y, gn_rel, state, state2, weights, sides = saved[layer]
        z_low, z_high, out_w = weights
        gain, gate = gains[layer], gate_gains[layer]
        mixed = grad.astype(BF16)
        gy, gy2, gz, gate_grad, skip_grad, own, msg = kernel_call(
            post_back_kernel,
            [((rows, half), BF16)] * 2 + [((rows, INNER), BF16), ((8, INNER), F32), ((8, LANES), F32)]
            + [state_out(half), state_out(half, BF16)],
            (dot_t(mixed, out_w), y, z, gate, conv_l, conv_r, bc, log, marks, me_ref),
            scratch=[scratch_wide], flops=2 * rows * STATE * INNER * 8,
        )
        halves_back = [
            kernel_call(
                partial(within_back_kernel, first=part * PAIRS // 2),
                [((rows, half), F32), ((rows, LANES), F32), ((rows, LANES), F32), ((rows, LANES), F32)],
                ((conv_l, conv_r)[part], bc, dt, log, (gy, gy2)[part], (state, state2)[part], marks, seg_row),
                scratch=[
                    scratch_half, scratch_half, scratch_cols, scratch_rows,
                    pltpu.VMEM((rows, rows), F32), scratch_rows, pltpu.VMEM((rows, LANES), F32),
                ],
                flops=2 * rows * rows * half * 32,
            )
            for part in range(2)
        ]
        normed_planes = dot(normed, plane_order).astype(BF16)
        (term,) = grads_call(gn_rel, normed_planes, mixed, gz, count, 1)
        pack_sums[layer] = scatter_planes(term.reshape(-1, width))
        pack_terms[layer] = line_terms(pack_sums[layer])
        deps = [(), (far(term),), (halves_back[0][0],), (halves_back[1][0],)]
        late = ()
        if layer + 1 < layers_n:
            deps[0] += (far(pack_sums[layer + 1]),)
            late = tuple(far(part) for part in side_shares[layer + 1].terms[1:3])
        mine, recv = exchange(own, msg, me_ref, True, deps)

        (gx, *sums), (gx2, *sums2) = halves_back
        gp, wide = kernel_call(
            mixer_back_kernel,
            [((HALO + rows, WIDE), BF16), ((8, CONV_CH), F32)],
            (
                gx2, gy2, conv_r, pc, conv_rows[layer], gx, *sums, *sums2, mine, recv, gy, conv_l, bc, dt, log,
                state, state2, hp, marks, gate_grad, skip_grad, me_ref,
            ),
            scratch=[pltpu.VMEM((STATE, INNER), BF16), scratch_wide, pltpu.VMEM((HALO + rows, LANES), F32)],
            flops=2 * rows * STATE * INNER * 24, deps=late,
        )
        spilled = shifted(gp[:HALO], -1)
        side_shares[layer] = share_terms(normed_rel, gp)
        both = (side_shares[layer].terms[0], side_shares[layer].send)
        if layer:
            pieces = tuple(side_shares[layer].step())
        else:
            pieces = tuple(side_shares[layer].step())
        gp_own, gz = kernel_call(
            own_rows_kernel, [((rows, WIDE), BF16), ((rows, INNER), BF16)], (gp, spilled, gz),
            deps=both if layer else (far(pieces[0]), *[far(t) for above in pack_terms[1:] for t in above[1:]]),
        )
        if not layer:
            for share in side_shares[1:]:
                share.step(behind=gp_own)
        gn_z = dot_t(gz[:, :half], z_low) + dot_t(gz[:, half:], z_high)
        if layer:
            gn = gn_z
            for k, part in enumerate(sides):
                piece = gp_own[:, k * half : min((k + 1) * half, WIDE)]
                gn = gn + dot_t(piece, part[:, : piece.shape[1]])
        else:
            gp_left, gp_right = gp_own[:, :CUT], gp_own[:, CUT:]
            gn_side = jnp.concatenate(
                [dot_t(gp_left, left) + dot_t(gp_right, right), dot_t(gp_left, left2) + dot_t(gp_right, right2)],
                axis=1,
            )
            gn_high, gn_low = halves(gn_side)
            gn = gn_z + dot_t(gn_high, order) + dot_t(gn_low, order)
        grad, small_grads = kernel_call(
            norm_back_kernel, [((rows, width), F32), ((8 * (layers_n - layer), CONV_CH), F32)],
            (gn, h, grad, gain, wide) + ((small_grads,) if layer + 1 < layers_n else ()),
            deps=tuple(
                far(part)
                for part in (pieces if layer else (pack_sums[0], *[t for v in side_shares[1:] for t in v.terms[1:]]))
            ),
        )
    (sums,) = kernel_call(round_kernel, [(small_grads.shape, BF16)], (small_grads,))
    sums = sum_rounds(sums, count // 2, plane_n)
    pieces = side_shares[0].step()
    late = [(far(part),) for part in side_shares[0].terms[1:]]
    late[0] += tuple(far(part) for part in pack_terms[0][1:])
    sums = sum_rounds(sums, plane_n // 2, 1, late)
    in_grads, out_grads = [], []
    for layer in range(layers_n):
        pack, side = (
            sum((t.astype(F32) for t in terms[1:]), terms[0].astype(F32))
            for terms in (pack_terms[layer], side_shares[layer].terms)
        )
        if layer == 0:
            pack = pack + held_back(pieces[1])
        in_grads.append(jnp.concatenate([pack[:in_rows], pack[in_rows : 2 * in_rows], side[:, :SIDE]], axis=1))
        out_grads.append(pack[2 * in_rows :])
    in_grads, out_grads = jnp.stack(in_grads), jnp.stack(out_grads)
    sums = sums.reshape(layers_n, 8, CONV_CH)

    def share(values):
        span = values.shape[-1] // count
        return lax.dynamic_slice_in_dim(values, me * span, span, values.ndim - 1)

    heads = sums[:, 5, INNER : INNER + 3 * HEADS]
    return (
        residual, grad, in_grads, out_grads,
        share(sums[:, :CONV_K]), share(sums[:, CONV_K]), share(sums[:, 6, :width]), share(sums[:, 5, :INNER]),
        heads[:, :HEADS], heads[:, HEADS : 2 * HEADS], heads[:, 2 * HEADS :],
    )


def solution(mesh):
    return jax.shard_map(
        per_device,
        mesh=mesh,
        in_specs=(
            P("seq", None), P("seq"), P(None, "seq", None), P(None, "seq", None), P(None, None, "seq"),
            P(None, "seq"), P(None, "seq"), P(None, "seq"), P(), P(), P(), P("seq", None),
        ),
        out_specs=(
            P("seq", None), P("seq", None), P(None, "seq", None), P(None, "seq", None), P(None, None, "seq"),
            P(None, "seq"), P(None, "seq"), P(None, "seq"), P(), P(), P(),
        ),
        check_vma=False,
    )
```
